128 devices in a mesh: rep: 8 (over x_hi, y), fsdp: 16 (over z, x_lo, core).
Axes of the slice: x: 4 (x_hi: 2, x_lo: 2; x = x_hi * 2 + x_lo), y: 4, z: 4, core: 2. Of those that a mesh axis runs over, the one named last changes fastest.
Arguments:
- local_params: bfloat16 [8, 2, 8192, 1024], P('rep', None, 'fsdp'), may hold values from -6 to 6
- base: float32 [2, 8192, 1024], P(None, 'fsdp'), may hold values from -6 to 6
- momentum: float32 [2, 8192, 1024], P(None, 'fsdp'), may hold values from -3 to 3
Outputs:
- new_base: float32 [2, 8192, 1024], P(None, 'fsdp')
- new_momentum: float32 [2, 8192, 1024], P(None, 'fsdp')
- mixed_params: bfloat16 [8, 2, 8192, 1024], P('rep', None, 'fsdp')
The draws below stay inside these ranges and needn't reach their ends.
All inputs are finite; a program needn't handle non-finite values.
Results may differ from the reference program's by a relative error of at most 0.0035.
Values may be sent and summed in bfloat16 or wider, within the bound.
A program may use at most 128 MiB of HBM per device.

```python
import math
import jax
import jax.numpy as jnp
from jax import lax

D = 8192
KV = 1024
MATS = 2
BLOCK = 128
REPS = 8


def shared_base(key):
    inner = jax.random.fold_in(key, 11)
    key_vals, key_rows, key_cols, key_signs = jax.random.split(inner, 4)
    values = jnp.clip(jax.random.normal(key_vals, (MATS, D, KV), jnp.float32), -6.0, 6.0)
    rows = jax.random.randint(key_rows, (MATS,), 0, D)
    cols = jax.random.randint(key_cols, (MATS,), 0, KV)
    signs = jnp.where(jax.random.randint(key_signs, (MATS,), 0, 2) == 1, 6.0, -6.0).astype(jnp.float32)
    return values.at[jnp.arange(MATS), rows, cols].set(signs)


def draw_base(key, part):
    values = shared_base(key)
    return values.astype(jnp.float32)


def draw_local_params(key, part):
    values = shared_base(key)
    key = jax.random.fold_in(key, 2)
    keys = jax.random.split(key, 8)
    small_level, large_level, single_level, spread = (0.1, 0.6, 0.05, 10.0)
    common = jnp.clip(jax.random.normal(keys[3], (MATS, D, KV), jnp.float32), -4.0, 4.0)
    single = jnp.clip(jax.random.normal(keys[4], (REPS, MATS, D, KV), jnp.float32), -4.0, 4.0)
    order = jax.random.permutation(keys[0], MATS)
    level = jnp.where(order < MATS // 2, small_level, large_level).astype(jnp.float32)
    mean_square = (spread * spread - 1.0) / (2.0 * math.log(spread))
    trend = jnp.sqrt(1.0 + 2.0 * jnp.arange(D, dtype=jnp.float32) / D)
    row_scale = jnp.power(spread, jax.random.uniform(keys[1], (MATS, D), jnp.float32)) * trend[None, :]
    col_scale = jnp.power(spread, jax.random.uniform(keys[2], (MATS, KV), jnp.float32))
    scale = row_scale[:, :, None] * col_scale[:, None, :] / math.sqrt(2.0 * mean_square * mean_square)
    drift = scale[None] * (level[None, :, None, None] * common[None] + single_level * single)
    result = jnp.clip(values[None] + drift, -6.0, 6.0)
    rows = jax.random.randint(keys[5], (REPS, MATS), 0, D)
    cols = jax.random.randint(keys[6], (REPS, MATS), 0, KV)
    signs = jnp.where(jax.random.randint(keys[7], (REPS, MATS), 0, 2) == 1, 6.0, -6.0).astype(jnp.float32)
    replica_index = jnp.arange(REPS)[:, None]
    matrix_index = jnp.arange(MATS)[None, :]
    result = result.at[replica_index, matrix_index, rows, cols].set(signs)
    return result.astype(jnp.bfloat16)


def shard_levels(key, dims, shards, low, high):
    gain = 1.0
    for dim, blocks in shards:
        steps = jax.random.uniform(jax.random.fold_in(jax.random.fold_in(key, 6), dim), (blocks,), jnp.float32, low / len(shards), high / len(shards))
        gain = gain * jnp.repeat(jnp.exp(steps), dims[dim] // blocks).reshape((-1,) + (1,) * (len(dims) - 1 - dim))
    return gain


def bell_draw(own_key, dims, scale, most, shards=(), held_as=jnp.bfloat16):
    values = jax.random.normal(own_key, dims, jnp.float32) * scale
    if len(shards) > 0:
        values = shard_levels(own_key, dims, shards, -0.22, 0.18) * values
    return jnp.clip(values, min=-most, max=most).astype(held_as)


def setup_inputs(seed: int = 0) -> dict:
    key_list = jax.random.split(jax.random.key(seed), 4)
    return {
        "local_params": draw_local_params(jax.random.fold_in(key_list[3], 71), 0),
        "base": draw_base(jax.random.fold_in(key_list[3], 71), 0),
        "momentum": bell_draw(key_list[2], (MATS, D, KV), 0.5, 3.0, ((1, 16),), jnp.float32),
    }


def quantize(values):
    shaped = values.reshape(values.shape[:-1] + (values.shape[-1] // BLOCK, BLOCK))
    scale = jnp.sqrt(lax.optimization_barrier(jnp.mean(shaped * shaped, axis=-1)) + 1e-06).astype(jnp.bfloat16)
    code = jnp.clip(shaped / scale.astype(jnp.float32)[..., None], -2.5, 2.5).astype(jnp.bfloat16)
    return (code, scale)

def dequantize(code, scale):
    joined = code.astype(jnp.float32) * scale.astype(jnp.float32)[..., None]
    return joined.reshape(joined.shape[:-2] + (joined.shape[-2] * joined.shape[-1],))

def reference(local_params, base, momentum):
    total = jnp.zeros(base.shape, jnp.float32)
    for replica in range(REPS):
        delta = base - local_params[replica].astype(jnp.float32)
        code, scale = quantize(delta)
        total = total + dequantize(code, scale)
    average = total / REPS
    code, scale = quantize(average)
    step_zero = dequantize(code, scale)
    norm = jnp.sqrt(lax.optimization_barrier(jnp.sum(step_zero * step_zero, axis=(1, 2))) + 1e-06)
    factor = jnp.minimum(1.0, 0.25 * jnp.sqrt(jnp.float32(D * KV)) / norm)
    grad = factor[:, None, None] * step_zero
    new_momentum = 0.9 * momentum + grad
    new_base = base - 0.7 * (grad + 0.9 * new_momentum)
    mixed_params = (0.5 * local_params.astype(jnp.float32) + 0.5 * new_base[None]).astype(jnp.bfloat16)
    return (new_base, new_momentum, mixed_params)
```

```python
import functools

import jax
import jax.numpy as jnp
from jax import lax
from jax.experimental import pallas as pl
from jax.experimental.pallas import tpu as pltpu
from jax.sharding import PartitionSpec as P

D = 8192
KV = 1024
BLOCK = 128
NB = KV // BLOCK
OWN = 128
GX = 5
GY = 3
LX = GX * NB * 16
LY = GY * NB * 16
MESH = pl.DeviceIdType.MESH
F32 = jnp.float32
BF16 = jnp.bfloat16


def tile(block):
    return slice(block * 16, block * 16 + 16)


def lane(packed, index):
    return packed[:, index : index + 1]


def pack(load, groups):
    lanes = lax.broadcasted_iota(jnp.int32, (16, BLOCK), 1)
    packed = jnp.zeros((16, BLOCK), F32)
    for g in range(groups):
        for j in range(NB):
            x = load(g, j)
            total = jnp.sum(x * x, axis=1, keepdims=True)
            packed = jnp.where(lanes == NB * g + j, total, packed)
    return jnp.sqrt(packed * (1.0 / BLOCK) + 1e-06).astype(BF16)


def quantize(load, groups, put):
    scale = pack(load, groups)
    scale32 = scale.astype(F32)
    inverse = 1.0 / scale32
    put(groups * NB, scale)
    for g in range(groups):
        for j in range(NB):
            x = load(g, j)
            code = jnp.clip(x * lane(inverse, NB * g + j), -2.5, 2.5).astype(BF16)
            put(NB * g + j, code)


def gather_kernel(
    local_hbm, base_hbm, mom_hbm,
    ag_x, ag_y, factor, base, mom, local,
    code_x, code_y, recv_x, recv_y, sum_x, recv_s, sum_y, recv_t, acc_x, acc_y,
    norm_own, norm_f, norm_mid, norm_r,
    sem_local, sem_base, sem_mom,
    x1_s, x1_r, y1_s, y1_r, x2_s, x2_r, y2_s, y2_r,
    gx_s, gx_r, gy_s, gy_r, nf_s, nf_r, nr_s, nr_r,
):
    rep = lax.axis_index("rep")
    fsdp = lax.axis_index("fsdp")
    reps = lax.axis_size("rep")
    shards = lax.axis_size("fsdp")
    xh, y = rep // 4, rep % 4
    partner = ((1 - xh) * 4 + y, fsdp)

    def ahead(i):
        return (xh * 4 + (y + 1 + i) % 4, fsdp)

    def behind(i):
        return xh * 4 + (y + 3 - i) % 4

    def remote(src, dst, send, recv, device):
        return pltpu.make_async_remote_copy(
            src_ref=src, dst_ref=dst, send_sem=send, recv_sem=recv, device_id=device, device_id_type=MESH
        )

    barrier = pltpu.get_barrier_semaphore()
    for k in range(1, reps):
        pl.semaphore_signal(barrier, inc=1, device_id=((rep + k) % reps, fsdp), device_id_type=MESH)
    for k in range(1, shards):
        pl.semaphore_signal(barrier, inc=1, device_id=(rep, (fsdp + k) % shards), device_id_type=MESH)

    def owner(i):
        return jnp.where(i < 4, 1 - xh, xh) * 4 + (y + 1 + i) % 4

    def loads(i):
        rows = pl.ds(pl.multiple_of(owner(i) * OWN, OWN), OWN)
        return (
            pltpu.make_async_copy(local_hbm.at[rows], local.at[rows], sem_local.at[i]),
            pltpu.make_async_copy(base_hbm.at[rows], base.at[rows], sem_base.at[i]),
        )

    @pl.loop(0, 8)
    def _(i):
        for copy in loads(i):
            copy.start()

    mom_copy = pltpu.make_async_copy(mom_hbm, mom, sem_mom)
    mom_copy.start()

    def quantize_owner(i):
        for copy in loads(i):
            copy.wait()
        o = owner(i)

        def loader(first):
            def load(g, j):
                rows = pl.ds(pl.multiple_of(o * OWN + first + g * 16, 16), 16)
                cols = slice(j * BLOCK, (j + 1) * BLOCK)
                return base[rows, cols] - local[rows, cols].astype(F32)

            return load

        def putter(ref):
            def put(t, value):
                ref[o, tile(t)] = value

            return put

        quantize(loader(0), GX, putter(code_x))
        quantize(loader(GX * 16), GY, putter(code_y))

    def send_x1(i):
        return remote(code_x.at[owner(i)], recv_x.at[i], x1_s.at[i], x1_r.at[i], partner)

    def send_y1(h, i):
        return remote(
            code_y.at[owner(i + 4 - 4 * h)], recv_y.at[h, i], y1_s.at[h, i], y1_r.at[h, i], ahead(i)
        )

    def send_x2():
        return remote(sum_y, recv_t, x2_s, x2_r, partner)

    def send_y2(i):
        return remote(sum_x.at[i], recv_s.at[i], y2_s.at[i], y2_r.at[i], ahead(i))

    quantize_owner(0)
    pl.semaphore_wait(barrier, reps + shards - 2)
    send_x1(0).start()
    send_y1(1, 0).start()

    @pl.loop(1, 4)
    def _(i):
        quantize_owner(i)
        send_x1(i).start()

        @pl.when(i < 3)
        def _():
            send_y1(1, i).start()

    @pl.loop(4, 8)
    def _(i):
        quantize_owner(i)

        @pl.when(i < 7)
        def _():
            send_y1(0, i - 4).start()

    def dequantized(pieces, t, scales):
        total = None
        for ref, scale in zip(pieces, scales):
            value = ref[tile(t)].astype(F32) * lane(scale, t)
            total = value if total is None else total + value
        return total

    def combine(pieces, groups, put):
        scales = [ref[tile(groups * NB)].astype(F32) for ref in pieces]
        for t in range(groups * NB):
            put(t, dequantized(pieces, t, scales))

    @pl.loop(0, 4)
    def _(i):
        send_x1(i).wait_recv()
        pieces = [code_x.at[owner(i + 4)], recv_x.at[i]]

        @pl.when(i < 3)
        def _():
            def put(t, value):
                sum_x[i, tile(t)] = value.astype(BF16)

            combine(pieces, GX, put)
            send_y2(i).start()

        @pl.when(i == 3)
        def _():
            def put(t, value):
                acc_x[tile(t)] = value

            combine(pieces, GX, put)

    for h in (1, 0):
        for i in range(3):
            send_y1(h, i).wait_recv()
        pieces = [code_y.at[owner(7 - 4 * h)]] + [recv_y.at[h, i] for i in range(3)]

        def put_sum(t, value):
            sum_y[tile(t)] = value.astype(BF16)

        def put_acc(t, value):
            acc_y[tile(t)] = value

        combine(pieces, GY, put_sum if h else put_acc)
        if h:
            send_x2().start()

    def average(acc, groups, received, gathered):
        for t in range(groups * NB):
            total = acc[tile(t)]
            for ref in received:
                total = total + ref[tile(t)].astype(F32)
            acc[tile(t)] = total * 0.125

        def load(g, j):
            return acc[tile(NB * g + j)]

        def put(t, value):
            gathered[rep, tile(t)] = value

        quantize(load, groups, put)

    def squares(groups, gathered):
        scale = gathered[rep, tile(groups * NB)].astype(F32)
        total = jnp.zeros((16, BLOCK), F32)
        for t in range(groups * NB):
            step = gathered[rep, tile(t)].astype(F32) * lane(scale, t)
            total = total + step * step
        return total[:8] + total[8:]

    def gx(kind, i, o):
        k = (0, 1, 4)[kind] + i
        device = partner if kind != 1 else ahead(i)
        return remote(ag_x.at[o], ag_x.at[o], gx_s.at[k], gx_r.at[k], device)

    def gy(kind, i, o):
        k = (0, 1, 4)[kind] + i
        device = partner if kind == 0 else ahead(i)
        return remote(ag_y.at[o], ag_y.at[o], gy_s.at[k], gy_r.at[k], device)

    for i in range(3):
        send_y2(i).wait_recv()
    average(acc_x, GX, [recv_s.at[i] for i in range(3)], ag_x)
    for i in (0, 2, 1):
        gx(1, i, rep).start()
    gx(0, 0, rep).start()
    send_x2().wait_recv()
    average(acc_y, GY, [recv_t], ag_y)
    gy(0, 0, rep).start()
    for i in (0, 2, 1):
        gy(1, i, rep).start()

    norm_own[...] = squares(GX, ag_x) + squares(GY, ag_y)

    def norm_f_copy(k):
        device = (rep, (fsdp + 1 + k) % shards)
        return remote(norm_own, norm_f.at[k], nf_s.at[k], nf_r.at[k], device)

    def norm_r_copy(k):
        device = ((rep + 1 + k) % reps, fsdp)
        return remote(norm_mid, norm_r.at[k], nr_s.at[k], nr_r.at[k], device)

    for k in range(shards - 1):
        norm_f_copy(k).start()

    other = (1 - xh) * 4
    gy(0, 0, other + y).wait_recv()
    for i in range(3):
        gy(2, i, other + y).start()

    total = norm_own[...]
    for k in range(shards - 1):
        norm_f_copy(k).wait_recv()
        total = total + norm_f[k]
    norm_mid[...] = total
    for k in range(reps - 1):
        norm_r_copy(k).start()

    for i in (0, 2, 1):
        gx(1, i, behind(i)).wait_recv()
        gx(2, i, behind(i)).start()

    same = total
    cross = jnp.zeros((8, BLOCK), F32)
    for k in range(reps - 1):
        norm_r_copy(k).wait_recv()
        sender = (rep + 2 * reps - 1 - k) % reps
        mine = (sender // 4 == xh).astype(F32)
        same = same + mine * norm_r[k]
        cross = cross + (1.0 - mine) * norm_r[k]
    for index, value in ((xh, same), (1 - xh, cross)):
        total = jnp.sum(jnp.sum(value, axis=1, keepdims=True), axis=0, keepdims=True)
        norm = jnp.sqrt(jnp.broadcast_to(total, (8, BLOCK)) + 1e-06)
        factor[index] = jnp.minimum(1.0, 0.25 * jnp.sqrt(F32(D * KV)) / norm)

    gx(0, 0, other + y).wait_recv()
    for i in range(3):
        back = (y + 3 - i) % 4
        gy(1, i, behind(i)).wait_recv()
        gy(2, i, other + back).wait_recv()
        gx(2, i, other + back).wait_recv()
    mom_copy.wait()
    for i in range(4):
        send_x1(i).wait_send()
    for i in range(3):
        for h in range(2):
            send_y1(h, i).wait_send()
        send_y2(i).wait_send()
        gx(1, i, rep).wait_send()
        gx(2, i, behind(i)).wait_send()
        gy(1, i, rep).wait_send()
        gy(2, i, other + y).wait_send()
    send_x2().wait_send()
    gx(0, 0, rep).wait_send()
    gy(0, 0, rep).wait_send()
    for k in range(shards - 1):
        norm_f_copy(k).wait_send()
    for k in range(reps - 1):
        norm_r_copy(k).wait_send()


def update_kernel(
    ag_x, ag_y, factor, base, mom, local,
    base_hbm, mom_hbm, mixed_hbm,
    new_base, new_mom, mixed, sem,
):
    def stores(o):
        rows = pl.ds(pl.multiple_of(o * OWN, OWN), OWN)
        return [
            pltpu.make_async_copy(src.at[rows], dst.at[rows], sem.at[k, o])
            for k, (src, dst) in enumerate(((new_base, base_hbm), (new_mom, mom_hbm), (mixed, mixed_hbm)))
        ]

    @pl.loop(0, 8)
    def _(o):
        clip = factor[o // 4, 0:1]
        for ref, groups, first in ((ag_x, GX, 0), (ag_y, GY, GX * 16)):
            scale = ref[o, tile(groups * NB)].astype(F32)
            for g in range(groups):
                rows = pl.ds(pl.multiple_of(o * OWN + first + g * 16, 16), 16)
                for j in range(NB):
                    cols = slice(j * BLOCK, (j + 1) * BLOCK)
                    t = NB * g + j
                    grad = clip * (ref[o, tile(t)].astype(F32) * lane(scale, t))
                    moved = 0.9 * mom[rows, cols] + grad
                    shared = base[rows, cols] - 0.7 * (grad + 0.9 * moved)
                    new_mom[rows, cols] = moved
                    new_base[rows, cols] = shared
                    mixed[rows, cols] = (0.5 * local[rows, cols].astype(F32) + 0.5 * shared).astype(BF16)
        for copy in stores(o):
            copy.start()

    @pl.loop(0, 8)
    def _(o):
        for copy in stores(o):
            copy.wait()


def local_step(local_params, base, momentum):
    rows = base.shape[0] * base.shape[1]
    shards = lax.axis_size("fsdp")
    flat = lambda a: a.reshape(rows, KV)
    dma = lambda *n: pltpu.SemaphoreType.DMA(n) if n else pltpu.SemaphoreType.DMA
    vmem = pl.BlockSpec(memory_space=pltpu.VMEM)
    hbm = pl.BlockSpec(memory_space=pltpu.HBM)
    lx, ly = LX + 16, LY + 16
    held = pl.pallas_call(
        gather_kernel,
        out_shape=[
            pltpu.VMEM((8, lx, BLOCK), BF16),
            pltpu.VMEM((8, ly, BLOCK), BF16),
            pltpu.VMEM((2, 8, BLOCK), F32),
            pltpu.VMEM((rows, KV), F32),
            pltpu.VMEM((rows, KV), F32),
            pltpu.VMEM((rows, KV), BF16),
        ],
        in_specs=[hbm] * 3,
        out_specs=[vmem] * 6,
        scratch_shapes=[
            pltpu.VMEM((8, lx, BLOCK), BF16),
            pltpu.VMEM((8, ly, BLOCK), BF16),
            pltpu.VMEM((4, lx, BLOCK), BF16),
            pltpu.VMEM((2, 3, ly, BLOCK), BF16),
            pltpu.VMEM((3, LX, BLOCK), BF16),
            pltpu.VMEM((3, LX, BLOCK), BF16),
            pltpu.VMEM((LY, BLOCK), BF16),
            pltpu.VMEM((LY, BLOCK), BF16),
            pltpu.VMEM((LX, BLOCK), F32),
            pltpu.VMEM((LY, BLOCK), F32),
            pltpu.VMEM((8, BLOCK), F32),
            pltpu.VMEM((shards - 1, 8, BLOCK), F32),
            pltpu.VMEM((8, BLOCK), F32),
            pltpu.VMEM((7, 8, BLOCK), F32),
            dma(8), dma(8), dma(),
            dma(4), dma(4), dma(2, 3), dma(2, 3), dma(), dma(), dma(3), dma(3),
            dma(7), dma(7), dma(7), dma(7), dma(shards - 1), dma(shards - 1), dma(7), dma(7),
        ],
        compiler_params=pltpu.CompilerParams(
            collective_id=0, has_side_effects=True, vmem_limit_bytes=26 * 2**20
        ),
        name="gather",
    )(flat(local_params), flat(base), flat(momentum))
    new_base, new_momentum, mixed = pl.pallas_call(
        update_kernel,
        out_shape=[
            jax.ShapeDtypeStruct((rows, KV), F32),
            jax.ShapeDtypeStruct((rows, KV), F32),
            jax.ShapeDtypeStruct((rows, KV), BF16),
        ],
        in_specs=[vmem] * 6,
        out_specs=[hbm] * 3,
        scratch_shapes=[
            pltpu.VMEM((rows, KV), F32),
            pltpu.VMEM((rows, KV), F32),
            pltpu.VMEM((rows, KV), BF16),
            dma(3, 8),
        ],
        compiler_params=pltpu.CompilerParams(vmem_limit_bytes=26 * 2**20),
        name="update",
    )(*held)
    return (
        new_base.reshape(base.shape),
        new_momentum.reshape(base.shape),
        mixed.reshape(local_params.shape),
    )


def solution(mesh):
    return jax.shard_map(
        local_step,
        mesh=mesh,
        in_specs=(P("rep", None, "fsdp", None), P(None, "fsdp", None), P(None, "fsdp", None)),
        out_specs=(P(None, "fsdp", None), P(None, "fsdp", None), P("rep", None, "fsdp", None)),
        check_vma=False,
    )
```

```python
import functools

import jax
import jax.numpy as jnp
from jax import lax
from jax.experimental import pallas as pl
from jax.experimental.pallas import tpu as pltpu
from jax.sharding import PartitionSpec as P

D = 8192
KV = 1024
BLOCK = 128
NB = KV // BLOCK
OWN = 128
GX = 5
GY = 3
LX = GX * NB * 16
LY = GY * NB * 16
MESH = pl.DeviceIdType.MESH
F32 = jnp.float32
BF16 = jnp.bfloat16


def tile(block):
    return slice(block * 16, block * 16 + 16)


def lane(packed, index):
    return packed[:, index : index + 1]


def pack(load, groups):
    lanes = lax.broadcasted_iota(jnp.int32, (16, BLOCK), 1)
    packed = jnp.zeros((16, BLOCK), F32)
    for g in range(groups):
        for j in range(NB):
            x = load(g, j)
            total = jnp.sum(x * x, axis=1, keepdims=True)
            packed = jnp.where(lanes == NB * g + j, total, packed)
    return jnp.sqrt(packed * (1.0 / BLOCK) + 1e-06).astype(BF16)


def quantize(load, groups, put):
    scale = pack(load, groups)
    scale32 = scale.astype(F32)
    inverse = 1.0 / scale32
    put(groups * NB, scale)
    for g in range(groups):
        for j in range(NB):
            x = load(g, j)
            code = jnp.clip(x * lane(inverse, NB * g + j), -2.5, 2.5).astype(BF16)
            put(NB * g + j, code)


def gather_kernel(
    local_hbm, base_hbm, mom_hbm,
    ag_x, ag_y, factor, base, mom, local,
    code_x, code_y, recv_x, recv_y, sum_x, recv_s, sum_y, recv_t, acc_x, acc_y,
    norm_own, norm_f, norm_mid, norm_r,
    sem_local, sem_base, sem_mom,
    x1_s, x1_r, y1_s, y1_r, x2_s, x2_r, y2_s, y2_r,
    gx_s, gx_r, gy_s, gy_r, nf_s, nf_r, nr_s, nr_r,
):
    rep = lax.axis_index("rep")
    fsdp = lax.axis_index("fsdp")
    reps = lax.axis_size("rep")
    shards = lax.axis_size("fsdp")
    xh, y = rep // 4, rep % 4
    partner = ((1 - xh) * 4 + y, fsdp)

    def ahead(i):
        return (xh * 4 + (y + 1 + i) % 4, fsdp)

    def behind(i):
        return xh * 4 + (y + 3 - i) % 4

    def remote(src, dst, send, recv, device):
        return pltpu.make_async_remote_copy(
            src_ref=src, dst_ref=dst, send_sem=send, recv_sem=recv, device_id=device, device_id_type=MESH
        )

    barrier = pltpu.get_barrier_semaphore()
    for k in range(1, reps):
        pl.semaphore_signal(barrier, inc=1, device_id=((rep + k) % reps, fsdp), device_id_type=MESH)
    for k in range(1, shards):
        pl.semaphore_signal(barrier, inc=1, device_id=(rep, (fsdp + k) % shards), device_id_type=MESH)

    def owner(i):
        return jnp.where(i < 4, 1 - xh, xh) * 4 + (y + 1 + i) % 4

    def loads(i):
        rows = pl.ds(pl.multiple_of(owner(i) * OWN, OWN), OWN)
        return (
            pltpu.make_async_copy(local_hbm.at[rows], local.at[rows], sem_local.at[i]),
            pltpu.make_async_copy(base_hbm.at[rows], base.at[rows], sem_base.at[i]),
        )

    @pl.loop(0, 8)
    def _(i):
        for copy in loads(i):
            copy.start()

    mom_copy = pltpu.make_async_copy(mom_hbm, mom, sem_mom)
    mom_copy.start()

    def quantize_owner(i):
        for copy in loads(i):
            copy.wait()
        o = owner(i)

        def loader(first):
            def load(g, j):
                rows = pl.ds(pl.multiple_of(o * OWN + first + g * 16, 16), 16)
                cols = slice(j * BLOCK, (j + 1) * BLOCK)
                return base[rows, cols] - local[rows, cols].astype(F32)

            return load

        def putter(ref):
            def put(t, value):
                ref[o, tile(t)] = value

            return put

        quantize(loader(0), GX, putter(code_x))
        quantize(loader(GX * 16), GY, putter(code_y))

    def send_x1(i):
        return remote(code_x.at[owner(i)], recv_x.at[i], x1_s.at[i], x1_r.at[i], partner)

    def send_y1(h, i):
        return remote(
            code_y.at[owner(i + 4 - 4 * h)], recv_y.at[h, i], y1_s.at[h, i], y1_r.at[h, i], ahead(i)
        )

    def send_x2():
        return remote(sum_y, recv_t, x2_s, x2_r, partner)

    def send_y2(i):
        return remote(sum_x.at[i], recv_s.at[i], y2_s.at[i], y2_r.at[i], ahead(i))

    quantize_owner(0)
    pl.semaphore_wait(barrier, reps + shards - 2)
    send_x1(0).start()
    send_y1(1, 0).start()

    @pl.loop(1, 4)
    def _(i):
        quantize_owner(i)
        send_x1(i).start()

        @pl.when(i < 3)
        def _():
            send_y1(1, i).start()

    @pl.loop(4, 8)
    def _(i):
        quantize_owner(i)

        @pl.when(i < 7)
        def _():
            send_y1(0, i - 4).start()

    def dequantized(pieces, t, scales):
        total = None
        for ref, scale in zip(pieces, scales):
            value = ref[tile(t)].astype(F32) * lane(scale, t)
            total = value if total is None else total + value
        return total

    def combine(pieces, groups, put):
        scales = [ref[tile(groups * NB)].astype(F32) for ref in pieces]
        for t in range(groups * NB):
            put(t, dequantized(pieces, t, scales))

    @pl.loop(0, 4)
    def _(i):
        send_x1(i).wait_recv()
        pieces = [code_x.at[owner(i + 4)], recv_x.at[i]]

        @pl.when(i < 3)
        def _():
            def put(t, value):
                sum_x[i, tile(t)] = value.astype(BF16)

            combine(pieces, GX, put)
            send_y2(i).start()

        @pl.when(i == 3)
        def _():
            def put(t, value):
                acc_x[tile(t)] = value

            combine(pieces, GX, put)

    for h in (1, 0):
        for i in range(3):
            send_y1(h, i).wait_recv()
        pieces = [code_y.at[owner(7 - 4 * h)]] + [recv_y.at[h, i] for i in range(3)]

        def put_sum(t, value):
            sum_y[tile(t)] = value.astype(BF16)

        def put_acc(t, value):
            acc_y[tile(t)] = value

        combine(pieces, GY, put_sum if h else put_acc)
        if h:
            send_x2().start()

    def average(acc, groups, received, gathered):
        for t in range(groups * NB):
            total = acc[tile(t)]
            for ref in received:
                total = total + ref[tile(t)].astype(F32)
            acc[tile(t)] = total * 0.125

        def load(g, j):
            return acc[tile(NB * g + j)]

        def put(t, value):
            gathered[rep, tile(t)] = value

        quantize(load, groups, put)

    def squares(groups, gathered):
        scale = gathered[rep, tile(groups * NB)].astype(F32)
        total = jnp.zeros((16, BLOCK), F32)
        for t in range(groups * NB):
            step = gathered[rep, tile(t)].astype(F32) * lane(scale, t)
            total = total + step * step
        return total[:8] + total[8:]

    def gx(kind, i, o):
        k = (0, 1, 4)[kind] + i
        device = partner if kind != 1 else ahead(i)
        return remote(ag_x.at[o], ag_x.at[o], gx_s.at[k], gx_r.at[k], device)

    def gy(kind, i, o):
        k = (0, 1, 4)[kind] + i
        device = partner if kind == 0 else ahead(i)
        return remote(ag_y.at[o], ag_y.at[o], gy_s.at[k], gy_r.at[k], device)

    for i in range(3):
        send_y2(i).wait_recv()
    average(acc_x, GX, [recv_s.at[i] for i in range(3)], ag_x)
    for i in (0, 2, 1):
        gx(1, i, rep).start()
    gx(0, 0, rep).start()
    send_x2().wait_recv()
    average(acc_y, GY, [recv_t], ag_y)
    gy(0, 0, rep).start()
    for i in (0, 2, 1):
        gy(1, i, rep).start()

    norm_own[...] = squares(GX, ag_x) + squares(GY, ag_y)

    def norm_f_copy(k):
        device = (rep, (fsdp + 1 + k) % shards)
        return remote(norm_own, norm_f.at[k], nf_s.at[k], nf_r.at[k], device)

    def norm_r_copy(k):
        device = ((rep + 1 + k) % reps, fsdp)
        return remote(norm_mid, norm_r.at[k], nr_s.at[k], nr_r.at[k], device)

    for k in range(shards - 1):
        norm_f_copy(k).start()

    other = (1 - xh) * 4
    gy(0, 0, other + y).wait_recv()
    for i in range(3):
        gy(2, i, other + y).start()

    total = norm_own[...]
    for k in range(shards - 1):
        norm_f_copy(k).wait_recv()
        total = total + norm_f[k]
    norm_mid[...] = total
    for k in range(reps - 1):
        norm_r_copy(k).start()

    for i in (0, 2, 1):
        gx(1, i, behind(i)).wait_recv()
        gx(2, i, behind(i)).start()

    same = total
    cross = jnp.zeros((8, BLOCK), F32)
    for k in range(reps - 1):
        norm_r_copy(k).wait_recv()
        sender = (rep + 2 * reps - 1 - k) % reps
        mine = (sender // 4 == xh).astype(F32)
        same = same + mine * norm_r[k]
        cross = cross + (1.0 - mine) * norm_r[k]
    for index, value in ((xh, same), (1 - xh, cross)):
        total = jnp.sum(jnp.sum(value, axis=1, keepdims=True), axis=0, keepdims=True)
        norm = jnp.sqrt(jnp.broadcast_to(total, (8, BLOCK)) + 1e-06)
        factor[index] = jnp.minimum(1.0, 0.25 * jnp.sqrt(F32(D * KV)) / norm)

    gx(0, 0, other + y).wait_recv()
    for i in range(3):
        back = (y + 3 - i) % 4
        gy(1, i, behind(i)).wait_recv()
        gy(2, i, other + back).wait_recv()
        gx(2, i, other + back).wait_recv()
    mom_copy.wait()
    for i in range(4):
        send_x1(i).wait_send()
    for i in range(3):
        for h in range(2):
            send_y1(h, i).wait_send()
        send_y2(i).wait_send()
        gx(1, i, rep).wait_send()
        gx(2, i, behind(i)).wait_send()
        gy(1, i, rep).wait_send()
        gy(2, i, other + y).wait_send()
    send_x2().wait_send()
    gx(0, 0, rep).wait_send()
    gy(0, 0, rep).wait_send()
    for k in range(shards - 1):
        norm_f_copy(k).wait_send()
    for k in range(reps - 1):
        norm_r_copy(k).wait_send()


def update_kernel(
    ag_x, ag_y, factor, base, mom, local,
    base_hbm, mom_hbm, mixed_hbm,
    new_base, new_mom, mixed, sem,
):
    def stores(o):
        rows = pl.ds(pl.multiple_of(o * OWN, OWN), OWN)
        return [
            pltpu.make_async_copy(src.at[rows], dst.at[rows], sem.at[k, o])
            for k, (src, dst) in enumerate(((new_base, base_hbm), (new_mom, mom_hbm), (mixed, mixed_hbm)))
        ]

    @pl.loop(0, 8)
    def _(o):
        clip = factor[o // 4, 0:1]
        for ref, groups, first in ((ag_x, GX, 0), (ag_y, GY, GX * 16)):
            scale = ref[o, tile(groups * NB)].astype(F32)
            for g in range(groups):
                rows = pl.ds(pl.multiple_of(o * OWN + first + g * 16, 16), 16)
                for j in range(NB):
                    cols = slice(j * BLOCK, (j + 1) * BLOCK)
                    t = NB * g + j
                    grad = clip * (ref[o, tile(t)].astype(F32) * lane(scale, t))
                    moved = 0.9 * mom[rows, cols] + grad
                    shared = base[rows, cols] - 0.7 * (grad + 0.9 * moved)
                    new_mom[rows, cols] = moved
                    new_base[rows, cols] = shared
                    mixed[rows, cols] = (0.5 * local[rows, cols].astype(F32) + 0.5 * shared).astype(BF16)
        for copy in stores(o):
            copy.start()

    @pl.loop(0, 8)
    def _(o):
        for copy in stores(o):
            copy.wait()


def local_step(local_params, base, momentum):
    rows = base.shape[0] * base.shape[1]
    shards = lax.axis_size("fsdp")
    flat = lambda a: a.reshape(rows, KV)
    dma = lambda *n: pltpu.SemaphoreType.DMA(n) if n else pltpu.SemaphoreType.DMA
    vmem = pl.BlockSpec(memory_space=pltpu.VMEM)
    hbm = pl.BlockSpec(memory_space=pltpu.HBM)
    lx, ly = LX + 16, LY + 16
    held = pl.pallas_call(
        gather_kernel,
        out_shape=[
            pltpu.VMEM((8, lx, BLOCK), BF16),
            pltpu.VMEM((8, ly, BLOCK), BF16),
            pltpu.VMEM((2, 8, BLOCK), F32),
            pltpu.VMEM((rows, KV), F32),
            pltpu.VMEM((rows, KV), F32),
            pltpu.VMEM((rows, KV), BF16),
        ],
        in_specs=[hbm] * 3,
        out_specs=[vmem] * 6,
        scratch_shapes=[
            pltpu.VMEM((8, lx, BLOCK), BF16),
            pltpu.VMEM((8, ly, BLOCK), BF16),
            pltpu.VMEM((4, lx, BLOCK), BF16),
            pltpu.VMEM((2, 3, ly, BLOCK), BF16),
            pltpu.VMEM((3, LX, BLOCK), BF16),
            pltpu.VMEM((3, LX, BLOCK), BF16),
            pltpu.VMEM((LY, BLOCK), BF16),
            pltpu.VMEM((LY, BLOCK), BF16),
            pltpu.VMEM((LX, BLOCK), F32),
            pltpu.VMEM((LY, BLOCK), F32),
            pltpu.VMEM((8, BLOCK), F32),
            pltpu.VMEM((shards - 1, 8, BLOCK), F32),
            pltpu.VMEM((8, BLOCK), F32),
            pltpu.VMEM((7, 8, BLOCK), F32),
            dma(8), dma(8), dma(),
            dma(4), dma(4), dma(2, 3), dma(2, 3), dma(), dma(), dma(3), dma(3),
            dma(7), dma(7), dma(7), dma(7), dma(shards - 1), dma(shards - 1), dma(7), dma(7),
        ],
        compiler_params=pltpu.CompilerParams(
            collective_id=0, has_side_effects=True, vmem_limit_bytes=26 * 2**20
        ),
        name="gather",
    )(*[pltpu.with_memory_space_constraint(flat(a), pltpu.HBM) for a in (local_params, base, momentum)])
    new_base, new_momentum, mixed = pl.pallas_call(
        update_kernel,
        out_shape=[
            jax.ShapeDtypeStruct((rows, KV), F32),
            jax.ShapeDtypeStruct((rows, KV), F32),
            jax.ShapeDtypeStruct((rows, KV), BF16),
        ],
        in_specs=[vmem] * 6,
        out_specs=[hbm] * 3,
        scratch_shapes=[
            pltpu.VMEM((rows, KV), F32),
            pltpu.VMEM((rows, KV), F32),
            pltpu.VMEM((rows, KV), BF16),
            dma(3, 8),
        ],
        compiler_params=pltpu.CompilerParams(vmem_limit_bytes=26 * 2**20),
        name="update",
    )(*held)
    return (
        new_base.reshape(base.shape),
        new_momentum.reshape(base.shape),
        mixed.reshape(local_params.shape),
    )


def solution(mesh):
    return jax.shard_map(
        local_step,
        mesh=mesh,
        in_specs=(P("rep", None, "fsdp", None), P(None, "fsdp", None), P(None, "fsdp", None)),
        out_specs=(P(None, "fsdp", None), P(None, "fsdp", None), P("rep", None, "fsdp", None)),
        check_vma=False,
    )
```

```python
import functools

import jax
import jax.numpy as jnp
from jax import lax
from jax.experimental import pallas as pl
from jax.experimental.pallas import tpu as pltpu
from jax.sharding import PartitionSpec as P

D = 8192
KV = 1024
BLOCK = 128
NB = KV // BLOCK
OWN = 128
PARTS = 2
GROUPS = 4
TILES = GROUPS * NB
HALF = TILES // 2
SCALE = HALF
LINES = (TILES + 1) * 16
FIRST = slice(0, (HALF + 1) * 16)
SECOND = slice((HALF + 1) * 16, LINES)
MESH = pl.DeviceIdType.MESH
F32 = jnp.float32
BF16 = jnp.bfloat16


def tile(t):
    return slice(t * 16, t * 16 + 16)


def code_tile(t):
    return tile(t if t < HALF else t + 1)


def lane(packed, index):
    return packed[:, index : index + 1]


def pack(load):
    lanes = lax.broadcasted_iota(jnp.int32, (16, BLOCK), 1)
    packed = jnp.zeros((16, BLOCK), F32)
    for t in range(TILES):
        x = load(t)
        total = jnp.sum(x * x, axis=1, keepdims=True)
        packed = jnp.where(lanes == t, total, packed)
    return jnp.sqrt(packed * (1.0 / BLOCK) + 1e-06).astype(BF16)


def quantize(load, put):
    scale = pack(load)
    inverse = 1.0 / scale.astype(F32)
    put(tile(SCALE), scale)
    for t in range(TILES):
        x = load(t)
        put(code_tile(t), jnp.clip(x * lane(inverse, t), -2.5, 2.5).astype(BF16))


def gather_kernel(
    local_hbm, base_hbm, mom_hbm,
    gathered, factor, base, mom, local,
    code, recv_x, recv_y, sum_x, recv_s, sum_y, recv_t, acc,
    norm_own, norm_f, norm_mid, norm_r,
    sem_local, sem_base, sem_mom,
    x1_s, x1_r, y1_s, y1_r, x2_s, x2_r, y2_s, y2_r,
    g_s, g_r, nf_s, nf_r, nr_s, nr_r,
):
    rep = lax.axis_index("rep")
    fsdp = lax.axis_index("fsdp")
    reps = lax.axis_size("rep")
    shards = lax.axis_size("fsdp")
    xh, y = rep // 4, rep % 4
    other = 1 - xh
    partner = (other * 4 + y, fsdp)

    def along(k):
        return (xh * 4 + (y + k) % 4, fsdp)

    def remote(src, dst, send, recv, device):
        return pltpu.make_async_remote_copy(
            src_ref=src, dst_ref=dst, send_sem=send, recv_sem=recv, device_id=device, device_id_type=MESH
        )

    def owner(i):
        return jnp.where(i < 4, other, xh) * 4 + (y + 1 + i) % 4

    def loads(i):
        rows = pl.ds(pl.multiple_of(owner(i) * OWN, OWN), OWN)
        return (
            pltpu.make_async_copy(local_hbm.at[rows], local.at[rows], sem_local.at[i]),
            pltpu.make_async_copy(base_hbm.at[rows], base.at[rows], sem_base.at[i]),
        )

    def start_loads(i):
        for copy in loads(i):
            copy.start()

    start_loads(0)
    barrier = pltpu.get_barrier_semaphore()
    for k in range(1, reps):
        pl.semaphore_signal(barrier, inc=1, device_id=((rep + k) % reps, fsdp), device_id_type=MESH)
    start_loads(1)
    for k in range(1, shards):
        pl.semaphore_signal(barrier, inc=1, device_id=(rep, (fsdp + k) % shards), device_id_type=MESH)
    start_loads(2)
    mom_copy = pltpu.make_async_copy(mom_hbm, mom, sem_mom)

    def quantize_part(i, part):
        o = owner(i)

        def load(t):
            first = o * OWN + (part * GROUPS + t // NB) * 16
            rows = pl.ds(pl.multiple_of(first, 16), 16)
            cols = slice(t % NB * BLOCK, (t % NB + 1) * BLOCK)
            return base[rows, cols] - local[rows, cols].astype(F32)

        def put(where, value):
            code[part, o, where] = value

        quantize(load, put)

    def send_x1(i):
        return remote(code.at[0, owner(i)], recv_x.at[i], x1_s.at[i], x1_r.at[i], partner)

    def send_y1(h, i):
        return remote(
            code.at[1, owner(i + 4 - 4 * h)], recv_y.at[h, i], y1_s.at[h, i], y1_r.at[h, i], along(1 + i)
        )

    def send_x2():
        return remote(sum_y, recv_t, x2_s, x2_r, partner)

    def send_y2(i):
        return remote(sum_x.at[i], recv_s.at[i], y2_s.at[i], y2_r.at[i], along(1 + i))

    @pl.loop(0, 8)
    def _(i):
        for copy in loads(i):
            copy.wait()

        @pl.when(i < 5)
        def _():
            start_loads(i + 3)

        quantize_part(i, 0)

        @pl.when(i == 0)
        def _():
            pl.semaphore_wait(barrier, reps + shards - 2)

        @pl.when(i < 4)
        def _():
            send_x1(i).start()

        quantize_part(i, 1)

        @pl.when(i < 3)
        def _():
            send_y1(1, i).start()

        @pl.when(jnp.logical_and(i >= 4, i < 7))
        def _():
            send_y1(0, i - 4).start()

    mom_copy.start()

    def combine(pieces, put):
        scales = [ref[tile(SCALE)].astype(F32) for ref in pieces]
        for t in range(TILES):
            total = None
            for ref, scale in zip(pieces, scales):
                value = ref[code_tile(t)].astype(F32) * lane(scale, t)
                total = value if total is None else total + value
            put(t, total)

    def sum_pair(i):
        send_x1(i).wait_recv()
        pieces = [code.at[0, owner(i + 4)], recv_x.at[i]]

        def put_sum(t, value):
            sum_x[i, tile(t)] = value.astype(BF16)

        def put_acc(t, value):
            acc[0, tile(t)] = value

        combine(pieces, put_acc if i == 3 else put_sum)
        if i < 3:
            send_y2(i).start()

    def sum_column(h):
        for i in range(3):
            send_y1(h, i).wait_recv()
        pieces = [code.at[1, owner(7 - 4 * h)]] + [recv_y.at[h, i] for i in range(3)]

        def put_sum(t, value):
            sum_y[tile(t)] = value.astype(BF16)

        def put_acc(t, value):
            acc[1, tile(t)] = value

        combine(pieces, put_sum if h else put_acc)
        if h:
            send_x2().start()

    sum_pair(0)
    sum_pair(1)
    sum_column(1)
    sum_pair(2)
    sum_pair(3)
    sum_column(0)

    def average(part, received):
        for t in range(TILES):
            total = acc[part, tile(t)]
            for ref in received:
                total = total + ref[tile(t)].astype(F32)
            acc[part, tile(t)] = total * 0.125

        def load(t):
            return acc[part, tile(t)]

        def put(where, value):
            gathered[part, rep, where] = value

        quantize(load, put)

    def squares(part):
        scale = gathered[part, rep, tile(SCALE)].astype(F32)
        total = jnp.zeros((16, BLOCK), F32)
        for t in range(TILES):
            step = gathered[part, rep, code_tile(t)].astype(F32) * lane(scale, t)
            total = total + step * step
        return total[:8] + total[8:]

    def move(k, part, o, device, lines=None):
        ref = gathered.at[part, o] if lines is None else gathered.at[part, o, lines]
        return remote(ref, ref, g_s.at[k], g_r.at[k], device)

    def near(d):
        return xh * 4 + (y + d) % 4, other * 4 + (y + d) % 4

    def p_own(k, o):
        return move(k, 0, o, (along(1), along(3), partner)[k])

    def p_on(k, o):
        return move(5 + k, 0, o, along((1, 3)[k]), (FIRST, SECOND)[k])

    def p_cross(k, o):
        return move((3, 4, 7, 8)[k], 0, o, partner, (None, None, FIRST, SECOND)[k])

    def q_cross(o):
        return move(9, 1, o, partner)

    def q_own(side, k, o):
        return move(10 + 4 * side + k, 1, o, along((1, 3)[k]))

    def q_on(side, k, o):
        return move(12 + 4 * side + k, 1, o, along((1, 3)[k]), (FIRST, SECOND)[k])

    below, above, far = near(3), near(1), near(2)
    own, across = near(0)

    send_x2().wait_recv()
    average(1, [recv_t])
    q_cross(own).start()
    for i in range(3):
        send_y2(i).wait_recv()
    average(0, [recv_s.at[i] for i in range(3)])
    for k in range(3):
        p_own(k, own).start()
    for k in range(2):
        q_own(0, k, own).start()

    norm_own[...] = squares(0) + squares(1)

    def norm_f_copy(k):
        device = (rep, (fsdp + 1 + k) % shards)
        return remote(norm_own, norm_f.at[k], nf_s.at[k], nf_r.at[k], device)

    def norm_r_copy(k):
        device = ((rep + 1 + k) % reps, fsdp)
        return remote(norm_mid, norm_r.at[k], nr_s.at[k], nr_r.at[k], device)

    for k in range(shards - 1):
        norm_f_copy(k).start()

    for k, o in enumerate((below, above)):
        p_own(k, o[0]).wait_recv()
        p_on(k, o[0]).start()
        p_cross(k, o[0]).start()
    q_cross(across).wait_recv()
    for k in range(2):
        q_own(1, k, across).start()
    for k, o in enumerate((below, above)):
        q_own(0, k, o[0]).wait_recv()
        q_on(0, k, o[0]).start()
    for k in range(2):
        p_on(k, far[0]).wait_recv()
        p_cross(2 + k, far[0]).start()

    total = norm_own[...]
    for k in range(shards - 1):
        norm_f_copy(k).wait_recv()
        total = total + norm_f[k]
    norm_mid[...] = total
    for k in range(reps - 1):
        norm_r_copy(k).start()

    for k, o in enumerate((below, above)):
        q_own(1, k, o[1]).wait_recv()
        q_on(1, k, o[1]).start()

    same = total
    cross = jnp.zeros((8, BLOCK), F32)
    for k in range(reps - 1):
        norm_r_copy(k).wait_recv()
        sender = (rep + 2 * reps - 1 - k) % reps
        mine = (sender // 4 == xh).astype(F32)
        same = same + mine * norm_r[k]
        cross = cross + (1.0 - mine) * norm_r[k]
    for index, value in ((xh, same), (other, cross)):
        total = jnp.sum(jnp.sum(value, axis=1, keepdims=True), axis=0, keepdims=True)
        norm = jnp.sqrt(jnp.broadcast_to(total, (8, BLOCK)) + 1e-06)
        factor[index] = jnp.minimum(1.0, 0.25 * jnp.sqrt(F32(D * KV)) / norm)

    p_own(2, across).wait_recv()
    for k, o in enumerate((below, above, far, far)):
        p_cross(k, o[1]).wait_recv()
    for side in range(2):
        for k in range(2):
            q_on(side, k, far[side]).wait_recv()
    mom_copy.wait()
    for i in range(4):
        send_x1(i).wait_send()
    for i in range(3):
        for h in range(2):
            send_y1(h, i).wait_send()
        send_y2(i).wait_send()
    send_x2().wait_send()
    for k in range(3):
        p_own(k, own).wait_send()
    for k, o in enumerate((below, above, far, far)):
        p_cross(k, o[0]).wait_send()
    for k, o in enumerate((below, above)):
        p_on(k, o[0]).wait_send()
        for side in range(2):
            q_own(side, k, (own, across)[side]).wait_send()
            q_on(side, k, o[side]).wait_send()
    q_cross(own).wait_send()
    for k in range(shards - 1):
        norm_f_copy(k).wait_send()
    for k in range(reps - 1):
        norm_r_copy(k).wait_send()


def update_kernel(
    gathered, factor, base, mom, local,
    base_hbm, mom_hbm, mixed_hbm,
    new_base, new_mom, mixed, sem,
):
    def stores(o):
        rows = pl.ds(pl.multiple_of(o * OWN, OWN), OWN)
        return [
            pltpu.make_async_copy(src.at[rows], dst.at[rows], sem.at[k, o])
            for k, (src, dst) in enumerate(((new_base, base_hbm), (new_mom, mom_hbm), (mixed, mixed_hbm)))
        ]

    @pl.loop(0, 8)
    def _(o):
        clip = factor[o // 4, 0:1]
        for part in range(PARTS):
            scale = gathered[part, o, tile(SCALE)].astype(F32)
            for t in range(TILES):
                first = o * OWN + (part * GROUPS + t // NB) * 16
                rows = pl.ds(pl.multiple_of(first, 16), 16)
                cols = slice(t % NB * BLOCK, (t % NB + 1) * BLOCK)
                grad = clip * (gathered[part, o, code_tile(t)].astype(F32) * lane(scale, t))
                moved = 0.9 * mom[rows, cols] + grad
                shared = base[rows, cols] - 0.7 * (grad + 0.9 * moved)
                new_mom[rows, cols] = moved
                new_base[rows, cols] = shared
                mixed[rows, cols] = (0.5 * local[rows, cols].astype(F32) + 0.5 * shared).astype(BF16)
        for copy in stores(o):
            copy.start()

    @pl.loop(0, 8)
    def _(o):
        for copy in stores(o):
            copy.wait()


def local_step(local_params, base, momentum):
    rows = base.shape[0] * base.shape[1]
    shards = lax.axis_size("fsdp")
    flat = lambda a: a.reshape(rows, KV)
    dma = lambda *n: pltpu.SemaphoreType.DMA(n) if n else pltpu.SemaphoreType.DMA
    vmem = pl.BlockSpec(memory_space=pltpu.VMEM)
    hbm = pl.BlockSpec(memory_space=pltpu.HBM)
    held = pl.pallas_call(
        gather_kernel,
        out_shape=[
            pltpu.VMEM((PARTS, 8, LINES, BLOCK), BF16),
            pltpu.VMEM((2, 8, BLOCK), F32),
            pltpu.VMEM((rows, KV), F32),
            pltpu.VMEM((rows, KV), F32),
            pltpu.VMEM((rows, KV), BF16),
        ],
        in_specs=[hbm] * 3,
        out_specs=[vmem] * 5,
        scratch_shapes=[
            pltpu.VMEM((PARTS, 8, LINES, BLOCK), BF16),
            pltpu.VMEM((4, LINES, BLOCK), BF16),
            pltpu.VMEM((2, 3, LINES, BLOCK), BF16),
            pltpu.VMEM((3, TILES * 16, BLOCK), BF16),
            pltpu.VMEM((3, TILES * 16, BLOCK), BF16),
            pltpu.VMEM((TILES * 16, BLOCK), BF16),
            pltpu.VMEM((TILES * 16, BLOCK), BF16),
            pltpu.VMEM((PARTS, TILES * 16, BLOCK), F32),
            pltpu.VMEM((8, BLOCK), F32),
            pltpu.VMEM((shards - 1, 8, BLOCK), F32),
            pltpu.VMEM((8, BLOCK), F32),
            pltpu.VMEM((7, 8, BLOCK), F32),
            dma(8), dma(8), dma(),
            dma(4), dma(4), dma(2, 3), dma(2, 3), dma(), dma(), dma(3), dma(3),
            dma(18), dma(18), dma(shards - 1), dma(shards - 1), dma(7), dma(7),
        ],
        compiler_params=pltpu.CompilerParams(
            collective_id=0, has_side_effects=True, vmem_limit_bytes=26 * 2**20
        ),
        name="gather",
    )(*[pltpu.with_memory_space_constraint(flat(a), pltpu.HBM) for a in (local_params, base, momentum)])
    new_base, new_momentum, mixed = pl.pallas_call(
        update_kernel,
        out_shape=[
            jax.ShapeDtypeStruct((rows, KV), F32),
            jax.ShapeDtypeStruct((rows, KV), F32),
            jax.ShapeDtypeStruct((rows, KV), BF16),
        ],
        in_specs=[vmem] * 5,
        out_specs=[hbm] * 3,
        scratch_shapes=[
            pltpu.VMEM((rows, KV), F32),
            pltpu.VMEM((rows, KV), F32),
            pltpu.VMEM((rows, KV), BF16),
            dma(3, 8),
        ],
        compiler_params=pltpu.CompilerParams(vmem_limit_bytes=26 * 2**20),
        name="update",
    )(*held)
    return (
        new_base.reshape(base.shape),
        new_momentum.reshape(base.shape),
        mixed.reshape(local_params.shape),
    )


def solution(mesh):
    return jax.shard_map(
        local_step,
        mesh=mesh,
        in_specs=(P("rep", None, "fsdp", None), P(None, "fsdp", None), P(None, "fsdp", None)),
        out_specs=(P(None, "fsdp", None), P(None, "fsdp", None), P("rep", None, "fsdp", None)),
        check_vma=False,
    )
```

```python
import functools

import jax
import jax.numpy as jnp
from jax import lax
from jax.experimental import pallas as pl
from jax.experimental.pallas import tpu as pltpu
from jax.sharding import PartitionSpec as P

D = 8192
KV = 1024
BLOCK = 128
NB = KV // BLOCK
OWN = 128
WAVES = 2
PARTS = 2
ROWS = OWN // (WAVES * PARTS)
TILES = ROWS // 16 * NB
SCALE = TILES
LINES = (TILES + 1) * 16
SUMS = TILES * 16
MESH = pl.DeviceIdType.MESH
F32 = jnp.float32
BF16 = jnp.bfloat16


def tile(t):
    return slice(t * 16, t * 16 + 16)


def lane(packed, index):
    return packed[:, index : index + 1]


def where_in(o, piece, t):
    rows = pl.ds(pl.multiple_of(o * OWN + piece * ROWS + t // NB * 16, 16), 16)
    return rows, slice(t % NB * BLOCK, (t % NB + 1) * BLOCK)


def quantize(load, tiles, put, put_scale):
    lanes = lax.broadcasted_iota(jnp.int32, (16, BLOCK), 1)
    packed = jnp.zeros((16, BLOCK), F32)
    for t in range(tiles):
        x = load(t)
        total = jnp.sum(x * x, axis=1, keepdims=True)
        packed = jnp.where(lanes == t, total, packed)
    scale = jnp.sqrt(packed * (1.0 / BLOCK) + 1e-06).astype(BF16)
    put_scale(scale)
    inverse = 1.0 / scale.astype(F32)
    for t in range(tiles):
        put(t, jnp.clip(load(t) * lane(inverse, t), -2.5, 2.5).astype(BF16))


def gather_kernel(
    low, planes,
    local_hbm, base_hbm, mom_hbm,
    gathered, factor, base, mom, local,
    code, recv_x, recv_yf, recv_yn, recv_ym, sum_c, sum_x, recv_s, sum_y, recv_t, acc, acc_m,
    norm_own, norm_xy, norm_mid, norm_z,
    sem_local, sem_base, sem_mom,
    x1_s, x1_r, yf_s, yf_r, yn_s, yn_r, ym_s, ym_r, s_s, s_r, t_s, t_r,
    g_s, g_r, nx_s, nx_r, nz_s, nz_r,
):
    rep = lax.axis_index("rep")
    fsdp = lax.axis_index("fsdp")
    xh, y = rep // 4, rep % 4
    core, lo, z = fsdp % 2, fsdp // 2 % low, fsdp // (2 * low)
    other = 1 - xh
    partner = (other * 4 + y, fsdp)

    def along(k):
        return (xh * 4 + (y + k) % 4, fsdp)

    up, down = along(1), along(3)

    def remote(src, dst, send, recv, device):
        return pltpu.make_async_remote_copy(
            src_ref=src, dst_ref=dst, send_sem=send, recv_sem=recv, device_id=device, device_id_type=MESH
        )

    peers_xy = [(d, e) for d in range(8) for e in range(low) if d or e]
    peers_z = [(d, e) for d in range(planes) for e in range(2) if d or e]

    def device_xy(d, e):
        return ((rep + d) % 8, (z * low + (lo + e) % low) * 2 + core)

    def device_z(d, e):
        return (rep, ((z + d) % planes * low + lo) * 2 + (core + e) % 2)

    def owner(i):
        return jnp.where(i < 4, other, xh) * 4 + (y + 1 + i) % 4

    def loads(w, i):
        start = owner(i) * OWN + w * (OWN // WAVES)
        rows = pl.ds(pl.multiple_of(start, OWN // WAVES), OWN // WAVES)
        return (
            pltpu.make_async_copy(local_hbm.at[rows], local.at[rows], sem_local.at[w, i]),
            pltpu.make_async_copy(base_hbm.at[rows], base.at[rows], sem_base.at[w, i]),
        )

    def start_loads(w, i):
        for copy in loads(w, i):
            copy.start()

    start_loads(0, 0)
    barrier = pltpu.get_barrier_semaphore()
    for d, e in peers_xy:
        pl.semaphore_signal(barrier, inc=1, device_id=device_xy(d, e), device_id_type=MESH)
    start_loads(0, 1)
    for d, e in peers_z:
        pl.semaphore_signal(barrier, inc=1, device_id=device_z(d, e), device_id_type=MESH)
    start_loads(0, 2)
    start_loads(0, 3)
    mom_copy = pltpu.make_async_copy(mom_hbm, mom, sem_mom)

    def quantize_owner(w, i):
        o = owner(i)

        def load(t):
            at = where_in(o, w * PARTS + t // TILES, t % TILES)
            return base[at] - local[at].astype(F32)

        def put(t, value):
            code[w, t // TILES, o, tile(t % TILES)] = value

        def put_scale(value):
            for part in range(PARTS):
                code[w, part, o, tile(SCALE)] = value

        quantize(load, PARTS * TILES, put, put_scale)

    def rises(w, h):
        return (h + w) % 2 == 1

    def near_index(w, h):
        return 0 if rises(w, h) else 2

    def send_x1(w, i):
        return remote(code.at[w, 0, owner(i)], recv_x.at[w, i], x1_s.at[w, i], x1_r.at[w, i], partner)

    def coded(w, h, i):
        return code.at[w, 1, owner(i + 4 - 4 * h)]

    def send_yf(w, h):
        to = up if rises(w, h) else down
        return remote(coded(w, h, 1), recv_yf.at[w, h], yf_s.at[w, h], yf_r.at[w, h], to)

    def send_yn(w, h):
        to = down if rises(w, h) else up
        return remote(coded(w, h, 2 - near_index(w, h)), recv_yn.at[w, h], yn_s.at[w, h], yn_r.at[w, h], to)

    def send_ym(w, h):
        to = up if rises(w, h) else down
        return remote(sum_c.at[w, h], recv_ym.at[w, h], ym_s.at[w, h], ym_r.at[w, h], to)

    def send_s(w, k):
        near = near_index(w, 0)
        to = up if rises(w, 0) == (k != 1) else down
        src = sum_x.at[w, (1, 2 - near, near)[k]]
        return remote(src, recv_s.at[w, k], s_s.at[w, k], s_r.at[w, k], to)

    def send_t(w):
        return remote(sum_y.at[w], recv_t.at[w], t_s.at[w], t_r.at[w], partner)

    def add(pieces, part, put):
        scales = [ref[tile(SCALE)].astype(F32) if has else None for ref, has in pieces]
        for t in range(TILES):
            total = None
            for (ref, _), scale in zip(pieces, scales):
                value = ref[tile(t)].astype(F32)
                if scale is not None:
                    value = value * lane(scale, part * TILES + t)
                total = value if total is None else total + value
            put(t, total)

    def putter(ref, index):
        def put(t, value):
            ref[(*index, tile(t))] = value.astype(ref.dtype)

        return put

    def merge_y(w, h):
        send_yf(w, h).wait_recv()
        pieces = [(coded(w, h, near_index(w, h)), True), (recv_yf.at[w, h], True)]
        add(pieces, 1, putter(sum_c, (w, h)))
        send_ym(w, h).start()

    def sum_pair(w, i):
        send_x1(w, i).wait_recv()
        pieces = [(code.at[w, 0, owner(i + 4)], True), (recv_x.at[w, i], True)]
        near = near_index(w, 0)
        if i == 3:
            add(pieces, 0, putter(acc, (w, 0)))
        elif i == near:
            add(pieces, 0, putter(acc_m, (w,)))
        else:
            add(pieces, 0, putter(sum_x, (w, i)))
            send_s(w, 0 if i == 1 else 1).start()

    def merge_s(w):
        send_s(w, 0).wait_recv()
        pieces = [(acc_m.at[w], False), (recv_s.at[w, 0], False)]
        add(pieces, 0, putter(sum_x, (w, near_index(w, 0))))
        send_s(w, 2).start()

    def sum_column(w, h):
        send_ym(w, h).wait_recv()
        send_yn(w, h).wait_recv()
        pieces = [(coded(w, h, 3), True), (recv_ym.at[w, h], False), (recv_yn.at[w, h], True)]
        add(pieces, 1, putter(sum_y, (w,)) if h else putter(acc, (w, 1)))
        if h:
            send_t(w).start()

    def average(w, part):
        if part == 0:
            send_s(w, 1).wait_recv()
            send_s(w, 2).wait_recv()
            received = [recv_s.at[w, 1], recv_s.at[w, 2]]
        else:
            send_t(w).wait_recv()
            received = [recv_t.at[w]]
        for t in range(TILES):
            total = acc[w, part, tile(t)]
            for ref in received:
                total = total + ref[tile(t)].astype(F32)
            acc[w, part, tile(t)] = total * 0.125

        def load(t):
            return acc[w, part, tile(t)]

        def put(t, value):
            gathered[w, part, rep, tile(t)] = value

        def put_scale(value):
            gathered[w, part, rep, tile(SCALE)] = value

        quantize(load, TILES, put, put_scale)

    def squares(w, part):
        scale = gathered[w, part, rep, tile(SCALE)].astype(F32)
        total = jnp.zeros((16, BLOCK), F32)
        for t in range(TILES):
            step = gathered[w, part, rep, tile(t)].astype(F32) * lane(scale, t)
            total = total + step * step
        return total[:8] + total[8:]

    def move(k, w, part, o, device):
        ref = gathered.at[w, part, o]
        return remote(ref, ref, g_s.at[w, k], g_r.at[w, k], device)

    def near(d):
        return xh * 4 + (y + d) % 4, other * 4 + (y + d) % 4

    below, above, far = near(3), near(1), near(2)
    own, across = near(0)
    side = (below, above)

    def p_own(w, k, o):
        return move(k, w, 0, o, (up, down, partner)[k])

    def p_cross(w, k, o):
        return move((3, 4, 6)[k], w, 0, o, partner)

    def p_way(w):
        return 0 if w % 2 else 1

    def p_on(w, o):
        return move(5, w, 0, o, (up, down)[p_way(w)])

    def q_cross(w, o):
        return move(7, w, 1, o, partner)

    def q_own(w, k, o):
        return move(8 + k, w, 1, o, (up, down)[k])

    def q_across(w, k, o):
        return move(10 + k, w, 1, o, (up, down)[k])

    def q_on(w, k, o):
        return move(12 + k, w, 1, o, (up, down)[k])

    def gather_p(w):
        for k in range(3):
            p_own(w, k, own).start()

    def gather_q(w):
        q_cross(w, own).start()
        for k in range(2):
            q_own(w, k, own).start()

    def pass_p(w):
        for k in (p_way(w), 1 - p_way(w)):
            p_own(w, k, side[k][0]).wait_recv()
            if k == p_way(w):
                p_on(w, side[k][0]).start()
            p_cross(w, k, side[k][0]).start()

    def pass_p_far(w):
        p_on(w, far[0]).wait_recv()
        p_cross(w, 2, far[0]).start()

    def pass_q(w):
        q_cross(w, across).wait_recv()
        for k in range(2):
            q_across(w, k, across).start()

    def pass_q_own(w):
        q_own(w, 0, below[0]).wait_recv()
        q_on(w, 0, below[0]).start()

    def pass_q_across(w):
        q_across(w, 1, above[1]).wait_recv()
        q_on(w, 1, above[1]).start()

    @pl.loop(0, 8)
    def _(i):
        for copy in loads(0, i):
            copy.wait()

        @pl.when(i < 4)
        def _():
            start_loads(0, i + 4)

        @pl.when(i >= 4)
        def _():
            start_loads(1, i - 4)

        quantize_owner(0, i)

        @pl.when(i == 0)
        def _():
            pl.semaphore_wait(barrier, len(peers_xy) + len(peers_z))

        @pl.when(i < 4)
        def _():
            send_x1(0, i).start()

        for h in range(2):
            first = 4 - 4 * h

            @pl.when(i == first + 1)
            def _():
                send_yf(0, h).start()

            @pl.when(i == first + 2 - near_index(0, h))
            def _():
                send_yn(0, h).start()

    def second_wave(first, last):
        @pl.loop(first, last)
        def _(i):
            for copy in loads(1, i):
                copy.wait()

            @pl.when(i < 4)
            def _():
                start_loads(1, i + 4)

            quantize_owner(1, i)

            @pl.when(i < 4)
            def _():
                send_x1(1, i).start()

            for h in range(2):
                start = 4 - 4 * h

                @pl.when(i == start + 1)
                def _():
                    send_yf(1, h).start()

                @pl.when(i == start + 2 - near_index(1, h))
                def _():
                    send_yn(1, h).start()

    second_wave(0, 2)
    merge_y(0, 1)
    sum_pair(0, 0)
    second_wave(2, 4)
    merge_y(0, 0)
    sum_pair(0, 1)
    second_wave(4, 8)
    mom_copy.start()
    sum_pair(0, 2)
    merge_y(1, 1)
    sum_column(0, 1)
    sum_pair(0, 3)
    sum_column(0, 0)
    merge_s(0)
    sum_pair(1, 0)
    merge_y(1, 0)
    sum_pair(1, 1)
    sum_column(1, 1)
    sum_pair(1, 2)
    sum_column(1, 0)
    average(0, 0)
    gather_p(0)
    sum_pair(1, 3)
    merge_s(1)
    average(0, 1)
    gather_q(0)
    pass_p(0)
    average(1, 1)
    gather_q(1)
    average(1, 0)
    gather_p(1)
    norm_own[...] = squares(0, 0) + squares(0, 1) + squares(1, 0) + squares(1, 1)

    def norm_xy_copy(k):
        return remote(norm_own, norm_xy.at[k], nx_s.at[k], nx_r.at[k], device_xy(*peers_xy[k]))

    def norm_z_copy(k):
        return remote(norm_mid, norm_z.at[k], nz_s.at[k], nz_r.at[k], device_z(*peers_z[k]))

    for k in range(len(peers_xy)):
        norm_xy_copy(k).start()
    pass_q_own(0)
    pass_q(0)
    pass_p_far(0)
    pass_q_own(1)
    pass_p(1)
    pass_q(1)
    pass_q_across(0)

    same = norm_own[...]
    cross = jnp.zeros((8, BLOCK), F32)
    for k, (d, e) in enumerate(peers_xy):
        norm_xy_copy(k).wait_recv()
        mine = ((rep + 8 - d) % 8 // 4 == xh).astype(F32)
        same = same + mine * norm_xy[k]
        cross = cross + (1.0 - mine) * norm_xy[k]
    norm_mid[xh] = same
    norm_mid[other] = cross
    for k in range(len(peers_z)):
        norm_z_copy(k).start()
    pass_q_across(1)
    pass_p_far(1)
    for k in range(len(peers_z)):
        norm_z_copy(k).wait_recv()
    for m in range(2):
        value = norm_mid[m]
        for k in range(len(peers_z)):
            value = value + norm_z[k, m]
        total = jnp.sum(jnp.sum(value, axis=1, keepdims=True), axis=0, keepdims=True)
        norm = jnp.sqrt(jnp.broadcast_to(total, (8, BLOCK)) + 1e-06)
        factor[m] = jnp.minimum(1.0, 0.25 * jnp.sqrt(F32(D * KV)) / norm)

    mom_copy.wait()
    for w in range(WAVES):
        p_own(w, 2, across).wait_recv()
        for k, o in enumerate((below, above, far)):
            p_cross(w, k, o[1]).wait_recv()
        q_own(w, 1, above[0]).wait_recv()
        q_across(w, 0, below[1]).wait_recv()
        q_on(w, 0, far[0]).wait_recv()
        q_on(w, 1, far[1]).wait_recv()
        for i in range(4):
            send_x1(w, i).wait_send()
        for h in range(2):
            send_yf(w, h).wait_send()
            send_yn(w, h).wait_send()
            send_ym(w, h).wait_send()
        for k in range(3):
            send_s(w, k).wait_send()
            p_own(w, k, own).wait_send()
            p_cross(w, k, (below, above, far)[k][0]).wait_send()
        send_t(w).wait_send()
        p_on(w, side[p_way(w)][0]).wait_send()
        q_cross(w, own).wait_send()
        for k in range(2):
            q_own(w, k, own).wait_send()
            q_across(w, k, across).wait_send()
            q_on(w, k, (below[0], above[1])[k]).wait_send()
    for k in range(len(peers_xy)):
        norm_xy_copy(k).wait_send()
    for k in range(len(peers_z)):
        norm_z_copy(k).wait_send()


def update_kernel(
    gathered, factor, base, mom, local,
    base_hbm, mom_hbm, mixed_hbm,
    new_base, new_mom, mixed, sem,
):
    def stores(o):
        rows = pl.ds(pl.multiple_of(o * OWN, OWN), OWN)
        return [
            pltpu.make_async_copy(src.at[rows], dst.at[rows], sem.at[k, o])
            for k, (src, dst) in enumerate(((new_base, base_hbm), (new_mom, mom_hbm), (mixed, mixed_hbm)))
        ]

    @pl.loop(0, 8)
    def _(o):
        clip = factor[o // 4, 0:1]
        for piece in range(WAVES * PARTS):
            w, part = piece // PARTS, piece % PARTS
            scale = gathered[w, part, o, tile(SCALE)].astype(F32)
            for t in range(TILES):
                at = where_in(o, piece, t)
                grad = clip * (gathered[w, part, o, tile(t)].astype(F32) * lane(scale, t))
                moved = 0.9 * mom[at] + grad
                shared = base[at] - 0.7 * (grad + 0.9 * moved)
                new_mom[at] = moved
                new_base[at] = shared
                mixed[at] = (0.5 * local[at].astype(F32) + 0.5 * shared).astype(BF16)
        for copy in stores(o):
            copy.start()

    @pl.loop(0, 8)
    def _(o):
        for copy in stores(o):
            copy.wait()


def local_step(local_params, base, momentum):
    rows = base.shape[0] * base.shape[1]
    shards = lax.axis_size("fsdp")
    flat = lambda a: a.reshape(rows, KV)
    dma = lambda *n: pltpu.SemaphoreType.DMA(n) if n else pltpu.SemaphoreType.DMA
    vmem = pl.BlockSpec(memory_space=pltpu.VMEM)
    hbm = pl.BlockSpec(memory_space=pltpu.HBM)
    low = 2 if shards % 4 == 0 else 1
    planes = shards // (2 * low)
    waves = lambda *shape: pltpu.VMEM((WAVES, *shape, BLOCK), BF16)
    held = pl.pallas_call(
        functools.partial(gather_kernel, low, planes),
        out_shape=[
            waves(PARTS, 8, LINES),
            pltpu.VMEM((2, 8, BLOCK), F32),
            pltpu.VMEM((rows, KV), F32),
            pltpu.VMEM((rows, KV), F32),
            pltpu.VMEM((rows, KV), BF16),
        ],
        in_specs=[hbm] * 3,
        out_specs=[vmem] * 5,
        scratch_shapes=[
            waves(PARTS, 8, LINES),
            waves(4, LINES),
            waves(2, LINES), waves(2, LINES), waves(2, SUMS), waves(2, SUMS),
            waves(3, SUMS), waves(3, SUMS), waves(SUMS), waves(SUMS),
            pltpu.VMEM((WAVES, PARTS, SUMS, BLOCK), F32),
            pltpu.VMEM((WAVES, SUMS, BLOCK), F32),
            pltpu.VMEM((8, BLOCK), F32),
            pltpu.VMEM((8 * low - 1, 8, BLOCK), F32),
            pltpu.VMEM((2, 8, BLOCK), F32),
            pltpu.VMEM((2 * planes - 1, 2, 8, BLOCK), F32),
            dma(2, 8), dma(2, 8), dma(),
            dma(2, 4), dma(2, 4), dma(2, 2), dma(2, 2), dma(2, 2), dma(2, 2), dma(2, 2), dma(2, 2),
            dma(2, 3), dma(2, 3), dma(2), dma(2),
            dma(2, 14), dma(2, 14),
            dma(8 * low - 1), dma(8 * low - 1), dma(2 * planes - 1), dma(2 * planes - 1),
        ],
        compiler_params=pltpu.CompilerParams(
            collective_id=0, has_side_effects=True, vmem_limit_bytes=26 * 2**20
        ),
        name="gather",
    )(*[pltpu.with_memory_space_constraint(flat(a), pltpu.HBM) for a in (local_params, base, momentum)])
    new_base, new_momentum, mixed = pl.pallas_call(
        update_kernel,
        out_shape=[
            jax.ShapeDtypeStruct((rows, KV), F32),
            jax.ShapeDtypeStruct((rows, KV), F32),
            jax.ShapeDtypeStruct((rows, KV), BF16),
        ],
        in_specs=[vmem] * 5,
        out_specs=[hbm] * 3,
        scratch_shapes=[
            pltpu.VMEM((rows, KV), F32),
            pltpu.VMEM((rows, KV), F32),
            pltpu.VMEM((rows, KV), BF16),
            dma(3, 8),
        ],
        compiler_params=pltpu.CompilerParams(vmem_limit_bytes=26 * 2**20),
        name="update",
    )(*held)
    return (
        new_base.reshape(base.shape),
        new_momentum.reshape(base.shape),
        mixed.reshape(local_params.shape),
    )


def solution(mesh):
    return jax.shard_map(
        local_step,
        mesh=mesh,
        in_specs=(P("rep", None, "fsdp", None), P(None, "fsdp", None), P(None, "fsdp", None)),
        out_specs=(P(None, "fsdp", None), P(None, "fsdp", None), P("rep", None, "fsdp", None)),
        check_vma=False,
    )
```

```python
import functools

import jax
import jax.numpy as jnp
from jax import lax
from jax.experimental import pallas as pl
from jax.experimental.pallas import tpu as pltpu
from jax.sharding import PartitionSpec as P

D = 8192
KV = 1024
BLOCK = 128
NB = KV // BLOCK
OWN = 128
WAVES = 2
PARTS = 2
ROWS = OWN // (WAVES * PARTS)
TILES = ROWS // 16 * NB
SCALE = TILES
LINES = (TILES + 1) * 16
SUMS = TILES * 16
MESH = pl.DeviceIdType.MESH
F32 = jnp.float32
BF16 = jnp.bfloat16


def tile(t):
    return slice(t * 16, t * 16 + 16)


def lane(packed, index):
    return packed[:, index : index + 1]


def where_in(o, piece, t):
    rows = pl.ds(pl.multiple_of(o * OWN + piece * ROWS + t // NB * 16, 16), 16)
    return rows, slice(t % NB * BLOCK, (t % NB + 1) * BLOCK)


def quantize(load, tiles, put, put_scale):
    lanes = lax.broadcasted_iota(jnp.int32, (16, BLOCK), 1)
    packed = jnp.zeros((16, BLOCK), F32)
    for t in range(tiles):
        x = load(t)
        total = jnp.sum(x * x, axis=1, keepdims=True)
        packed = jnp.where(lanes == t, total, packed)
    scale = jnp.sqrt(packed * (1.0 / BLOCK) + 1e-06).astype(BF16)
    put_scale(scale)
    inverse = 1.0 / scale.astype(F32)
    for t in range(tiles):
        put(t, jnp.clip(load(t) * lane(inverse, t), -2.5, 2.5).astype(BF16))


def gather_kernel(
    low, planes,
    local_hbm, base_hbm, mom_hbm,
    gathered, factor, base, mom, local,
    code, recv_x, recv_yf, recv_yn, recv_ym, sum_c, sum_x, recv_s, sum_y, recv_t, acc, acc_m,
    norm_xy, norm_mid, norm_core, norm_z, entered,
    sem_local, sem_base, sem_mom,
    x1_s, x1_r, yf_s, yf_r, yn_s, yn_r, ym_s, ym_r, s_s, s_r, t_s, t_r,
    g_s, g_r, nx_s, nx_r, nc_s, nc_r, nz_s, nz_r,
):
    rep = lax.axis_index("rep")
    fsdp = lax.axis_index("fsdp")
    xh, y = rep // 4, rep % 4
    core, lo, z = fsdp % 2, fsdp // 2 % low, fsdp // (2 * low)
    other = 1 - xh
    partner = (other * 4 + y, fsdp)

    def along(k):
        return (xh * 4 + (y + k) % 4, fsdp)

    up, down = along(1), along(3)

    def remote(src, dst, send, recv, device):
        return pltpu.make_async_remote_copy(
            src_ref=src, dst_ref=dst, send_sem=send, recv_sem=recv, device_id=device, device_id_type=MESH
        )

    places = 8 * low
    place = rep * low + lo

    def in_plane(p, at_core):
        p = p % places
        return (p // low, (z * low + p % low) * 2 + at_core)

    def in_line(plane, at_core):
        return (rep, (plane % planes * low + lo) * 2 + at_core)

    chips = [partner[0] * low + lo, up[0] * low + lo, down[0] * low + lo]
    if low > 1:
        chips.append(rep * low + 1 - lo)

    def owner(i):
        return jnp.where(i < 4, other, xh) * 4 + (y + 1 + i) % 4

    def loads(w, i):
        start = owner(i) * OWN + w * (OWN // WAVES)
        rows = pl.ds(pl.multiple_of(start, OWN // WAVES), OWN // WAVES)
        return (
            pltpu.make_async_copy(local_hbm.at[rows], local.at[rows], sem_local.at[w, i]),
            pltpu.make_async_copy(base_hbm.at[rows], base.at[rows], sem_base.at[w, i]),
        )

    def start_loads(w, i):
        for copy in loads(w, i):
            copy.start()

    start_loads(0, 0)
    barrier = pltpu.get_barrier_semaphore()
    for p in chips:
        pl.semaphore_signal(barrier, inc=1, device_id=in_plane(p, 0), device_id_type=MESH)

    @pl.when(core == 1)
    def _():
        pl.semaphore_signal(barrier, inc=1, device_id=in_line(z, 0), device_id_type=MESH)

    def enter():
        @pl.when(core == 0)
        def _():
            pl.semaphore_wait(barrier, 2 * len(chips) + 1)
            pl.semaphore_signal(entered, inc=1, device_id=in_line(z, 1), device_id_type=MESH)

        @pl.when(core == 1)
        def _():
            pl.semaphore_wait(entered, 1)
            for d in range(1, planes):
                pl.semaphore_signal(barrier, inc=1, device_id=in_line(z + d, 1), device_id_type=MESH)

    start_loads(0, 1)
    start_loads(0, 2)
    start_loads(0, 3)
    mom_copy = pltpu.make_async_copy(mom_hbm, mom, sem_mom)

    def quantize_owner(w, i):
        o = owner(i)

        def load(t):
            at = where_in(o, w * PARTS + t // TILES, t % TILES)
            return base[at] - local[at].astype(F32)

        def put(t, value):
            code[w, t // TILES, o, tile(t % TILES)] = value

        def put_scale(value):
            for part in range(PARTS):
                code[w, part, o, tile(SCALE)] = value

        quantize(load, PARTS * TILES, put, put_scale)

    def rises(w, h):
        return (h + w) % 2 == 1

    def near_index(w, h):
        return 0 if rises(w, h) else 2

    def send_x1(w, i):
        return remote(code.at[w, 0, owner(i)], recv_x.at[w, i], x1_s.at[w, i], x1_r.at[w, i], partner)

    def coded(w, h, i):
        return code.at[w, 1, owner(i + 4 - 4 * h)]

    def send_yf(w, h):
        to = up if rises(w, h) else down
        return remote(coded(w, h, 1), recv_yf.at[w, h], yf_s.at[w, h], yf_r.at[w, h], to)

    def send_yn(w, h):
        to = down if rises(w, h) else up
        return remote(coded(w, h, 2 - near_index(w, h)), recv_yn.at[w, h], yn_s.at[w, h], yn_r.at[w, h], to)

    def send_ym(w, h):
        to = up if rises(w, h) else down
        return remote(sum_c.at[w, h], recv_ym.at[w, h], ym_s.at[w, h], ym_r.at[w, h], to)

    def send_s(w, k):
        near = near_index(w, 0)
        to = up if rises(w, 0) == (k != 1) else down
        src = sum_x.at[w, (1, 2 - near, near)[k]]
        return remote(src, recv_s.at[w, k], s_s.at[w, k], s_r.at[w, k], to)

    def send_t(w):
        return remote(sum_y.at[w], recv_t.at[w], t_s.at[w], t_r.at[w], partner)

    def add(pieces, part, put):
        scales = [ref[tile(SCALE)].astype(F32) if has else None for ref, has in pieces]
        for t in range(TILES):
            total = None
            for (ref, _), scale in zip(pieces, scales):
                value = ref[tile(t)].astype(F32)
                if scale is not None:
                    value = value * lane(scale, part * TILES + t)
                total = value if total is None else total + value
            put(t, total)

    def putter(ref, index):
        def put(t, value):
            ref[(*index, tile(t))] = value.astype(ref.dtype)

        return put

    def merge_y(w, h):
        send_yf(w, h).wait_recv()
        pieces = [(coded(w, h, near_index(w, h)), True), (recv_yf.at[w, h], True)]
        add(pieces, 1, putter(sum_c, (w, h)))
        send_ym(w, h).start()

    def sum_pair(w, i):
        send_x1(w, i).wait_recv()
        pieces = [(code.at[w, 0, owner(i + 4)], True), (recv_x.at[w, i], True)]
        near = near_index(w, 0)
        if i == 3:
            add(pieces, 0, putter(acc, (w, 0)))
        elif i == near:
            add(pieces, 0, putter(acc_m, (w,)))
        else:
            add(pieces, 0, putter(sum_x, (w, i)))
            send_s(w, 0 if i == 1 else 1).start()

    def merge_s(w):
        send_s(w, 0).wait_recv()
        pieces = [(acc_m.at[w], False), (recv_s.at[w, 0], False)]
        add(pieces, 0, putter(sum_x, (w, near_index(w, 0))))
        send_s(w, 2).start()

    def sum_column(w, h):
        send_ym(w, h).wait_recv()
        send_yn(w, h).wait_recv()
        pieces = [(coded(w, h, 3), True), (recv_ym.at[w, h], False), (recv_yn.at[w, h], True)]
        add(pieces, 1, putter(sum_y, (w,)) if h else putter(acc, (w, 1)))
        if h:
            send_t(w).start()

    def average(w, part):
        if part == 0:
            send_s(w, 1).wait_recv()
            send_s(w, 2).wait_recv()
            received = [recv_s.at[w, 1], recv_s.at[w, 2]]
        else:
            send_t(w).wait_recv()
            received = [recv_t.at[w]]
        for t in range(TILES):
            total = acc[w, part, tile(t)]
            for ref in received:
                total = total + ref[tile(t)].astype(F32)
            acc[w, part, tile(t)] = total * 0.125

        def load(t):
            return acc[w, part, tile(t)]

        def put(t, value):
            gathered[w, part, rep, tile(t)] = value

        def put_scale(value):
            gathered[w, part, rep, tile(SCALE)] = value

        quantize(load, TILES, put, put_scale)

    def squares(w, part):
        scale = gathered[w, part, rep, tile(SCALE)].astype(F32)
        total = jnp.zeros((16, BLOCK), F32)
        for t in range(TILES):
            step = gathered[w, part, rep, tile(t)].astype(F32) * lane(scale, t)
            total = total + step * step
        return total[:8] + total[8:]

    def move(k, w, part, o, device):
        ref = gathered.at[w, part, o]
        return remote(ref, ref, g_s.at[w, k], g_r.at[w, k], device)

    def near(d):
        return xh * 4 + (y + d) % 4, other * 4 + (y + d) % 4

    below, above, far = near(3), near(1), near(2)
    own, across = near(0)
    side = (below, above)

    def p_own(w, k, o):
        return move(k, w, 0, o, (up, down, partner)[k])

    def p_cross(w, k, o):
        return move((3, 4, 6)[k], w, 0, o, partner)

    def p_way(w):
        return 0 if w % 2 else 1

    def p_on(w, o):
        return move(5, w, 0, o, (up, down)[p_way(w)])

    def q_cross(w, o):
        return move(7, w, 1, o, partner)

    def q_own(w, k, o):
        return move(8 + k, w, 1, o, (up, down)[k])

    def q_across(w, k, o):
        return move(10 + k, w, 1, o, (up, down)[k])

    def q_on(w, k, o):
        return move(12 + k, w, 1, o, (up, down)[k])

    def gather_p(w):
        for k in range(3):
            p_own(w, k, own).start()

    def gather_q(w):
        q_cross(w, own).start()
        for k in range(2):
            q_own(w, k, own).start()

    def pass_p(w):
        for k in (p_way(w), 1 - p_way(w)):
            p_own(w, k, side[k][0]).wait_recv()
            if k == p_way(w):
                p_on(w, side[k][0]).start()
            p_cross(w, k, side[k][0]).start()

    def pass_p_far(w):
        p_on(w, far[0]).wait_recv()
        p_cross(w, 2, far[0]).start()

    def pass_q(w):
        q_cross(w, across).wait_recv()
        for k in range(2):
            q_across(w, k, across).start()

    def pass_q_own(w):
        q_own(w, 0, below[0]).wait_recv()
        q_on(w, 0, below[0]).start()

    def pass_q_across(w):
        q_across(w, 1, above[1]).wait_recv()
        q_on(w, 1, above[1]).start()

    @pl.loop(0, 8)
    def _(i):
        for copy in loads(0, i):
            copy.wait()

        @pl.when(i < 4)
        def _():
            start_loads(0, i + 4)

        @pl.when(i >= 4)
        def _():
            start_loads(1, i - 4)

        quantize_owner(0, i)

        @pl.when(i == 0)
        def _():
            enter()

        @pl.when(i < 4)
        def _():
            send_x1(0, i).start()

        for h in range(2):
            first = 4 - 4 * h

            @pl.when(i == first + 1)
            def _():
                send_yf(0, h).start()

            @pl.when(i == first + 2 - near_index(0, h))
            def _():
                send_yn(0, h).start()

    def second_wave(first, last):
        @pl.loop(first, last)
        def _(i):
            for copy in loads(1, i):
                copy.wait()

            @pl.when(i < 4)
            def _():
                start_loads(1, i + 4)

            quantize_owner(1, i)

            @pl.when(i < 4)
            def _():
                send_x1(1, i).start()

            for h in range(2):
                start = 4 - 4 * h

                @pl.when(i == start + 1)
                def _():
                    send_yf(1, h).start()

                @pl.when(i == start + 2 - near_index(1, h))
                def _():
                    send_yn(1, h).start()

    second_wave(0, 2)
    merge_y(0, 1)
    sum_pair(0, 0)
    second_wave(2, 4)
    merge_y(0, 0)
    sum_pair(0, 1)
    second_wave(4, 8)
    mom_copy.start()
    sum_pair(0, 2)
    merge_y(1, 1)
    sum_column(0, 1)
    sum_pair(0, 3)
    sum_column(0, 0)
    merge_s(0)
    sum_pair(1, 0)
    merge_y(1, 0)
    sum_pair(1, 1)
    sum_column(1, 1)
    sum_pair(1, 2)
    sum_column(1, 0)
    average(0, 0)
    gather_p(0)
    sum_pair(1, 3)
    merge_s(1)
    average(0, 1)
    gather_q(0)
    pass_p(0)
    early = squares(0, 0) + squares(0, 1)
    average(1, 1)
    gather_q(1)
    early = early + squares(1, 1)
    average(1, 0)

    def norm_xy_copy(k, p):
        slot = norm_xy.at[p]
        return remote(slot, slot, nx_s.at[k], nx_r.at[p], in_plane(place + k, core))

    def norm_core_copy():
        return remote(norm_mid, norm_core, nc_s, nc_r, in_line(z, 1))

    def norm_z_copy(d, e, plane):
        slot = norm_z.at[plane]
        return remote(slot, slot, nz_s.at[d, e], nz_r.at[plane], in_line(z + d, e))

    line_peers = [(d, e) for d in range(planes) for e in range(2) if (d, e) != (0, 1)]

    norm_xy[place] = early + squares(1, 0)
    for k in range(1, places):
        norm_xy_copy(k, place).start()
    gather_p(1)
    pass_q_own(0)
    pass_q(0)
    pass_p_far(0)
    pass_q_own(1)
    pass_p(1)
    pass_q(1)
    pass_q_across(0)

    for k in range(1, places):
        norm_xy_copy(k, (place + k) % places).wait_recv()
    for m in range(2):
        total = norm_xy[m * 4 * low]
        for p in range(1, 4 * low):
            total = total + norm_xy[m * 4 * low + p]
        norm_mid[m] = total

    @pl.when(core == 0)
    def _():
        norm_core_copy().start()

    @pl.when(core == 1)
    def _():
        norm_core_copy().wait_recv()
        norm_z[z] = norm_mid[...] + norm_core[...]
        if planes > 1:
            pl.semaphore_wait(barrier, planes - 1)
        for d, e in line_peers:
            norm_z_copy(d, e, z).start()

    pass_q_across(1)
    pass_p_far(1)

    @pl.when(core == 0)
    def _():
        norm_z_copy(0, 0, z).wait_recv()

    for d in range(1, planes):
        norm_z_copy(d, 0, (z + d) % planes).wait_recv()
    for m in range(2):
        value = norm_z[0, m]
        for plane in range(1, planes):
            value = value + norm_z[plane, m]
        total = jnp.sum(jnp.sum(value, axis=1, keepdims=True), axis=0, keepdims=True)
        norm = jnp.sqrt(jnp.broadcast_to(total, (8, BLOCK)) + 1e-06)
        factor[m] = jnp.minimum(1.0, 0.25 * jnp.sqrt(F32(D * KV)) / norm)

    mom_copy.wait()
    for w in range(WAVES):
        p_own(w, 2, across).wait_recv()
        for k, o in enumerate((below, above, far)):
            p_cross(w, k, o[1]).wait_recv()
        q_own(w, 1, above[0]).wait_recv()
        q_across(w, 0, below[1]).wait_recv()
        q_on(w, 0, far[0]).wait_recv()
        q_on(w, 1, far[1]).wait_recv()
        for i in range(4):
            send_x1(w, i).wait_send()
        for h in range(2):
            send_yf(w, h).wait_send()
            send_yn(w, h).wait_send()
            send_ym(w, h).wait_send()
        for k in range(3):
            send_s(w, k).wait_send()
            p_own(w, k, own).wait_send()
            p_cross(w, k, (below, above, far)[k][0]).wait_send()
        send_t(w).wait_send()
        p_on(w, side[p_way(w)][0]).wait_send()
        q_cross(w, own).wait_send()
        for k in range(2):
            q_own(w, k, own).wait_send()
            q_across(w, k, across).wait_send()
            q_on(w, k, (below[0], above[1])[k]).wait_send()
    for k in range(1, places):
        norm_xy_copy(k, place).wait_send()

    @pl.when(core == 0)
    def _():
        norm_core_copy().wait_send()

    @pl.when(core == 1)
    def _():
        for d, e in line_peers:
            norm_z_copy(d, e, z).wait_send()


def update_kernel(
    gathered, factor, base, mom, local,
    base_hbm, mom_hbm, mixed_hbm,
    new_base, new_mom, mixed, sem,
):
    def stores(o):
        rows = pl.ds(pl.multiple_of(o * OWN, OWN), OWN)
        return [
            pltpu.make_async_copy(src.at[rows], dst.at[rows], sem.at[k, o])
            for k, (src, dst) in enumerate(((new_base, base_hbm), (new_mom, mom_hbm), (mixed, mixed_hbm)))
        ]

    @pl.loop(0, 8)
    def _(o):
        clip = factor[o // 4, 0:1]
        for piece in range(WAVES * PARTS):
            w, part = piece // PARTS, piece % PARTS
            scale = gathered[w, part, o, tile(SCALE)].astype(F32)
            for t in range(TILES):
                at = where_in(o, piece, t)
                grad = clip * (gathered[w, part, o, tile(t)].astype(F32) * lane(scale, t))
                moved = 0.9 * mom[at] + grad
                shared = base[at] - 0.7 * (grad + 0.9 * moved)
                new_mom[at] = moved
                new_base[at] = shared
                mixed[at] = (0.5 * local[at].astype(F32) + 0.5 * shared).astype(BF16)
        for copy in stores(o):
            copy.start()

    @pl.loop(0, 8)
    def _(o):
        for copy in stores(o):
            copy.wait()


def local_step(local_params, base, momentum):
    rows = base.shape[0] * base.shape[1]
    shards = lax.axis_size("fsdp")
    flat = lambda a: a.reshape(rows, KV)
    dma = lambda *n: pltpu.SemaphoreType.DMA(n) if n else pltpu.SemaphoreType.DMA
    vmem = pl.BlockSpec(memory_space=pltpu.VMEM)
    hbm = pl.BlockSpec(memory_space=pltpu.HBM)
    low = 2 if shards % 4 == 0 else 1
    planes = shards // (2 * low)
    waves = lambda *shape: pltpu.VMEM((WAVES, *shape, BLOCK), BF16)
    held = pl.pallas_call(
        functools.partial(gather_kernel, low, planes),
        out_shape=[
            waves(PARTS, 8, LINES),
            pltpu.VMEM((2, 8, BLOCK), F32),
            pltpu.VMEM((rows, KV), F32),
            pltpu.VMEM((rows, KV), F32),
            pltpu.VMEM((rows, KV), BF16),
        ],
        in_specs=[hbm] * 3,
        out_specs=[vmem] * 5,
        scratch_shapes=[
            waves(PARTS, 8, LINES),
            waves(4, LINES),
            waves(2, LINES), waves(2, LINES), waves(2, SUMS), waves(2, SUMS),
            waves(3, SUMS), waves(3, SUMS), waves(SUMS), waves(SUMS),
            pltpu.VMEM((WAVES, PARTS, SUMS, BLOCK), F32),
            pltpu.VMEM((WAVES, SUMS, BLOCK), F32),
            pltpu.VMEM((8 * low, 8, BLOCK), F32),
            pltpu.VMEM((2, 8, BLOCK), F32),
            pltpu.VMEM((2, 8, BLOCK), F32),
            pltpu.VMEM((planes, 2, 8, BLOCK), F32),
            pltpu.SemaphoreType.REGULAR,
            dma(2, 8), dma(2, 8), dma(),
            dma(2, 4), dma(2, 4), dma(2, 2), dma(2, 2), dma(2, 2), dma(2, 2), dma(2, 2), dma(2, 2),
            dma(2, 3), dma(2, 3), dma(2), dma(2),
            dma(2, 14), dma(2, 14),
            dma(8 * low), dma(8 * low), dma(), dma(), dma(planes, 2), dma(planes),
        ],
        compiler_params=pltpu.CompilerParams(
            collective_id=0, has_side_effects=True, vmem_limit_bytes=26 * 2**20
        ),
        name="gather",
    )(*[pltpu.with_memory_space_constraint(flat(a), pltpu.HBM) for a in (local_params, base, momentum)])
    new_base, new_momentum, mixed = pl.pallas_call(
        update_kernel,
        out_shape=[
            jax.ShapeDtypeStruct((rows, KV), F32),
            jax.ShapeDtypeStruct((rows, KV), F32),
            jax.ShapeDtypeStruct((rows, KV), BF16),
        ],
        in_specs=[vmem] * 5,
        out_specs=[hbm] * 3,
        scratch_shapes=[
            pltpu.VMEM((rows, KV), F32),
            pltpu.VMEM((rows, KV), F32),
            pltpu.VMEM((rows, KV), BF16),
            dma(3, 8),
        ],
        compiler_params=pltpu.CompilerParams(vmem_limit_bytes=26 * 2**20),
        name="update",
    )(*held)
    return (
        new_base.reshape(base.shape),
        new_momentum.reshape(base.shape),
        mixed.reshape(local_params.shape),
    )


def solution(mesh):
    return jax.shard_map(
        local_step,
        mesh=mesh,
        in_specs=(P("rep", None, "fsdp", None), P(None, "fsdp", None), P(None, "fsdp", None)),
        out_specs=(P(None, "fsdp", None), P(None, "fsdp", None), P("rep", None, "fsdp", None)),
        check_vma=False,
    )
```

```python
import functools

import jax
import jax.numpy as jnp
from jax import lax
from jax.experimental import pallas as pl
from jax.experimental.pallas import tpu as pltpu
from jax.sharding import PartitionSpec as P

D = 8192
KV = 1024
BLOCK = 128
NB = KV // BLOCK
OWN = 128
WAVES = 2
PARTS = 2
ROWS = OWN // (WAVES * PARTS)
TILES = ROWS // 16 * NB
SCALE = TILES
LINES = (TILES + 1) * 16
SUMS = TILES * 16
MESH = pl.DeviceIdType.MESH
F32 = jnp.float32
BF16 = jnp.bfloat16


def tile(t):
    return slice(t * 16, t * 16 + 16)


def lane(packed, index):
    return packed[:, index : index + 1]


def where_in(o, piece, t):
    rows = pl.ds(pl.multiple_of(o * OWN + piece * ROWS + t // NB * 16, 16), 16)
    return rows, slice(t % NB * BLOCK, (t % NB + 1) * BLOCK)


def quantize(load, tiles, put, put_scale):
    lanes = lax.broadcasted_iota(jnp.int32, (16, BLOCK), 1)
    packed = jnp.zeros((16, BLOCK), F32)
    for t in range(tiles):
        x = load(t)
        total = jnp.sum(x * x, axis=1, keepdims=True)
        packed = jnp.where(lanes == t, total, packed)
    scale = jnp.sqrt(packed * (1.0 / BLOCK) + 1e-06).astype(BF16)
    put_scale(scale)
    inverse = 1.0 / scale.astype(F32)
    for t in range(tiles):
        put(t, jnp.clip(load(t) * lane(inverse, t), -2.5, 2.5).astype(BF16))


def gather_kernel(
    low, planes,
    local_hbm, base_hbm, mom_hbm,
    gathered, factor, base, mom, local,
    code, recv_x, recv_yf, recv_yn, recv_ym, sum_c, sum_x, recv_s, sum_y, recv_t, acc, acc_m,
    norm_own, norm_core, norm_z, norm_xy, entered,
    sem_local, sem_base, sem_mom,
    x1_s, x1_r, yf_s, yf_r, yn_s, yn_r, ym_s, ym_r, s_s, s_r, t_s, t_r,
    g_s, g_r, nx_s, nx_r, nc_s, nc_r, nz_s, nz_r,
):
    rep = lax.axis_index("rep")
    fsdp = lax.axis_index("fsdp")
    xh, y = rep // 4, rep % 4
    core, lo, z = fsdp % 2, fsdp // 2 % low, fsdp // (2 * low)
    other = 1 - xh
    partner = (other * 4 + y, fsdp)

    def along(k):
        return (xh * 4 + (y + k) % 4, fsdp)

    up, down = along(1), along(3)

    def remote(src, dst, send, recv, device):
        return pltpu.make_async_remote_copy(
            src_ref=src, dst_ref=dst, send_sem=send, recv_sem=recv, device_id=device, device_id_type=MESH
        )

    places = 8 * low
    place = rep * low + lo

    def in_plane(p, at_core):
        p = p % places
        return (p // low, (z * low + p % low) * 2 + at_core)

    def in_line(plane, at_core):
        return (rep, (plane % planes * low + lo) * 2 + at_core)

    chips = [partner[0] * low + lo, up[0] * low + lo, down[0] * low + lo]
    if low > 1:
        chips.append(rep * low + 1 - lo)

    def owner(i):
        return jnp.where(i < 4, other, xh) * 4 + (y + 1 + i) % 4

    def at_step(step):
        pair = step // 2
        return jnp.where(pair < 2, 1 - pair, pair) + step % 2 * 4

    def loads(w, i):
        start = owner(i) * OWN + w * (OWN // WAVES)
        rows = pl.ds(pl.multiple_of(start, OWN // WAVES), OWN // WAVES)
        return (
            pltpu.make_async_copy(local_hbm.at[rows], local.at[rows], sem_local.at[w, i]),
            pltpu.make_async_copy(base_hbm.at[rows], base.at[rows], sem_base.at[w, i]),
        )

    def start_loads(w, i):
        for copy in loads(w, i):
            copy.start()

    start_loads(0, at_step(0))
    barrier = pltpu.get_barrier_semaphore()
    for p in chips:
        pl.semaphore_signal(barrier, inc=1, device_id=in_plane(p, 0), device_id_type=MESH)

    @pl.when(core == 1)
    def _():
        pl.semaphore_signal(barrier, inc=1, device_id=in_line(z, 0), device_id_type=MESH)

    def enter():
        @pl.when(core == 0)
        def _():
            pl.semaphore_wait(barrier, 2 * len(chips) + 1)
            pl.semaphore_signal(entered, inc=1, device_id=in_line(z, 1), device_id_type=MESH)

        @pl.when(core == 1)
        def _():
            pl.semaphore_wait(entered, 1)
            for d in range(1, planes):
                pl.semaphore_signal(barrier, inc=1, device_id=in_line(z + d, 1), device_id_type=MESH)

    for step in range(1, 4):
        start_loads(0, at_step(step))

    mom_copy = pltpu.make_async_copy(mom_hbm, mom, sem_mom)

    def quantize_owner(w, i):
        o = owner(i)

        def load(t):
            at = where_in(o, w * PARTS + t // TILES, t % TILES)
            return base[at] - local[at].astype(F32)

        def put(t, value):
            code[w, t // TILES, o, tile(t % TILES)] = value

        def put_scale(value):
            for part in range(PARTS):
                code[w, part, o, tile(SCALE)] = value

        quantize(load, PARTS * TILES, put, put_scale)

    def rises(w, h):
        return (h + w) % 2 == 1

    def near_index(w, h):
        return 0 if rises(w, h) else 2

    def send_x1(w, i):
        return remote(code.at[w, 0, owner(i)], recv_x.at[w, i], x1_s.at[w, i], x1_r.at[w, i], partner)

    def coded(w, h, i):
        return code.at[w, 1, owner(i + 4 - 4 * h)]

    def send_yf(w, h):
        to = up if rises(w, h) else down
        return remote(coded(w, h, 1), recv_yf.at[w, h], yf_s.at[w, h], yf_r.at[w, h], to)

    def send_yn(w, h):
        to = down if rises(w, h) else up
        return remote(coded(w, h, 2 - near_index(w, h)), recv_yn.at[w, h], yn_s.at[w, h], yn_r.at[w, h], to)

    def send_ym(w, h):
        to = up if rises(w, h) else down
        return remote(sum_c.at[w, h], recv_ym.at[w, h], ym_s.at[w, h], ym_r.at[w, h], to)

    def send_s(w, k):
        near = near_index(w, 0)
        to = up if rises(w, 0) == (k != 1) else down
        src = sum_x.at[w, (1, 2 - near, near)[k]]
        return remote(src, recv_s.at[w, k], s_s.at[w, k], s_r.at[w, k], to)

    def send_t(w):
        return remote(sum_y.at[w], recv_t.at[w], t_s.at[w], t_r.at[w], partner)

    def add(pieces, part, put):
        scales = [ref[tile(SCALE)].astype(F32) if has else None for ref, has in pieces]
        for t in range(TILES):
            total = None
            for (ref, _), scale in zip(pieces, scales):
                value = ref[tile(t)].astype(F32)
                if scale is not None:
                    value = value * lane(scale, part * TILES + t)
                total = value if total is None else total + value
            put(t, total)

    def putter(ref, index):
        def put(t, value):
            ref[(*index, tile(t))] = value.astype(ref.dtype)

        return put

    def merge_y(w, h):
        send_yf(w, h).wait_recv()
        pieces = [(coded(w, h, near_index(w, h)), True), (recv_yf.at[w, h], True)]
        add(pieces, 1, putter(sum_c, (w, h)))
        send_ym(w, h).start()

    def sum_pair(w, i):
        send_x1(w, i).wait_recv()
        pieces = [(code.at[w, 0, owner(i + 4)], True), (recv_x.at[w, i], True)]
        near = near_index(w, 0)
        if i == 3:
            add(pieces, 0, putter(acc, (w, 0)))
        elif i == near:
            add(pieces, 0, putter(acc_m, (w,)))
        else:
            add(pieces, 0, putter(sum_x, (w, i)))
            send_s(w, 0 if i == 1 else 1).start()

    def merge_s(w):
        send_s(w, 0).wait_recv()
        pieces = [(acc_m.at[w], False), (recv_s.at[w, 0], False)]
        add(pieces, 0, putter(sum_x, (w, near_index(w, 0))))
        send_s(w, 2).start()

    def sum_column(w, h):
        send_ym(w, h).wait_recv()
        send_yn(w, h).wait_recv()
        pieces = [(coded(w, h, 3), True), (recv_ym.at[w, h], False), (recv_yn.at[w, h], True)]
        add(pieces, 1, putter(sum_y, (w,)) if h else putter(acc, (w, 1)))
        if h:
            send_t(w).start()

    def average(w, part):
        if part == 0:
            send_s(w, 1).wait_recv()
            send_s(w, 2).wait_recv()
            received = [recv_s.at[w, 1], recv_s.at[w, 2]]
        else:
            send_t(w).wait_recv()
            received = [recv_t.at[w]]
        for t in range(TILES):
            total = acc[w, part, tile(t)]
            for ref in received:
                total = total + ref[tile(t)].astype(F32)
            acc[w, part, tile(t)] = total * 0.125

        def load(t):
            return acc[w, part, tile(t)]

        def put(t, value):
            gathered[w, part, rep, tile(t)] = value

        def put_scale(value):
            gathered[w, part, rep, tile(SCALE)] = value

        quantize(load, TILES, put, put_scale)

    def squares(w, part):
        scale = gathered[w, part, rep, tile(SCALE)].astype(F32)
        total = jnp.zeros((16, BLOCK), F32)
        for t in range(TILES):
            step = gathered[w, part, rep, tile(t)].astype(F32) * lane(scale, t)
            total = total + step * step
        return total[:8] + total[8:]

    def move(k, w, part, o, device):
        ref = gathered.at[w, part, o]
        return remote(ref, ref, g_s.at[w, k], g_r.at[w, k], device)

    def near(d):
        return xh * 4 + (y + d) % 4, other * 4 + (y + d) % 4

    below, above, far = near(3), near(1), near(2)
    own, across = near(0)
    side = (below, above)

    def p_own(w, k, o):
        return move(k, w, 0, o, (up, down, partner)[k])

    def p_cross(w, k, o):
        return move((3, 4, 6)[k], w, 0, o, partner)

    def p_way(w):
        return 0 if w % 2 else 1

    def p_on(w, o):
        return move(5, w, 0, o, (up, down)[p_way(w)])

    def q_cross(w, o):
        return move(7, w, 1, o, partner)

    def q_own(w, k, o):
        return move(8 + k, w, 1, o, (up, down)[k])

    def q_across(w, k, o):
        return move(10 + k, w, 1, o, (up, down)[k])

    def q_on(w, k, o):
        return move(12 + k, w, 1, o, (up, down)[k])

    def gather_p(w):
        for k in range(3):
            p_own(w, k, own).start()

    def gather_q(w):
        q_cross(w, own).start()
        for k in range(2):
            q_own(w, k, own).start()

    def pass_p(w):
        for k in (p_way(w), 1 - p_way(w)):
            p_own(w, k, side[k][0]).wait_recv()
            if k == p_way(w):
                p_on(w, side[k][0]).start()
            p_cross(w, k, side[k][0]).start()

    def pass_p_far(w):
        p_on(w, far[0]).wait_recv()
        p_cross(w, 2, far[0]).start()

    def pass_q(w):
        q_cross(w, across).wait_recv()
        for k in range(2):
            q_across(w, k, across).start()

    def pass_q_own(w):
        q_own(w, 0, below[0]).wait_recv()
        q_on(w, 0, below[0]).start()

    def pass_q_across(w):
        q_across(w, 1, above[1]).wait_recv()
        q_on(w, 1, above[1]).start()

    def codes(w, first, last):
        @pl.loop(first, last)
        def _(step):
            i = at_step(step)
            for copy in loads(w, i):
                copy.wait()

            @pl.when(step < 4)
            def _():
                start_loads(w, at_step(step + 4))

            if w == 0:

                @pl.when(step >= 4)
                def _():
                    start_loads(1, at_step(step - 4))

            quantize_owner(w, i)
            if w == 0:

                @pl.when(step == 0)
                def _():
                    enter()

            @pl.when(i < 4)
            def _():
                send_x1(w, i).start()

            for h in range(2):
                start = 4 - 4 * h

                @pl.when(i == start + 1)
                def _():
                    send_yf(w, h).start()

                @pl.when(i == start + 2 - near_index(w, h))
                def _():
                    send_yn(w, h).start()

    codes(0, 0, 8)
    codes(1, 0, 2)
    merge_y(0, 1)
    merge_y(0, 0)
    sum_pair(0, 1)
    codes(1, 2, 4)
    sum_pair(0, 0)
    codes(1, 4, 8)
    mom_copy.start()
    merge_y(1, 1)
    merge_y(1, 0)
    sum_pair(0, 2)
    sum_pair(0, 3)
    merge_s(0)
    sum_column(0, 1)
    sum_column(0, 0)
    sum_pair(1, 1)
    sum_pair(1, 0)
    sum_column(1, 1)
    sum_column(1, 0)
    sum_pair(1, 2)
    merge_s(1)
    average(0, 0)
    gather_p(0)
    average(0, 1)
    gather_q(0)
    sum_pair(1, 3)
    early = squares(0, 0) + squares(0, 1)
    average(1, 1)
    gather_q(1)
    early = early + squares(1, 1)
    average(1, 0)
    gather_p(1)

    def norm_core_copy():
        return remote(norm_own, norm_core, nc_s, nc_r, in_line(z, 1))

    def norm_z_copy(d, e, plane):
        slot = norm_z.at[plane]
        return remote(slot, slot, nz_s.at[d, e], nz_r.at[plane], in_line(z + d, e))

    def norm_xy_copy(k, p):
        slot = norm_xy.at[p]
        return remote(slot, slot, nx_s.at[k], nx_r.at[p], in_plane(place + k, core))

    line_peers = [(d, e) for d in range(planes) for e in range(2) if (d, e) != (0, 1)]

    norm_own[...] = early + squares(1, 0)

    @pl.when(core == 0)
    def _():
        norm_core_copy().start()

    pass_p(0)
    pass_q_own(0)
    @pl.when(core == 1)
    def _():
        if planes > 1:
            pl.semaphore_wait(barrier, planes - 1)
        norm_core_copy().wait_recv()
        norm_z[z] = norm_own[...] + norm_core[...]
        for d, e in line_peers:
            norm_z_copy(d, e, z).start()

    pass_q(0)
    pass_p_far(0)
    pass_q_own(1)
    pass_p(1)
    pass_q(1)
    pass_q_across(0)
    @pl.when(core == 0)
    def _():
        norm_z_copy(0, 0, z).wait_recv()

    for d in range(1, planes):
        norm_z_copy(d, 0, (z + d) % planes).wait_recv()
    total = norm_z[0]
    for plane in range(1, planes):
        total = total + norm_z[plane]
    norm_xy[place] = total
    for k in range(1, places):
        norm_xy_copy(k, place).start()
    pass_q_across(1)
    pass_p_far(1)

    mom_copy.wait()
    for w in range(WAVES):
        for i in range(4):
            send_x1(w, i).wait_send()
        for h in range(2):
            send_yf(w, h).wait_send()
            send_yn(w, h).wait_send()
            send_ym(w, h).wait_send()
        for k in range(3):
            send_s(w, k).wait_send()
        send_t(w).wait_send()

    @pl.when(core == 0)
    def _():
        norm_core_copy().wait_send()

    @pl.when(core == 1)
    def _():
        for d, e in line_peers:
            norm_z_copy(d, e, z).wait_send()

    def send_last():
        for w in range(WAVES):
            for k in range(3):
                p_own(w, k, own).wait_send()
                p_cross(w, k, (below, above, far)[k][0]).wait_send()
            p_on(w, side[p_way(w)][0]).wait_send()
            q_cross(w, own).wait_send()
            for k in range(2):
                q_own(w, k, own).wait_send()
                q_across(w, k, across).wait_send()
                q_on(w, k, (below[0], above[1])[k]).wait_send()
        for k in range(1, places):
            norm_xy_copy(k, place).wait_send()

    for k in range(1, places):
        norm_xy_copy(k, (place + k) % places).wait_recv()
    for m in range(2):
        value = norm_xy[m * 4 * low]
        for p in range(1, 4 * low):
            value = value + norm_xy[m * 4 * low + p]
        total = jnp.sum(jnp.sum(value, axis=1, keepdims=True), axis=0, keepdims=True)
        norm = jnp.sqrt(jnp.broadcast_to(total, (8, BLOCK)) + 1e-06)
        factor[m] = jnp.minimum(1.0, 0.25 * jnp.sqrt(F32(D * KV)) / norm)

    for w in range(WAVES):
        p_own(w, 2, across).wait_recv()
        q_own(w, 1, above[0]).wait_recv()
        q_across(w, 0, below[1]).wait_recv()
        for k, o in enumerate((below, above, far)):
            p_cross(w, k, o[1]).wait_recv()
        q_on(w, 0, far[0]).wait_recv()
        q_on(w, 1, far[1]).wait_recv()
    send_last()

def update_kernel(
    gathered, factor, base, mom, local,
    base_hbm, mom_hbm, mixed_hbm,
    new_base, new_mom, mixed, sem,
):
    def stores(o):
        rows = pl.ds(pl.multiple_of(o * OWN, OWN), OWN)
        return [
            pltpu.make_async_copy(src.at[rows], dst.at[rows], sem.at[k, o])
            for k, (src, dst) in enumerate(((new_base, base_hbm), (new_mom, mom_hbm), (mixed, mixed_hbm)))
        ]

    @pl.loop(0, 8)
    def _(o):
        clip = factor[o // 4, 0:1]
        for piece in range(WAVES * PARTS):
            w, part = piece // PARTS, piece % PARTS
            scale = gathered[w, part, o, tile(SCALE)].astype(F32)
            for t in range(TILES):
                at = where_in(o, piece, t)
                grad = clip * (gathered[w, part, o, tile(t)].astype(F32) * lane(scale, t))
                moved = 0.9 * mom[at] + grad
                shared = base[at] - 0.7 * (grad + 0.9 * moved)
                new_mom[at] = moved
                new_base[at] = shared
                mixed[at] = (0.5 * local[at].astype(F32) + 0.5 * shared).astype(BF16)
        for copy in stores(o):
            copy.start()

    @pl.loop(0, 8)
    def _(o):
        for copy in stores(o):
            copy.wait()


def local_step(local_params, base, momentum):
    rows = base.shape[0] * base.shape[1]
    shards = lax.axis_size("fsdp")
    flat = lambda a: a.reshape(rows, KV)
    dma = lambda *n: pltpu.SemaphoreType.DMA(n) if n else pltpu.SemaphoreType.DMA
    vmem = pl.BlockSpec(memory_space=pltpu.VMEM)
    hbm = pl.BlockSpec(memory_space=pltpu.HBM)
    low = 2 if shards % 4 == 0 else 1
    planes = shards // (2 * low)
    waves = lambda *shape: pltpu.VMEM((WAVES, *shape, BLOCK), BF16)
    held = pl.pallas_call(
        functools.partial(gather_kernel, low, planes),
        out_shape=[
            waves(PARTS, 8, LINES),
            pltpu.VMEM((2, 8, BLOCK), F32),
            pltpu.VMEM((rows, KV), F32),
            pltpu.VMEM((rows, KV), F32),
            pltpu.VMEM((rows, KV), BF16),
        ],
        in_specs=[hbm] * 3,
        out_specs=[vmem] * 5,
        scratch_shapes=[
            waves(PARTS, 8, LINES),
            waves(4, LINES),
            waves(2, LINES), waves(2, LINES), waves(2, SUMS), waves(2, SUMS),
            waves(3, SUMS), waves(3, SUMS), waves(SUMS), waves(SUMS),
            pltpu.VMEM((WAVES, PARTS, SUMS, BLOCK), F32),
            pltpu.VMEM((WAVES, SUMS, BLOCK), F32),
            pltpu.VMEM((8, BLOCK), F32),
            pltpu.VMEM((8, BLOCK), F32),
            pltpu.VMEM((planes, 8, BLOCK), F32),
            pltpu.VMEM((8 * low, 8, BLOCK), F32),
            pltpu.SemaphoreType.REGULAR,
            dma(2, 8), dma(2, 8), dma(),
            dma(2, 4), dma(2, 4), dma(2, 2), dma(2, 2), dma(2, 2), dma(2, 2), dma(2, 2), dma(2, 2),
            dma(2, 3), dma(2, 3), dma(2), dma(2),
            dma(2, 14), dma(2, 14),
            dma(8 * low), dma(8 * low), dma(), dma(), dma(planes, 2), dma(planes),
        ],
        compiler_params=pltpu.CompilerParams(
            collective_id=0, has_side_effects=True, vmem_limit_bytes=26 * 2**20
        ),
        name="gather",
    )(*[pltpu.with_memory_space_constraint(flat(a), pltpu.HBM) for a in (local_params, base, momentum)])
    new_base, new_momentum, mixed = pl.pallas_call(
        update_kernel,
        out_shape=[
            jax.ShapeDtypeStruct((rows, KV), F32),
            jax.ShapeDtypeStruct((rows, KV), F32),
            jax.ShapeDtypeStruct((rows, KV), BF16),
        ],
        in_specs=[vmem] * 5,
        out_specs=[hbm] * 3,
        scratch_shapes=[
            pltpu.VMEM((rows, KV), F32),
            pltpu.VMEM((rows, KV), F32),
            pltpu.VMEM((rows, KV), BF16),
            dma(3, 8),
        ],
        compiler_params=pltpu.CompilerParams(vmem_limit_bytes=26 * 2**20),
        name="update",
    )(*held)
    return (
        new_base.reshape(base.shape),
        new_momentum.reshape(base.shape),
        mixed.reshape(local_params.shape),
    )


def solution(mesh):
    return jax.shard_map(
        local_step,
        mesh=mesh,
        in_specs=(P("rep", None, "fsdp", None), P(None, "fsdp", None), P(None, "fsdp", None)),
        out_specs=(P(None, "fsdp", None), P(None, "fsdp", None), P("rep", None, "fsdp", None)),
        check_vma=False,
    )
```

```python
import functools

import jax
import jax.numpy as jnp
from jax import lax
from jax.experimental import pallas as pl
from jax.experimental.pallas import tpu as pltpu
from jax.sharding import PartitionSpec as P

D = 8192
KV = 1024
BLOCK = 128
NB = KV // BLOCK
OWN = 128
WAVES = 2
PARTS = 2
ROWS = OWN // (WAVES * PARTS)
TILES = ROWS // 16 * NB
SCALE = TILES
LINES = (TILES + 1) * 16
SUMS = TILES * 16
MESH = pl.DeviceIdType.MESH
F32 = jnp.float32
BF16 = jnp.bfloat16


def tile(t):
    return slice(t * 16, t * 16 + 16)


def lane(packed, index):
    return packed[:, index : index + 1]


def where_in(o, piece, t):
    rows = pl.ds(pl.multiple_of(o * OWN + piece * ROWS + t // NB * 16, 16), 16)
    return rows, slice(t % NB * BLOCK, (t % NB + 1) * BLOCK)


def quantize(load, tiles, put, put_scale):
    lanes = lax.broadcasted_iota(jnp.int32, (16, BLOCK), 1)
    packed = jnp.zeros((16, BLOCK), F32)
    for t in range(tiles):
        x = load(t)
        total = jnp.sum(x * x, axis=1, keepdims=True)
        packed = jnp.where(lanes == t, total, packed)
    scale = jnp.sqrt(packed * (1.0 / BLOCK) + 1e-06).astype(BF16)
    put_scale(scale)
    scale = scale.astype(F32)
    for t in range(tiles):
        spread = lane(scale, t) + jnp.zeros((16, BLOCK), F32)
        put(t, jnp.clip(load(t) / spread, -2.5, 2.5).astype(BF16), spread)


def gather_kernel(
    low, planes,
    local_hbm, base_hbm, mom_hbm,
    gathered, factor, base, mom, local,
    code, kept, recv_x, recv_yf, recv_yn, recv_ym, sum_c, sum_x, recv_s, sum_y, recv_t, acc, acc_m,
    norm_own, norm_core, norm_z, norm_xy, entered,
    sem_local, sem_base, sem_mom,
    x1_s, x1_r, yf_s, yf_r, yn_s, yn_r, ym_s, ym_r, s_s, s_r, t_s, t_r,
    g_s, g_r, nx_s, nx_r, nc_s, nc_r, nz_s, nz_r,
):
    rep = lax.axis_index("rep")
    fsdp = lax.axis_index("fsdp")
    xh, y = rep // 4, rep % 4
    core, lo, z = fsdp % 2, fsdp // 2 % low, fsdp // (2 * low)
    other = 1 - xh
    partner = (other * 4 + y, fsdp)

    def along(k):
        return (xh * 4 + (y + k) % 4, fsdp)

    up, down = along(1), along(3)

    def remote(src, dst, send, recv, device):
        return pltpu.make_async_remote_copy(
            src_ref=src, dst_ref=dst, send_sem=send, recv_sem=recv, device_id=device, device_id_type=MESH
        )

    places = 8 * low
    place = rep * low + lo

    def in_plane(p, at_core):
        p = p % places
        return (p // low, (z * low + p % low) * 2 + at_core)

    def in_line(plane, at_core):
        return (rep, (plane % planes * low + lo) * 2 + at_core)

    chips = [partner[0] * low + lo, up[0] * low + lo, down[0] * low + lo]
    if low > 1:
        chips.append(rep * low + 1 - lo)

    def owner(i):
        return jnp.where(i < 4, other, xh) * 4 + (y + 1 + i) % 4

    def at_step(step):
        pair = step // 2
        return jnp.where(pair < 2, 1 - pair, pair) + step % 2 * 4

    def loads(w, i):
        start = owner(i) * OWN + w * (OWN // WAVES)
        rows = pl.ds(pl.multiple_of(start, OWN // WAVES), OWN // WAVES)
        return (
            pltpu.make_async_copy(local_hbm.at[rows], local.at[rows], sem_local.at[w, i]),
            pltpu.make_async_copy(base_hbm.at[rows], base.at[rows], sem_base.at[w, i]),
        )

    def start_loads(w, i):
        for copy in loads(w, i):
            copy.start()

    start_loads(0, at_step(0))
    barrier = pltpu.get_barrier_semaphore()
    for p in chips:
        pl.semaphore_signal(barrier, inc=1, device_id=in_plane(p, 0), device_id_type=MESH)

    @pl.when(core == 1)
    def _():
        pl.semaphore_signal(barrier, inc=1, device_id=in_line(z, 0), device_id_type=MESH)

    def enter():
        @pl.when(core == 0)
        def _():
            pl.semaphore_wait(barrier, 2 * len(chips) + 1)
            pl.semaphore_signal(entered, inc=1, device_id=in_line(z, 1), device_id_type=MESH)

        @pl.when(core == 1)
        def _():
            pl.semaphore_wait(entered, 1)
            for d in range(1, planes):
                pl.semaphore_signal(barrier, inc=1, device_id=in_line(z + d, 1), device_id_type=MESH)

    for step in range(1, 4):
        start_loads(0, at_step(step))

    mom_copy = pltpu.make_async_copy(mom_hbm, mom, sem_mom)

    def quantize_owner(w, i):
        o = owner(i)

        def load(t):
            at = where_in(o, w * PARTS + t // TILES, t % TILES)
            return base[at] - local[at].astype(F32)

        def put(t, value, scale):
            at = (w, t // TILES, o, tile(t % TILES))
            value = value.astype(F32) * scale
            kept[at] = value
            code[at] = value.astype(BF16)

        quantize(load, PARTS * TILES, put, lambda scale: None)

    def rises(w, h):
        return (h + w) % 2 == 1

    def near_index(w, h):
        return 0 if rises(w, h) else 2

    def send_x1(w, i):
        return remote(code.at[w, 0, owner(i)], recv_x.at[w, i], x1_s.at[w, i], x1_r.at[w, i], partner)

    def coded(w, h, i):
        return code.at[w, 1, owner(i + 4 - 4 * h)]

    def mine(w, h, i):
        return kept.at[w, 1, owner(i + 4 - 4 * h)]

    def send_yf(w, h):
        to = up if rises(w, h) else down
        return remote(coded(w, h, 1), recv_yf.at[w, h], yf_s.at[w, h], yf_r.at[w, h], to)

    def send_yn(w, h):
        to = down if rises(w, h) else up
        return remote(coded(w, h, 2 - near_index(w, h)), recv_yn.at[w, h], yn_s.at[w, h], yn_r.at[w, h], to)

    def send_ym(w, h):
        to = up if rises(w, h) else down
        return remote(sum_c.at[w, h], recv_ym.at[w, h], ym_s.at[w, h], ym_r.at[w, h], to)

    def send_s(w, k):
        near = near_index(w, 0)
        to = up if rises(w, 0) == (k != 1) else down
        src = sum_x.at[w, (1, 2 - near, near)[k]]
        return remote(src, recv_s.at[w, k], s_s.at[w, k], s_r.at[w, k], to)

    def send_t(w):
        return remote(sum_y.at[w], recv_t.at[w], t_s.at[w], t_r.at[w], partner)

    def add(pieces, put):
        for t in range(TILES):
            total = None
            for ref in pieces:
                value = ref[tile(t)].astype(F32)
                total = value if total is None else total + value
            put(t, total)

    def putter(ref, index):
        def put(t, value):
            ref[(*index, tile(t))] = value.astype(ref.dtype)

        return put

    def merge_y(w, h):
        send_yf(w, h).wait_recv()
        pieces = [mine(w, h, near_index(w, h)), recv_yf.at[w, h]]
        add(pieces, putter(sum_c, (w, h)))
        send_ym(w, h).start()

    def sum_pair(w, i):
        send_x1(w, i).wait_recv()
        pieces = [kept.at[w, 0, owner(i + 4)], recv_x.at[w, i]]
        near = near_index(w, 0)
        if i == 3:
            add(pieces, putter(acc, (w, 0)))
        elif i == near:
            add(pieces, putter(acc_m, (w,)))
        else:
            add(pieces, putter(sum_x, (w, i)))
            send_s(w, 0 if i == 1 else 1).start()

    def merge_s(w):
        send_s(w, 0).wait_recv()
        pieces = [acc_m.at[w], recv_s.at[w, 0]]
        add(pieces, putter(sum_x, (w, near_index(w, 0))))
        send_s(w, 2).start()

    def sum_column(w, h):
        send_ym(w, h).wait_recv()
        send_yn(w, h).wait_recv()
        pieces = [mine(w, h, 3), recv_ym.at[w, h], recv_yn.at[w, h]]
        add(pieces, putter(sum_y, (w,)) if h else putter(acc, (w, 1)))
        if h:
            send_t(w).start()

    def average(w, part):
        if part == 0:
            send_s(w, 1).wait_recv()
            send_s(w, 2).wait_recv()
            received = [recv_s.at[w, 1], recv_s.at[w, 2]]
        else:
            send_t(w).wait_recv()
            received = [recv_t.at[w]]
        for t in range(TILES):
            total = acc[w, part, tile(t)]
            for ref in received:
                total = total + ref[tile(t)].astype(F32)
            acc[w, part, tile(t)] = total * 0.125

        def load(t):
            return acc[w, part, tile(t)]

        def put(t, value, _):
            gathered[w, part, rep, tile(t)] = value

        def put_scale(value):
            gathered[w, part, rep, tile(SCALE)] = value

        quantize(load, TILES, put, put_scale)

    def squares(w, part):
        scale = gathered[w, part, rep, tile(SCALE)].astype(F32)
        total = jnp.zeros((16, BLOCK), F32)
        for t in range(TILES):
            step = gathered[w, part, rep, tile(t)].astype(F32) * lane(scale, t)
            total = total + step * step
        return total[:8] + total[8:]

    def move(k, w, part, o, device):
        ref = gathered.at[w, part, o]
        return remote(ref, ref, g_s.at[w, k], g_r.at[w, k], device)

    def near(d):
        return xh * 4 + (y + d) % 4, other * 4 + (y + d) % 4

    below, above, far = near(3), near(1), near(2)
    own, across = near(0)
    side = (below, above)

    def p_own(w, k, o):
        return move(k, w, 0, o, (up, down, partner)[k])

    def p_cross(w, k, o):
        return move((3, 4, 6)[k], w, 0, o, partner)

    def p_way(w):
        return 0 if w % 2 else 1

    def p_on(w, o):
        return move(5, w, 0, o, (up, down)[p_way(w)])

    def q_cross(w, o):
        return move(7, w, 1, o, partner)

    def q_own(w, k, o):
        return move(8 + k, w, 1, o, (up, down)[k])

    def q_across(w, k, o):
        return move(10 + k, w, 1, o, (up, down)[k])

    def q_on(w, k, o):
        return move(12 + k, w, 1, o, (up, down)[k])

    def gather_p_y(w):
        for k in (p_way(w), 1 - p_way(w)):
            p_own(w, k, own).start()

    def gather_p_x(w):
        p_own(w, 2, own).start()

    def gather_q_y(w):
        for k in range(2):
            q_own(w, k, own).start()

    def gather_q_x(w):
        q_cross(w, own).start()

    def pass_p(w, later):
        k = 1 - p_way(w) if later else p_way(w)
        p_own(w, k, side[k][0]).wait_recv()
        if not later:
            p_on(w, side[k][0]).start()
        p_cross(w, k, side[k][0]).start()

    def pass_p_far(w):
        p_on(w, far[0]).wait_recv()
        p_cross(w, 2, far[0]).start()

    def pass_q(w):
        q_cross(w, across).wait_recv()
        for k in (1, 0):
            q_across(w, k, across).start()

    def pass_q_own(w):
        q_own(w, 0, below[0]).wait_recv()
        q_on(w, 0, below[0]).start()

    def pass_q_across(w):
        q_across(w, 1, above[1]).wait_recv()
        q_on(w, 1, above[1]).start()

    def codes(w, first, last):
        @pl.loop(first, last)
        def _(step):
            i = at_step(step)
            for copy in loads(w, i):
                copy.wait()

            @pl.when(step < 4)
            def _():
                start_loads(w, at_step(step + 4))

            if w == 0:

                @pl.when(step >= 4)
                def _():
                    start_loads(1, at_step(step - 4))

            quantize_owner(w, i)
            if w == 0:

                @pl.when(step == 0)
                def _():
                    enter()

            @pl.when(i < 4)
            def _():
                send_x1(w, i).start()

            for h in range(2):
                start = 4 - 4 * h

                @pl.when(i == start + 1)
                def _():
                    send_yf(w, h).start()

                @pl.when(i == start + 2 - near_index(w, h))
                def _():
                    send_yn(w, h).start()

    def norm_core_copy():
        return remote(norm_own, norm_core, nc_s, nc_r, in_line(z, 1))

    def norm_z_copy(d, e, plane):
        slot = norm_z.at[plane]
        return remote(slot, slot, nz_s.at[d, e], nz_r.at[plane], in_line(z + d, e))

    def norm_xy_copy(k, p):
        slot = norm_xy.at[p]
        return remote(slot, slot, nx_s.at[k], nx_r.at[p], in_plane(place + k, core))

    line_peers = [(d, e) for d in range(planes) for e in range(2) if (d, e) != (0, 1)]

    codes(0, 0, 8)
    codes(1, 0, 2)
    sum_pair(0, 1)
    sum_pair(0, 0)
    merge_y(0, 1)
    codes(1, 2, 4)
    codes(1, 4, 8)
    mom_copy.start()
    merge_y(1, 1)
    sum_pair(1, 1)
    sum_pair(0, 2)
    merge_s(0)
    merge_y(0, 0)
    merge_y(1, 0)
    sum_column(0, 1)
    sum_pair(1, 0)
    sum_pair(1, 2)
    sum_pair(0, 3)
    sum_column(1, 1)
    merge_s(1)
    average(0, 0)
    gather_p_x(0)
    sum_pair(1, 3)
    sum_column(1, 0)
    gather_p_y(0)
    sum_column(0, 0)
    average(0, 1)
    gather_q_y(0)
    gather_q_x(0)
    average(1, 1)
    gather_q_x(1)
    average(1, 0)
    gather_p_y(1)
    pass_p(0, 1)
    norm_own[...] = squares(0, 0) + squares(0, 1) + squares(1, 0) + squares(1, 1)

    @pl.when(core == 0)
    def _():
        norm_core_copy().start()

    gather_q_y(1)
    pass_p(0, 0)
    pass_p(1, 0)
    pass_q(1)
    @pl.when(core == 1)
    def _():
        if planes > 1:
            pl.semaphore_wait(barrier, planes - 1)
        norm_core_copy().wait_recv()
        norm_z[z] = norm_own[...] + norm_core[...]
        for d, e in line_peers:
            norm_z_copy(d, e, z).start()

    pass_q_own(0)
    pass_q(0)
    gather_p_x(1)
    pass_p(1, 1)
    pass_q_across(1)
    pass_p_far(0)
    pass_q_own(1)
    pass_q_across(0)
    pass_p_far(1)
    @pl.when(core == 0)
    def _():
        norm_z_copy(0, 0, z).wait_recv()

    for d in range(1, planes):
        norm_z_copy(d, 0, (z + d) % planes).wait_recv()
    total = norm_z[0]
    for plane in range(1, planes):
        total = total + norm_z[plane]
    norm_xy[place] = total
    for k in range(1, places):
        norm_xy_copy(k, place).start()

    mom_copy.wait()
    for w in range(WAVES):
        for i in range(4):
            send_x1(w, i).wait_send()
        for h in range(2):
            send_yf(w, h).wait_send()
            send_yn(w, h).wait_send()
            send_ym(w, h).wait_send()
        for k in range(3):
            send_s(w, k).wait_send()
        send_t(w).wait_send()

    @pl.when(core == 0)
    def _():
        norm_core_copy().wait_send()

    @pl.when(core == 1)
    def _():
        for d, e in line_peers:
            norm_z_copy(d, e, z).wait_send()

    def send_last():
        for w in range(WAVES):
            for k in range(3):
                p_own(w, k, own).wait_send()
                p_cross(w, k, (below, above, far)[k][0]).wait_send()
            p_on(w, side[p_way(w)][0]).wait_send()
            q_cross(w, own).wait_send()
            for k in range(2):
                q_own(w, k, own).wait_send()
                q_across(w, k, across).wait_send()
                q_on(w, k, (below[0], above[1])[k]).wait_send()
        for k in range(1, places):
            norm_xy_copy(k, place).wait_send()

    for k in range(1, places):
        norm_xy_copy(k, (place + k) % places).wait_recv()
    for m in range(2):
        value = norm_xy[m * 4 * low]
        for p in range(1, 4 * low):
            value = value + norm_xy[m * 4 * low + p]
        total = jnp.sum(jnp.sum(value, axis=1, keepdims=True), axis=0, keepdims=True)
        norm = jnp.sqrt(jnp.broadcast_to(total, (8, BLOCK)) + 1e-06)
        factor[m] = jnp.minimum(1.0, 0.25 * jnp.sqrt(F32(D * KV)) / norm)

    for w in range(WAVES):
        p_own(w, 2, across).wait_recv()
        q_own(w, 1, above[0]).wait_recv()
        q_across(w, 0, below[1]).wait_recv()
        for k, o in enumerate((below, above, far)):
            p_cross(w, k, o[1]).wait_recv()
        q_on(w, 0, far[0]).wait_recv()
        q_on(w, 1, far[1]).wait_recv()
    send_last()

def update_kernel(
    gathered, factor, base, mom, local,
    base_hbm, mom_hbm, mixed_hbm,
    new_base, new_mom, mixed, sem,
):
    def stores(o):
        rows = pl.ds(pl.multiple_of(o * OWN, OWN), OWN)
        return [
            pltpu.make_async_copy(src.at[rows], dst.at[rows], sem.at[k, o])
            for k, (src, dst) in enumerate(((new_base, base_hbm), (new_mom, mom_hbm), (mixed, mixed_hbm)))
        ]

    @pl.loop(0, 8)
    def _(o):
        clip = factor[o // 4, 0:1]
        for piece in range(WAVES * PARTS):
            w, part = piece // PARTS, piece % PARTS
            scale = gathered[w, part, o, tile(SCALE)].astype(F32)
            for t in range(TILES):
                at = where_in(o, piece, t)
                grad = clip * (gathered[w, part, o, tile(t)].astype(F32) * lane(scale, t))
                moved = 0.9 * mom[at] + grad
                shared = base[at] - 0.7 * (grad + 0.9 * moved)
                new_mom[at] = moved
                new_base[at] = shared
                mixed[at] = (0.5 * local[at].astype(F32) + 0.5 * shared).astype(BF16)
        for copy in stores(o):
            copy.start()

    @pl.loop(0, 8)
    def _(o):
        for copy in stores(o):
            copy.wait()


def local_step(local_params, base, momentum):
    rows = base.shape[0] * base.shape[1]
    shards = lax.axis_size("fsdp")
    flat = lambda a: a.reshape(rows, KV)
    dma = lambda *n: pltpu.SemaphoreType.DMA(n) if n else pltpu.SemaphoreType.DMA
    vmem = pl.BlockSpec(memory_space=pltpu.VMEM)
    hbm = pl.BlockSpec(memory_space=pltpu.HBM)
    low = 2 if shards % 4 == 0 else 1
    planes = shards // (2 * low)
    waves = lambda *shape: pltpu.VMEM((WAVES, *shape, BLOCK), BF16)
    held = pl.pallas_call(
        functools.partial(gather_kernel, low, planes),
        out_shape=[
            waves(PARTS, 8, LINES),
            pltpu.VMEM((2, 8, BLOCK), F32),
            pltpu.VMEM((rows, KV), F32),
            pltpu.VMEM((rows, KV), F32),
            pltpu.VMEM((rows, KV), BF16),
        ],
        in_specs=[hbm] * 3,
        out_specs=[vmem] * 5,
        scratch_shapes=[
            waves(PARTS, 8, SUMS),
            pltpu.VMEM((WAVES, PARTS, 8, SUMS, BLOCK), F32),
            waves(4, SUMS),
            waves(2, SUMS), waves(2, SUMS), waves(2, SUMS), waves(2, SUMS),
            waves(3, SUMS), waves(3, SUMS), waves(SUMS), waves(SUMS),
            pltpu.VMEM((WAVES, PARTS, SUMS, BLOCK), F32),
            pltpu.VMEM((WAVES, SUMS, BLOCK), F32),
            pltpu.VMEM((8, BLOCK), F32),
            pltpu.VMEM((8, BLOCK), F32),
            pltpu.VMEM((planes, 8, BLOCK), F32),
            pltpu.VMEM((8 * low, 8, BLOCK), F32),
            pltpu.SemaphoreType.REGULAR,
            dma(2, 8), dma(2, 8), dma(),
            dma(2, 4), dma(2, 4), dma(2, 2), dma(2, 2), dma(2, 2), dma(2, 2), dma(2, 2), dma(2, 2),
            dma(2, 3), dma(2, 3), dma(2), dma(2),
            dma(2, 14), dma(2, 14),
            dma(8 * low), dma(8 * low), dma(), dma(), dma(planes, 2), dma(planes),
        ],
        compiler_params=pltpu.CompilerParams(
            collective_id=0, has_side_effects=True, vmem_limit_bytes=26 * 2**20
        ),
        name="gather",
    )(*[pltpu.with_memory_space_constraint(flat(a), pltpu.HBM) for a in (local_params, base, momentum)])
    new_base, new_momentum, mixed = pl.pallas_call(
        update_kernel,
        out_shape=[
            jax.ShapeDtypeStruct((rows, KV), F32),
            jax.ShapeDtypeStruct((rows, KV), F32),
            jax.ShapeDtypeStruct((rows, KV), BF16),
        ],
        in_specs=[vmem] * 5,
        out_specs=[hbm] * 3,
        scratch_shapes=[
            pltpu.VMEM((rows, KV), F32),
            pltpu.VMEM((rows, KV), F32),
            pltpu.VMEM((rows, KV), BF16),
            dma(3, 8),
        ],
        compiler_params=pltpu.CompilerParams(vmem_limit_bytes=26 * 2**20),
        name="update",
    )(*held)
    return (
        new_base.reshape(base.shape),
        new_momentum.reshape(base.shape),
        mixed.reshape(local_params.shape),
    )


def solution(mesh):
    return jax.shard_map(
        local_step,
        mesh=mesh,
        in_specs=(P("rep", None, "fsdp", None), P(None, "fsdp", None), P(None, "fsdp", None)),
        out_specs=(P(None, "fsdp", None), P(None, "fsdp", None), P("rep", None, "fsdp", None)),
        check_vma=False,
    )
```

```python
import functools

import jax
import jax.numpy as jnp
from jax import lax
from jax.experimental import pallas as pl
from jax.experimental.pallas import tpu as pltpu
from jax.sharding import PartitionSpec as P

D = 8192
KV = 1024
BLOCK = 128
NB = KV // BLOCK
OWN = 128
WAVES = 2
PARTS = 2
ROWS = OWN // (WAVES * PARTS)
TILES = ROWS // 16 * NB
SCALE = TILES
LINES = (TILES + 1) * 16
SUMS = TILES * 16
MESH = pl.DeviceIdType.MESH
F32 = jnp.float32
BF16 = jnp.bfloat16


def tile(t):
    return slice(t * 16, t * 16 + 16)


def lane(packed, index):
    return packed[:, index : index + 1]


def where_in(o, piece, t):
    rows = pl.ds(pl.multiple_of(o * OWN + piece * ROWS + t // NB * 16, 16), 16)
    return rows, slice(t % NB * BLOCK, (t % NB + 1) * BLOCK)


def quantize(load, tiles, put, put_scale, first=0):
    lanes = lax.broadcasted_iota(jnp.int32, (16, BLOCK), 1)
    packed = jnp.zeros((16, BLOCK), F32)
    for t in range(tiles):
        x = load(t)
        total = jnp.sum(x * x, axis=1, keepdims=True)
        packed = jnp.where(lanes == first + t, total, packed)
    scale = jnp.sqrt(packed * (1.0 / BLOCK) + 1e-06).astype(BF16)
    put_scale(scale)
    scale = scale.astype(F32)
    for t in range(tiles):
        spread = lane(scale, first + t) + jnp.zeros((16, BLOCK), F32)
        put(t, jnp.clip(load(t) / spread, -2.5, 2.5).astype(BF16), spread)


def gather_kernel(
    low, planes,
    local_hbm, base_hbm, mom_hbm,
    gathered, factor, base, mom, local,
    code, kept, recv_x, recv_yf, recv_yn, recv_ym, sum_c, sum_x, recv_s, sum_y, recv_t, acc, acc_m,
    norm_own, norm_core, norm_z, norm_xy, entered,
    sem_local, sem_base, sem_mom,
    x1_s, x1_r, yf_s, yf_r, yn_s, yn_r, ym_s, ym_r, s_s, s_r, t_s, t_r,
    g_s, g_r, nx_s, nx_r, nc_s, nc_r, nz_s, nz_r,
):
    rep = lax.axis_index("rep")
    fsdp = lax.axis_index("fsdp")
    xh, y = rep // 4, rep % 4
    core, lo, z = fsdp % 2, fsdp // 2 % low, fsdp // (2 * low)
    other = 1 - xh
    partner = (other * 4 + y, fsdp)

    def along(k):
        return (xh * 4 + (y + k) % 4, fsdp)

    up, down = along(1), along(3)

    def remote(src, dst, send, recv, device):
        return pltpu.make_async_remote_copy(
            src_ref=src, dst_ref=dst, send_sem=send, recv_sem=recv, device_id=device, device_id_type=MESH
        )

    places = 8 * low
    place = rep * low + lo

    def in_plane(p, at_core):
        p = p % places
        return (p // low, (z * low + p % low) * 2 + at_core)

    def in_line(plane, at_core):
        return (rep, (plane % planes * low + lo) * 2 + at_core)

    chips = [partner[0] * low + lo, up[0] * low + lo, down[0] * low + lo]
    if low > 1:
        chips.append(rep * low + 1 - lo)

    def owner(i):
        return jnp.where(i < 4, other, xh) * 4 + (y + 1 + i) % 4

    def at_step(step):
        pair = step // 2
        return jnp.where(pair < 2, 1 - pair, pair) + step % 2 * 4

    def loads(w, i):
        start = owner(i) * OWN + w * (OWN // WAVES)
        rows = pl.ds(pl.multiple_of(start, OWN // WAVES), OWN // WAVES)
        return (
            pltpu.make_async_copy(local_hbm.at[rows], local.at[rows], sem_local.at[w, i]),
            pltpu.make_async_copy(base_hbm.at[rows], base.at[rows], sem_base.at[w, i]),
        )

    def start_loads(w, i):
        for copy in loads(w, i):
            copy.start()

    start_loads(0, at_step(0))
    barrier = pltpu.get_barrier_semaphore()
    for p in chips:
        pl.semaphore_signal(barrier, inc=1, device_id=in_plane(p, 0), device_id_type=MESH)

    @pl.when(core == 1)
    def _():
        pl.semaphore_signal(barrier, inc=1, device_id=in_line(z, 0), device_id_type=MESH)

    def enter():
        @pl.when(core == 0)
        def _():
            pl.semaphore_wait(barrier, 2 * len(chips) + 1)
            pl.semaphore_signal(entered, inc=1, device_id=in_line(z, 1), device_id_type=MESH)

        @pl.when(core == 1)
        def _():
            pl.semaphore_wait(entered, 1)
            for d in range(1, planes):
                pl.semaphore_signal(barrier, inc=1, device_id=in_line(z + d, 1), device_id_type=MESH)

    for step in range(1, 4):
        start_loads(0, at_step(step))

    mom_copy = pltpu.make_async_copy(mom_hbm, mom, sem_mom)

    def quantize_owner(w, i):
        o = owner(i)

        def load(t):
            at = where_in(o, w * PARTS + t // TILES, t % TILES)
            return base[at] - local[at].astype(F32)

        def put(t, value, scale):
            at = (w, t // TILES, o, tile(t % TILES))
            value = value.astype(F32) * scale
            kept[at] = value
            code[at] = value.astype(BF16)

        quantize(load, PARTS * TILES, put, lambda scale: None)

    def rises(w, h):
        return (h + w) % 2 == 1

    def near_index(w, h):
        return 0 if rises(w, h) else 2

    def send_x1(w, i):
        return remote(code.at[w, 0, owner(i)], recv_x.at[w, i], x1_s.at[w, i], x1_r.at[w, i], partner)

    def coded(w, h, i):
        return code.at[w, 1, owner(i + 4 - 4 * h)]

    def mine(w, h, i):
        return kept.at[w, 1, owner(i + 4 - 4 * h)]

    def send_yf(w, h):
        to = up if rises(w, h) else down
        return remote(coded(w, h, 1), recv_yf.at[w, h], yf_s.at[w, h], yf_r.at[w, h], to)

    def send_yn(w, h):
        to = down if rises(w, h) else up
        return remote(coded(w, h, 2 - near_index(w, h)), recv_yn.at[w, h], yn_s.at[w, h], yn_r.at[w, h], to)

    def send_ym(w, h):
        to = up if rises(w, h) else down
        return remote(sum_c.at[w, h], recv_ym.at[w, h], ym_s.at[w, h], ym_r.at[w, h], to)

    def send_s(w, k):
        near = near_index(w, 0)
        to = up if rises(w, 0) == (k != 1) else down
        src = sum_x.at[w, (1, 2 - near, near)[k]]
        return remote(src, recv_s.at[w, k], s_s.at[w, k], s_r.at[w, k], to)

    def send_t(w):
        return remote(sum_y.at[w], recv_t.at[w], t_s.at[w], t_r.at[w], partner)

    def add(pieces, put):
        for t in range(TILES):
            total = None
            for ref in pieces:
                value = ref[tile(t)].astype(F32)
                total = value if total is None else total + value
            put(t, total)

    def putter(ref, index):
        def put(t, value):
            ref[(*index, tile(t))] = value.astype(ref.dtype)

        return put

    def merge_y(w, h):
        send_yf(w, h).wait_recv()
        pieces = [mine(w, h, near_index(w, h)), recv_yf.at[w, h]]
        add(pieces, putter(sum_c, (w, h)))
        send_ym(w, h).start()

    def sum_pair(w, i):
        send_x1(w, i).wait_recv()
        pieces = [kept.at[w, 0, owner(i + 4)], recv_x.at[w, i]]
        near = near_index(w, 0)
        if i == 3:
            add(pieces, putter(acc, (w, 0)))
        elif i == near:
            add(pieces, putter(acc_m, (w,)))
        else:
            add(pieces, putter(sum_x, (w, i)))
            send_s(w, 0 if i == 1 else 1).start()

    def merge_s(w):
        send_s(w, 0).wait_recv()
        pieces = [acc_m.at[w], recv_s.at[w, 0]]
        add(pieces, putter(sum_x, (w, near_index(w, 0))))
        send_s(w, 2).start()

    def sum_column(w, h):
        send_ym(w, h).wait_recv()
        send_yn(w, h).wait_recv()
        pieces = [mine(w, h, 3), recv_ym.at[w, h], recv_yn.at[w, h]]
        add(pieces, putter(sum_y, (w,)) if h else putter(acc, (w, 1)))
        if h:
            send_t(w).start()

    def average(w, part):
        if part == 0:
            send_s(w, 1).wait_recv()
            send_s(w, 2).wait_recv()
            received = [recv_s.at[w, 1], recv_s.at[w, 2]]
        else:
            send_t(w).wait_recv()
            received = [recv_t.at[w]]
        for t in range(TILES):
            total = acc[w, part, tile(t)]
            for ref in received:
                total = total + ref[tile(t)].astype(F32)
            acc[w, part, tile(t)] = total * 0.125

        def load(t):
            return acc[w, part, tile(t)]

        def put(t, value, _):
            gathered[w, part, rep, tile(t)] = value

        def put_scale(value):
            if part == 1:
                lanes = lax.broadcasted_iota(jnp.int32, (16, BLOCK), 1)
                own_scales = gathered[w, 0, rep, tile(SCALE)].astype(F32)
                value = jnp.where(lanes < TILES, own_scales, value.astype(F32)).astype(BF16)
            gathered[w, part, rep, tile(SCALE)] = value

        quantize(load, TILES, put, put_scale, part * TILES)

    def squares(w, part):
        scale = gathered[w, part, rep, tile(SCALE)].astype(F32)
        total = jnp.zeros((16, BLOCK), F32)
        for t in range(TILES):
            step = gathered[w, part, rep, tile(t)].astype(F32) * lane(scale, part * TILES + t)
            total = total + step * step
        return total[:8] + total[8:]

    def move(k, w, part, o, device):
        ref = gathered.at[w, part, o, slice(0, LINES if part else SUMS)]
        return remote(ref, ref, g_s.at[w, k], g_r.at[w, k], device)

    def near(d):
        return xh * 4 + (y + d) % 4, other * 4 + (y + d) % 4

    below, above, far = near(3), near(1), near(2)
    own, across = near(0)
    side = (below, above)

    def p_own(w, k, o):
        return move(k, w, 0, o, (up, down, partner)[k])

    def p_cross(w, k, o):
        return move((3, 4, 6)[k], w, 0, o, partner)

    def p_way(w):
        return 0 if w % 2 else 1

    def p_on(w, o):
        return move(5, w, 0, o, (up, down)[p_way(w)])

    def q_cross(w, o):
        return move(7, w, 1, o, partner)

    def q_own(w, k, o):
        return move(8 + k, w, 1, o, (up, down)[k])

    def q_across(w, k, o):
        return move(10 + k, w, 1, o, (up, down)[k])

    def q_on(w, k, o):
        return move(12 + k, w, 1, o, (up, down)[k])

    def gather_p_y(w):
        for k in (p_way(w), 1 - p_way(w)):
            p_own(w, k, own).start()

    def gather_p_x(w):
        p_own(w, 2, own).start()

    def gather_q_y(w):
        for k in range(2):
            q_own(w, k, own).start()

    def gather_q_x(w):
        q_cross(w, own).start()

    def pass_p(w, later):
        k = 1 - p_way(w) if later else p_way(w)
        p_own(w, k, side[k][0]).wait_recv()
        if not later:
            p_on(w, side[k][0]).start()
        p_cross(w, k, side[k][0]).start()

    def pass_p_far(w):
        p_on(w, far[0]).wait_recv()
        p_cross(w, 2, far[0]).start()

    def pass_q(w):
        q_cross(w, across).wait_recv()
        for k in (1, 0):
            q_across(w, k, across).start()

    def pass_q_own(w):
        q_own(w, 0, below[0]).wait_recv()
        q_on(w, 0, below[0]).start()

    def pass_q_across(w):
        q_across(w, 1, above[1]).wait_recv()
        q_on(w, 1, above[1]).start()

    def codes(w, first, last):
        @pl.loop(first, last)
        def _(step):
            i = at_step(step)
            for copy in loads(w, i):
                copy.wait()

            @pl.when(step < 4)
            def _():
                start_loads(w, at_step(step + 4))

            if w == 0:

                @pl.when(step >= 4)
                def _():
                    start_loads(1, at_step(step - 4))

            quantize_owner(w, i)
            if w == 0:

                @pl.when(step == 0)
                def _():
                    enter()

            @pl.when(i < 4)
            def _():
                send_x1(w, i).start()

            for h in range(2):
                start = 4 - 4 * h

                @pl.when(i == start + 1)
                def _():
                    send_yf(w, h).start()

                @pl.when(i == start + 2 - near_index(w, h))
                def _():
                    send_yn(w, h).start()

    def norm_core_copy():
        return remote(norm_own, norm_core, nc_s, nc_r, in_line(z, 1))

    def norm_z_copy(d, e, plane):
        slot = norm_z.at[plane]
        return remote(slot, slot, nz_s.at[d, e], nz_r.at[plane], in_line(z + d, e))

    def norm_xy_copy(k, p):
        slot = norm_xy.at[p]
        return remote(slot, slot, nx_s.at[k], nx_r.at[p], in_plane(place + k, core))

    line_peers = [(d, e) for d in range(planes) for e in range(2) if (d, e) != (0, 1)]

    codes(0, 0, 8)
    codes(1, 0, 2)
    merge_y(0, 1)
    sum_pair(0, 1)
    codes(1, 2, 4)
    sum_pair(0, 0)
    codes(1, 4, 8)
    mom_copy.start()
    merge_y(1, 1)
    sum_pair(0, 2)
    sum_column(0, 1)
    merge_s(0)
    sum_pair(1, 1)
    sum_pair(0, 3)
    merge_y(0, 0)
    merge_y(1, 0)
    sum_column(1, 1)
    sum_pair(1, 2)
    sum_pair(1, 0)
    merge_s(1)
    average(0, 0)
    sum_pair(1, 3)
    gather_p_x(0)
    gather_p_y(0)
    sum_column(0, 0)
    average(0, 1)
    gather_q_y(0)
    gather_q_x(0)
    sum_column(1, 0)
    average(1, 0)
    gather_p_x(1)
    gather_p_y(1)
    average(1, 1)
    gather_q_x(1)
    gather_q_y(1)
    norm_own[...] = squares(0, 0) + squares(0, 1) + squares(1, 0) + squares(1, 1)

    @pl.when(core == 0)
    def _():
        norm_core_copy().start()

    pass_q(0)
    pass_p(0, 1)
    @pl.when(core == 1)
    def _():
        if planes > 1:
            pl.semaphore_wait(barrier, planes - 1)
        norm_core_copy().wait_recv()
        norm_z[z] = norm_own[...] + norm_core[...]
        for d, e in line_peers:
            norm_z_copy(d, e, z).start()

    pass_p(0, 0)
    pass_p(1, 0)
    pass_p(1, 1)
    pass_q(1)
    pass_q_own(0)
    pass_p_far(0)
    pass_q_across(0)
    pass_p_far(1)
    @pl.when(core == 0)
    def _():
        norm_z_copy(0, 0, z).wait_recv()

    for d in range(1, planes):
        norm_z_copy(d, 0, (z + d) % planes).wait_recv()
    total = norm_z[0]
    for plane in range(1, planes):
        total = total + norm_z[plane]
    norm_xy[place] = total
    for k in range(1, places):
        norm_xy_copy(k, place).start()
    pass_q_across(1)
    pass_q_own(1)

    mom_copy.wait()
    for w in range(WAVES):
        for i in range(4):
            send_x1(w, i).wait_send()
        for h in range(2):
            send_yf(w, h).wait_send()
            send_yn(w, h).wait_send()
            send_ym(w, h).wait_send()
        for k in range(3):
            send_s(w, k).wait_send()
        send_t(w).wait_send()

    @pl.when(core == 0)
    def _():
        norm_core_copy().wait_send()

    @pl.when(core == 1)
    def _():
        for d, e in line_peers:
            norm_z_copy(d, e, z).wait_send()

    def send_last():
        for w in range(WAVES):
            for k in range(3):
                p_own(w, k, own).wait_send()
                p_cross(w, k, (below, above, far)[k][0]).wait_send()
            p_on(w, side[p_way(w)][0]).wait_send()
            q_cross(w, own).wait_send()
            for k in range(2):
                q_own(w, k, own).wait_send()
                q_across(w, k, across).wait_send()
                q_on(w, k, (below[0], above[1])[k]).wait_send()
        for k in range(1, places):
            norm_xy_copy(k, place).wait_send()

    for k in range(1, places):
        norm_xy_copy(k, (place + k) % places).wait_recv()
    for m in range(2):
        value = norm_xy[m * 4 * low]
        for p in range(1, 4 * low):
            value = value + norm_xy[m * 4 * low + p]
        total = jnp.sum(jnp.sum(value, axis=1, keepdims=True), axis=0, keepdims=True)
        norm = jnp.sqrt(jnp.broadcast_to(total, (8, BLOCK)) + 1e-06)
        factor[m] = jnp.minimum(1.0, 0.25 * jnp.sqrt(F32(D * KV)) / norm)

    for w in range(WAVES):
        p_own(w, 2, across).wait_recv()
        q_own(w, 1, above[0]).wait_recv()
        q_across(w, 0, below[1]).wait_recv()
        for k, o in enumerate((below, above, far)):
            p_cross(w, k, o[1]).wait_recv()
        q_on(w, 0, far[0]).wait_recv()
        q_on(w, 1, far[1]).wait_recv()
    send_last()

def update_kernel(
    gathered, factor, base, mom, local,
    base_hbm, mom_hbm, mixed_hbm,
    new_base, new_mom, mixed, sem,
):
    def stores(o):
        rows = pl.ds(pl.multiple_of(o * OWN, OWN), OWN)
        return [
            pltpu.make_async_copy(src.at[rows], dst.at[rows], sem.at[k, o])
            for k, (src, dst) in enumerate(((new_base, base_hbm), (new_mom, mom_hbm), (mixed, mixed_hbm)))
        ]

    @pl.loop(0, 8)
    def _(o):
        clip = factor[o // 4, 0:1]
        for piece in range(WAVES * PARTS):
            w, part = piece // PARTS, piece % PARTS
            scale = gathered[w, 1, o, tile(SCALE)].astype(F32)
            for t in range(TILES):
                at = where_in(o, piece, t)
                grad = clip * (gathered[w, part, o, tile(t)].astype(F32) * lane(scale, part * TILES + t))
                moved = 0.9 * mom[at] + grad
                shared = base[at] - 0.7 * (grad + 0.9 * moved)
                new_mom[at] = moved
                new_base[at] = shared
                mixed[at] = (0.5 * local[at].astype(F32) + 0.5 * shared).astype(BF16)
        for copy in stores(o):
            copy.start()

    @pl.loop(0, 8)
    def _(o):
        for copy in stores(o):
            copy.wait()


def local_step(local_params, base, momentum):
    rows = base.shape[0] * base.shape[1]
    shards = lax.axis_size("fsdp")
    flat = lambda a: a.reshape(rows, KV)
    dma = lambda *n: pltpu.SemaphoreType.DMA(n) if n else pltpu.SemaphoreType.DMA
    vmem = pl.BlockSpec(memory_space=pltpu.VMEM)
    hbm = pl.BlockSpec(memory_space=pltpu.HBM)
    low = 2 if shards % 4 == 0 else 1
    planes = shards // (2 * low)
    waves = lambda *shape: pltpu.VMEM((WAVES, *shape, BLOCK), BF16)
    held = pl.pallas_call(
        functools.partial(gather_kernel, low, planes),
        out_shape=[
            waves(PARTS, 8, LINES),
            pltpu.VMEM((2, 8, BLOCK), F32),
            pltpu.VMEM((rows, KV), F32),
            pltpu.VMEM((rows, KV), F32),
            pltpu.VMEM((rows, KV), BF16),
        ],
        in_specs=[hbm] * 3,
        out_specs=[vmem] * 5,
        scratch_shapes=[
            waves(PARTS, 8, SUMS),
            pltpu.VMEM((WAVES, PARTS, 8, SUMS, BLOCK), F32),
            waves(4, SUMS),
            waves(2, SUMS), waves(2, SUMS), waves(2, SUMS), waves(2, SUMS),
            waves(3, SUMS), waves(3, SUMS), waves(SUMS), waves(SUMS),
            pltpu.VMEM((WAVES, PARTS, SUMS, BLOCK), F32),
            pltpu.VMEM((WAVES, SUMS, BLOCK), F32),
            pltpu.VMEM((8, BLOCK), F32),
            pltpu.VMEM((8, BLOCK), F32),
            pltpu.VMEM((planes, 8, BLOCK), F32),
            pltpu.VMEM((8 * low, 8, BLOCK), F32),
            pltpu.SemaphoreType.REGULAR,
            dma(2, 8), dma(2, 8), dma(),
            dma(2, 4), dma(2, 4), dma(2, 2), dma(2, 2), dma(2, 2), dma(2, 2), dma(2, 2), dma(2, 2),
            dma(2, 3), dma(2, 3), dma(2), dma(2),
            dma(2, 14), dma(2, 14),
            dma(8 * low), dma(8 * low), dma(), dma(), dma(planes, 2), dma(planes),
        ],
        compiler_params=pltpu.CompilerParams(
            collective_id=0, has_side_effects=True, vmem_limit_bytes=26 * 2**20
        ),
        name="gather",
    )(*[pltpu.with_memory_space_constraint(flat(a), pltpu.HBM) for a in (local_params, base, momentum)])
    new_base, new_momentum, mixed = pl.pallas_call(
        update_kernel,
        out_shape=[
            jax.ShapeDtypeStruct((rows, KV), F32),
            jax.ShapeDtypeStruct((rows, KV), F32),
            jax.ShapeDtypeStruct((rows, KV), BF16),
        ],
        in_specs=[vmem] * 5,
        out_specs=[hbm] * 3,
        scratch_shapes=[
            pltpu.VMEM((rows, KV), F32),
            pltpu.VMEM((rows, KV), F32),
            pltpu.VMEM((rows, KV), BF16),
            dma(3, 8),
        ],
        compiler_params=pltpu.CompilerParams(vmem_limit_bytes=26 * 2**20),
        name="update",
    )(*held)
    return (
        new_base.reshape(base.shape),
        new_momentum.reshape(base.shape),
        mixed.reshape(local_params.shape),
    )


def solution(mesh):
    return jax.shard_map(
        local_step,
        mesh=mesh,
        in_specs=(P("rep", None, "fsdp", None), P(None, "fsdp", None), P(None, "fsdp", None)),
        out_specs=(P(None, "fsdp", None), P(None, "fsdp", None), P("rep", None, "fsdp", None)),
        check_vma=False,
    )
```

```python
import functools

import jax
import jax.numpy as jnp
from jax import lax
from jax.experimental import pallas as pl
from jax.experimental.pallas import tpu as pltpu
from jax.sharding import PartitionSpec as P

D = 8192
KV = 1024
BLOCK = 128
NB = KV // BLOCK
OWN = 128
WAVES = 2
PARTS = 2
ROWS = OWN // (WAVES * PARTS)
TILES = ROWS // 16 * NB
SCALE = TILES
LINES = (TILES + 1) * 16
SUMS = TILES * 16
MESH = pl.DeviceIdType.MESH
F32 = jnp.float32
BF16 = jnp.bfloat16


def tile(t):
    return slice(t * 16, t * 16 + 16)


def lane(packed, index):
    return packed[:, index : index + 1]


def where_in(o, piece, t):
    rows = pl.ds(pl.multiple_of(o * OWN + piece * ROWS + t // NB * 16, 16), 16)
    return rows, slice(t % NB * BLOCK, (t % NB + 1) * BLOCK)


def quantize(load, tiles, put, put_scale, first=0):
    lanes = lax.broadcasted_iota(jnp.int32, (16, BLOCK), 1)
    packed = jnp.zeros((16, BLOCK), F32)
    for t in range(tiles):
        x = load(t)
        total = jnp.sum(x * x, axis=1, keepdims=True)
        packed = jnp.where(lanes == first + t, total, packed)
    scale = jnp.sqrt(packed * (1.0 / BLOCK) + 1e-06).astype(BF16)
    put_scale(scale)
    scale = scale.astype(F32)
    for t in range(tiles):
        spread = lane(scale, first + t) + jnp.zeros((16, BLOCK), F32)
        put(t, jnp.clip(load(t) / spread, -2.5, 2.5).astype(BF16), spread)


def gather_kernel(
    low, planes,
    local_hbm, base_hbm, mom_hbm,
    gathered, factor, base, mom, local,
    code, kept, recv_x, recv_yf, recv_yn, recv_ym, sum_c, sum_x, recv_s, sum_y, recv_t, acc, acc_m,
    norm_own, norm_core, norm_z, norm_xy, entered,
    sem_local, sem_base, sem_mom,
    x1_s, x1_r, yf_s, yf_r, yn_s, yn_r, ym_s, ym_r, s_s, s_r, t_s, t_r,
    g_s, g_r, nx_s, nx_r, nc_s, nc_r, nz_s, nz_r,
):
    rep = lax.axis_index("rep")
    fsdp = lax.axis_index("fsdp")
    xh, y = rep // 4, rep % 4
    core, lo, z = fsdp % 2, fsdp // 2 % low, fsdp // (2 * low)
    other = 1 - xh
    partner = (other * 4 + y, fsdp)

    def along(k):
        return (xh * 4 + (y + k) % 4, fsdp)

    up, down = along(1), along(3)

    def remote(src, dst, send, recv, device):
        return pltpu.make_async_remote_copy(
            src_ref=src, dst_ref=dst, send_sem=send, recv_sem=recv, device_id=device, device_id_type=MESH
        )

    places = 8 * low
    place = rep * low + lo

    def in_plane(p, at_core):
        p = p % places
        return (p // low, (z * low + p % low) * 2 + at_core)

    def in_line(plane, at_core):
        return (rep, (plane % planes * low + lo) * 2 + at_core)

    chips = [partner[0] * low + lo, up[0] * low + lo, down[0] * low + lo]
    if low > 1:
        chips.append(rep * low + 1 - lo)

    def owner(i):
        return jnp.where(i < 4, other, xh) * 4 + (y + 1 + i) % 4

    def at_step(step):
        pair = step // 2
        return jnp.where(pair < 2, 1 - pair, pair) + step % 2 * 4

    def loads(w, i):
        start = owner(i) * OWN + w * (OWN // WAVES)
        rows = pl.ds(pl.multiple_of(start, OWN // WAVES), OWN // WAVES)
        return (
            pltpu.make_async_copy(local_hbm.at[rows], local.at[rows], sem_local.at[w, i]),
            pltpu.make_async_copy(base_hbm.at[rows], base.at[rows], sem_base.at[w, i]),
        )

    def start_loads(w, i):
        for copy in loads(w, i):
            copy.start()

    start_loads(0, at_step(0))
    barrier = pltpu.get_barrier_semaphore()
    for p in chips:
        pl.semaphore_signal(barrier, inc=1, device_id=in_plane(p, 0), device_id_type=MESH)

    @pl.when(core == 1)
    def _():
        pl.semaphore_signal(barrier, inc=1, device_id=in_line(z, 0), device_id_type=MESH)

    def enter():
        @pl.when(core == 0)
        def _():
            pl.semaphore_wait(barrier, 2 * len(chips) + 1)
            pl.semaphore_signal(entered, inc=1, device_id=in_line(z, 1), device_id_type=MESH)

        @pl.when(core == 1)
        def _():
            pl.semaphore_wait(entered, 1)
            for d in range(1, planes):
                pl.semaphore_signal(barrier, inc=1, device_id=in_line(z + d, 1), device_id_type=MESH)

    for step in range(1, 4):
        start_loads(0, at_step(step))

    mom_copy = pltpu.make_async_copy(mom_hbm, mom, sem_mom)

    def quantize_owner(w, i):
        o = owner(i)

        def load(t):
            at = where_in(o, w * PARTS + t // TILES, t % TILES)
            return base[at] - local[at].astype(F32)

        def put(t, value, scale):
            at = (w, t // TILES, o, tile(t % TILES))
            value = value.astype(F32) * scale
            kept[at] = value
            code[at] = value.astype(BF16)

        quantize(load, PARTS * TILES, put, lambda scale: None)

    def rises(w, h):
        return (h + w) % 2 == 1

    def near_index(w, h):
        return 0 if rises(w, h) else 2

    def send_x1(w, i):
        return remote(code.at[w, 0, owner(i)], recv_x.at[w, i], x1_s.at[w, i], x1_r.at[w, i], partner)

    def coded(w, h, i):
        return code.at[w, 1, owner(i + 4 - 4 * h)]

    def mine(w, h, i):
        return kept.at[w, 1, owner(i + 4 - 4 * h)]

    def send_yf(w, h):
        to = up if rises(w, h) else down
        return remote(coded(w, h, 1), recv_yf.at[w, h], yf_s.at[w, h], yf_r.at[w, h], to)

    def send_yn(w, h):
        to = down if rises(w, h) else up
        return remote(coded(w, h, 2 - near_index(w, h)), recv_yn.at[w, h], yn_s.at[w, h], yn_r.at[w, h], to)

    def send_ym(w, h):
        to = up if rises(w, h) else down
        return remote(sum_c.at[w, h], recv_ym.at[w, h], ym_s.at[w, h], ym_r.at[w, h], to)

    def send_s(w, k):
        near = near_index(w, 0)
        to = up if rises(w, 0) == (k != 1) else down
        src = sum_x.at[w, (1, 2 - near, near)[k]]
        return remote(src, recv_s.at[w, k], s_s.at[w, k], s_r.at[w, k], to)

    def send_t(w):
        return remote(sum_y.at[w], recv_t.at[w], t_s.at[w], t_r.at[w], partner)

    def add(pieces, put):
        for t in range(TILES):
            total = None
            for ref in pieces:
                value = ref[tile(t)].astype(F32)
                total = value if total is None else total + value
            put(t, total)

    def putter(ref, index):
        def put(t, value):
            ref[(*index, tile(t))] = value.astype(ref.dtype)

        return put

    def merge_y(w, h):
        send_yf(w, h).wait_recv()
        pieces = [mine(w, h, near_index(w, h)), recv_yf.at[w, h]]
        add(pieces, putter(sum_c, (w, h)))
        send_ym(w, h).start()

    def sum_pair(w, i):
        send_x1(w, i).wait_recv()
        pieces = [kept.at[w, 0, owner(i + 4)], recv_x.at[w, i]]
        near = near_index(w, 0)
        if i == 3:
            add(pieces, putter(acc, (w, 0)))
        elif i == near:
            add(pieces, putter(acc_m, (w,)))
        else:
            add(pieces, putter(sum_x, (w, i)))
            send_s(w, 0 if i == 1 else 1).start()

    def merge_s(w):
        send_s(w, 0).wait_recv()
        pieces = [acc_m.at[w], recv_s.at[w, 0]]
        add(pieces, putter(sum_x, (w, near_index(w, 0))))
        send_s(w, 2).start()

    def sum_column(w, h):
        send_ym(w, h).wait_recv()
        send_yn(w, h).wait_recv()
        pieces = [mine(w, h, 3), recv_ym.at[w, h], recv_yn.at[w, h]]
        add(pieces, putter(sum_y, (w,)) if h else putter(acc, (w, 1)))
        if h:
            send_t(w).start()

    def average(w, part):
        if part == 0:
            send_s(w, 1).wait_recv()
            send_s(w, 2).wait_recv()
            received = [recv_s.at[w, 1], recv_s.at[w, 2]]
        else:
            send_t(w).wait_recv()
            received = [recv_t.at[w]]
        for t in range(TILES):
            total = acc[w, part, tile(t)]
            for ref in received:
                total = total + ref[tile(t)].astype(F32)
            acc[w, part, tile(t)] = total * 0.125

        def load(t):
            return acc[w, part, tile(t)]

        def put(t, value, _):
            gathered[w, part, rep, tile(t)] = value

        def put_scale(value):
            if part == 1:
                lanes = lax.broadcasted_iota(jnp.int32, (16, BLOCK), 1)
                own_scales = gathered[w, 0, rep, tile(SCALE)].astype(F32)
                value = jnp.where(lanes < TILES, own_scales, value.astype(F32)).astype(BF16)
            gathered[w, part, rep, tile(SCALE)] = value

        quantize(load, TILES, put, put_scale, part * TILES)

    def squares(w, part):
        scale = gathered[w, part, rep, tile(SCALE)].astype(F32)
        total = jnp.zeros((16, BLOCK), F32)
        for t in range(TILES):
            step = gathered[w, part, rep, tile(t)].astype(F32) * lane(scale, part * TILES + t)
            total = total + step * step
        return total[:8] + total[8:]

    def move(k, w, part, o, device):
        ref = gathered.at[w, part, o, slice(0, LINES if part else SUMS)]
        return remote(ref, ref, g_s.at[w, k], g_r.at[w, k], device)

    def near(d):
        return xh * 4 + (y + d) % 4, other * 4 + (y + d) % 4

    below, above, far = near(3), near(1), near(2)
    own, across = near(0)
    side = (below, above)

    def p_own(w, k, o):
        return move(k, w, 0, o, (up, down, partner)[k])

    def p_cross(w, k, o):
        return move((3, 4, 6)[k], w, 0, o, partner)

    def p_way(w):
        return 0 if w % 2 else 1

    def p_on(w, o):
        return move(5, w, 0, o, (up, down)[p_way(w)])

    def q_cross(w, o):
        return move(7, w, 1, o, partner)

    def q_own(w, k, o):
        return move(8 + k, w, 1, o, (up, down)[k])

    def q_across(w, k, o):
        return move(10 + k, w, 1, o, (up, down)[k])

    def q_on(w, k, o):
        return move(12 + k, w, 1, o, (up, down)[k])

    def gather_p_y(w):
        for k in (p_way(w), 1 - p_way(w)):
            p_own(w, k, own).start()

    def gather_p_x(w):
        p_own(w, 2, own).start()

    def gather_q_y(w):
        for k in range(2):
            q_own(w, k, own).start()

    def gather_q_x(w):
        q_cross(w, own).start()

    def pass_p(w, later):
        k = 1 - p_way(w) if later else p_way(w)
        p_own(w, k, side[k][0]).wait_recv()
        if not later:
            p_on(w, side[k][0]).start()
        p_cross(w, k, side[k][0]).start()

    def pass_p_far(w):
        p_on(w, far[0]).wait_recv()
        p_cross(w, 2, far[0]).start()

    def pass_q(w):
        q_cross(w, across).wait_recv()
        for k in (1, 0):
            q_across(w, k, across).start()

    def pass_q_own(w):
        q_own(w, 0, below[0]).wait_recv()
        q_on(w, 0, below[0]).start()

    def pass_q_across(w):
        q_across(w, 1, above[1]).wait_recv()
        q_on(w, 1, above[1]).start()

    def codes(w, first, last):
        @pl.loop(first, last)
        def _(step):
            i = at_step(step)
            for copy in loads(w, i):
                copy.wait()

            @pl.when(step < 4)
            def _():
                start_loads(w, at_step(step + 4))

            if w == 0:

                @pl.when(step >= 4)
                def _():
                    start_loads(1, at_step(step - 4))

            quantize_owner(w, i)
            if w == 0:

                @pl.when(step == 0)
                def _():
                    enter()

            @pl.when(i < 4)
            def _():
                send_x1(w, i).start()

            for h in range(2):
                start = 4 - 4 * h

                @pl.when(i == start + 1)
                def _():
                    send_yf(w, h).start()

                @pl.when(i == start + 2 - near_index(w, h))
                def _():
                    send_yn(w, h).start()

    def norm_core_copy():
        return remote(norm_own, norm_core, nc_s, nc_r, in_line(z, 1))

    def norm_z_copy(d, e, plane):
        slot = norm_z.at[plane]
        return remote(slot, slot, nz_s.at[d, e], nz_r.at[plane], in_line(z + d, e))

    def norm_xy_copy(k, p):
        slot = norm_xy.at[p]
        return remote(slot, slot, nx_s.at[k], nx_r.at[p], in_plane(place + k, core))

    line_peers = [(d, e) for d in range(planes) for e in range(2) if (d, e) != (0, 1)]

    codes(0, 0, 8)
    codes(1, 0, 2)
    merge_y(0, 1)
    sum_pair(0, 0)
    sum_pair(0, 1)
    codes(1, 2, 4)
    codes(1, 4, 8)
    mom_copy.start()
    merge_y(1, 1)
    sum_column(0, 1)
    sum_pair(0, 2)
    merge_s(0)
    sum_pair(1, 1)
    merge_y(0, 0)
    sum_pair(0, 3)
    merge_y(1, 0)
    sum_column(1, 1)
    sum_pair(1, 2)
    sum_pair(1, 0)
    merge_s(1)
    average(0, 0)
    sum_pair(1, 3)
    gather_p_x(0)
    gather_p_y(0)
    sum_column(0, 0)
    average(0, 1)
    gather_q_y(0)
    gather_q_x(0)
    average(1, 0)
    gather_p_x(1)
    sum_column(1, 0)
    gather_p_y(1)
    average(1, 1)
    gather_q_x(1)
    gather_q_y(1)
    norm_own[...] = squares(0, 0) + squares(0, 1) + squares(1, 0) + squares(1, 1)

    @pl.when(core == 0)
    def _():
        norm_core_copy().start()

    pass_q(0)
    pass_p(0, 1)
    @pl.when(core == 1)
    def _():
        if planes > 1:
            pl.semaphore_wait(barrier, planes - 1)
        norm_core_copy().wait_recv()
        norm_z[z] = norm_own[...] + norm_core[...]
        for d, e in line_peers:
            norm_z_copy(d, e, z).start()

    pass_p(0, 0)
    pass_p(1, 0)
    pass_q_own(0)
    pass_p(1, 1)
    pass_q(1)
    @pl.when(core == 0)
    def _():
        norm_z_copy(0, 0, z).wait_recv()

    for d in range(1, planes):
        norm_z_copy(d, 0, (z + d) % planes).wait_recv()
    total = norm_z[0]
    for plane in range(1, planes):
        total = total + norm_z[plane]
    norm_xy[place] = total
    for k in range(1, places):
        norm_xy_copy(k, place).start()
    pass_p_far(0)
    pass_q_across(0)
    pass_p_far(1)
    pass_q_own(1)
    pass_q_across(1)

    mom_copy.wait()
    for w in range(WAVES):
        for i in range(4):
            send_x1(w, i).wait_send()
        for h in range(2):
            send_yf(w, h).wait_send()
            send_yn(w, h).wait_send()
            send_ym(w, h).wait_send()
        for k in range(3):
            send_s(w, k).wait_send()
        send_t(w).wait_send()

    @pl.when(core == 0)
    def _():
        norm_core_copy().wait_send()

    @pl.when(core == 1)
    def _():
        for d, e in line_peers:
            norm_z_copy(d, e, z).wait_send()

    def send_last():
        for w in range(WAVES):
            for k in range(3):
                p_own(w, k, own).wait_send()
                p_cross(w, k, (below, above, far)[k][0]).wait_send()
            p_on(w, side[p_way(w)][0]).wait_send()
            q_cross(w, own).wait_send()
            for k in range(2):
                q_own(w, k, own).wait_send()
                q_across(w, k, across).wait_send()
                q_on(w, k, (below[0], above[1])[k]).wait_send()
        for k in range(1, places):
            norm_xy_copy(k, place).wait_send()

    for k in range(1, places):
        norm_xy_copy(k, (place + k) % places).wait_recv()
    for m in range(2):
        value = norm_xy[m * 4 * low]
        for p in range(1, 4 * low):
            value = value + norm_xy[m * 4 * low + p]
        total = jnp.sum(jnp.sum(value, axis=1, keepdims=True), axis=0, keepdims=True)
        norm = jnp.sqrt(jnp.broadcast_to(total, (8, BLOCK)) + 1e-06)
        factor[m] = jnp.minimum(1.0, 0.25 * jnp.sqrt(F32(D * KV)) / norm)

    for w in range(WAVES):
        p_own(w, 2, across).wait_recv()
        q_own(w, 1, above[0]).wait_recv()
        q_across(w, 0, below[1]).wait_recv()
        for k, o in enumerate((below, above, far)):
            p_cross(w, k, o[1]).wait_recv()
        q_on(w, 0, far[0]).wait_recv()
        q_on(w, 1, far[1]).wait_recv()
    send_last()

def update_kernel(
    gathered, factor, base, mom, local,
    base_hbm, mom_hbm, mixed_hbm,
    new_base, new_mom, mixed, sem,
):
    def stores(o):
        rows = pl.ds(pl.multiple_of(o * OWN, OWN), OWN)
        return [
            pltpu.make_async_copy(src.at[rows], dst.at[rows], sem.at[k, o])
            for k, (src, dst) in enumerate(((new_base, base_hbm), (new_mom, mom_hbm), (mixed, mixed_hbm)))
        ]

    @pl.loop(0, 8)
    def _(o):
        clip = factor[o // 4, 0:1]
        for piece in range(WAVES * PARTS):
            w, part = piece // PARTS, piece % PARTS
            scale = gathered[w, 1, o, tile(SCALE)].astype(F32)
            for t in range(TILES):
                at = where_in(o, piece, t)
                grad = clip * (gathered[w, part, o, tile(t)].astype(F32) * lane(scale, part * TILES + t))
                moved = 0.9 * mom[at] + grad
                shared = base[at] - 0.7 * (grad + 0.9 * moved)
                new_mom[at] = moved
                new_base[at] = shared
                mixed[at] = (0.5 * local[at].astype(F32) + 0.5 * shared).astype(BF16)
        for copy in stores(o):
            copy.start()

    @pl.loop(0, 8)
    def _(o):
        for copy in stores(o):
            copy.wait()


def local_step(local_params, base, momentum):
    rows = base.shape[0] * base.shape[1]
    shards = lax.axis_size("fsdp")
    flat = lambda a: a.reshape(rows, KV)
    dma = lambda *n: pltpu.SemaphoreType.DMA(n) if n else pltpu.SemaphoreType.DMA
    vmem = pl.BlockSpec(memory_space=pltpu.VMEM)
    hbm = pl.BlockSpec(memory_space=pltpu.HBM)
    low = 2 if shards % 4 == 0 else 1
    planes = shards // (2 * low)
    waves = lambda *shape: pltpu.VMEM((WAVES, *shape, BLOCK), BF16)
    held = pl.pallas_call(
        functools.partial(gather_kernel, low, planes),
        out_shape=[
            waves(PARTS, 8, LINES),
            pltpu.VMEM((2, 8, BLOCK), F32),
            pltpu.VMEM((rows, KV), F32),
            pltpu.VMEM((rows, KV), F32),
            pltpu.VMEM((rows, KV), BF16),
        ],
        in_specs=[hbm] * 3,
        out_specs=[vmem] * 5,
        scratch_shapes=[
            waves(PARTS, 8, SUMS),
            pltpu.VMEM((WAVES, PARTS, 8, SUMS, BLOCK), F32),
            waves(4, SUMS),
            waves(2, SUMS), waves(2, SUMS), waves(2, SUMS), waves(2, SUMS),
            waves(3, SUMS), waves(3, SUMS), waves(SUMS), waves(SUMS),
            pltpu.VMEM((WAVES, PARTS, SUMS, BLOCK), F32),
            pltpu.VMEM((WAVES, SUMS, BLOCK), F32),
            pltpu.VMEM((8, BLOCK), F32),
            pltpu.VMEM((8, BLOCK), F32),
            pltpu.VMEM((planes, 8, BLOCK), F32),
            pltpu.VMEM((8 * low, 8, BLOCK), F32),
            pltpu.SemaphoreType.REGULAR,
            dma(2, 8), dma(2, 8), dma(),
            dma(2, 4), dma(2, 4), dma(2, 2), dma(2, 2), dma(2, 2), dma(2, 2), dma(2, 2), dma(2, 2),
            dma(2, 3), dma(2, 3), dma(2), dma(2),
            dma(2, 14), dma(2, 14),
            dma(8 * low), dma(8 * low), dma(), dma(), dma(planes, 2), dma(planes),
        ],
        compiler_params=pltpu.CompilerParams(
            collective_id=0, has_side_effects=True, vmem_limit_bytes=26 * 2**20
        ),
        name="gather",
    )(*[pltpu.with_memory_space_constraint(flat(a), pltpu.HBM) for a in (local_params, base, momentum)])
    new_base, new_momentum, mixed = pl.pallas_call(
        update_kernel,
        out_shape=[
            jax.ShapeDtypeStruct((rows, KV), F32),
            jax.ShapeDtypeStruct((rows, KV), F32),
            jax.ShapeDtypeStruct((rows, KV), BF16),
        ],
        in_specs=[vmem] * 5,
        out_specs=[hbm] * 3,
        scratch_shapes=[
            pltpu.VMEM((rows, KV), F32),
            pltpu.VMEM((rows, KV), F32),
            pltpu.VMEM((rows, KV), BF16),
            dma(3, 8),
        ],
        compiler_params=pltpu.CompilerParams(vmem_limit_bytes=26 * 2**20),
        name="update",
    )(*held)
    return (
        new_base.reshape(base.shape),
        new_momentum.reshape(base.shape),
        mixed.reshape(local_params.shape),
    )


def solution(mesh):
    return jax.shard_map(
        local_step,
        mesh=mesh,
        in_specs=(P("rep", None, "fsdp", None), P(None, "fsdp", None), P(None, "fsdp", None)),
        out_specs=(P(None, "fsdp", None), P(None, "fsdp", None), P("rep", None, "fsdp", None)),
        check_vma=False,
    )
```

```python
import functools

import jax
import jax.numpy as jnp
from jax import lax
from jax.experimental import pallas as pl
from jax.experimental.pallas import tpu as pltpu
from jax.sharding import PartitionSpec as P

D = 8192
KV = 1024
BLOCK = 128
NB = KV // BLOCK
OWN = 128
WAVES = 2
PARTS = 2
ROWS = OWN // (WAVES * PARTS)
TILES = ROWS // 16 * NB
SCALE = TILES
LINES = (TILES + 1) * 16
SUMS = TILES * 16
MESH = pl.DeviceIdType.MESH
F32 = jnp.float32
BF16 = jnp.bfloat16


def tile(t):
    return slice(t * 16, t * 16 + 16)


def lane(packed, index):
    return packed[:, index : index + 1]


def where_in(o, piece, t):
    rows = pl.ds(pl.multiple_of(o * OWN + piece * ROWS + t // NB * 16, 16), 16)
    return rows, slice(t % NB * BLOCK, (t % NB + 1) * BLOCK)


def quantize(load, tiles, put, put_scale, first=0):
    lanes = lax.broadcasted_iota(jnp.int32, (16, BLOCK), 1)
    packed = jnp.zeros((16, BLOCK), F32)
    for t in range(tiles):
        x = load(t)
        total = jnp.sum(x * x, axis=1, keepdims=True)
        packed = jnp.where(lanes == first + t, total, packed)
    scale = jnp.sqrt(packed * (1.0 / BLOCK) + 1e-06).astype(BF16)
    put_scale(scale)
    scale = scale.astype(F32)
    for t in range(tiles):
        spread = lane(scale, first + t) + jnp.zeros((16, BLOCK), F32)
        put(t, jnp.clip(load(t) / spread, -2.5, 2.5).astype(BF16), spread)


def gather_kernel(
    low, planes,
    local_hbm, base_hbm, mom_hbm,
    gathered, factor, base, mom, local,
    code, kept, recv_x, recv_yf, recv_yn, recv_ym, sum_c, sum_x, recv_s, sum_y, recv_t, acc, acc_m,
    norm_own, norm_core, norm_z, norm_xy, entered,
    sem_local, sem_base, sem_mom,
    x1_s, x1_r, yf_s, yf_r, yn_s, yn_r, ym_s, ym_r, s_s, s_r, t_s, t_r,
    g_s, g_r, nx_s, nx_r, nc_s, nc_r, nz_s, nz_r,
):
    rep = lax.axis_index("rep")
    fsdp = lax.axis_index("fsdp")
    xh, y = rep // 4, rep % 4
    core, lo, z = fsdp % 2, fsdp // 2 % low, fsdp // (2 * low)
    other = 1 - xh
    partner = (other * 4 + y, fsdp)

    def along(k):
        return (xh * 4 + (y + k) % 4, fsdp)

    up, down = along(1), along(3)

    def remote(src, dst, send, recv, device):
        return pltpu.make_async_remote_copy(
            src_ref=src, dst_ref=dst, send_sem=send, recv_sem=recv, device_id=device, device_id_type=MESH
        )

    places = 8 * low
    place = rep * low + lo

    def in_plane(p, at_core):
        p = p % places
        return (p // low, (z * low + p % low) * 2 + at_core)

    def in_line(plane, at_core):
        return (rep, (plane % planes * low + lo) * 2 + at_core)

    chips = [partner[0] * low + lo, up[0] * low + lo, down[0] * low + lo]
    if low > 1:
        chips.append(rep * low + 1 - lo)

    def owner(i):
        return jnp.where(i < 4, other, xh) * 4 + (y + 1 + i) % 4

    def at_step(step):
        pair = step // 2
        return jnp.where(pair < 2, 1 - pair, pair) + step % 2 * 4

    def loads(w, i):
        start = owner(i) * OWN + w * (OWN // WAVES)
        rows = pl.ds(pl.multiple_of(start, OWN // WAVES), OWN // WAVES)
        return (
            pltpu.make_async_copy(local_hbm.at[rows], local.at[rows], sem_local.at[w, i]),
            pltpu.make_async_copy(base_hbm.at[rows], base.at[rows], sem_base.at[w, i]),
        )

    def start_loads(w, i):
        for copy in loads(w, i):
            copy.start()

    start_loads(0, at_step(0))
    barrier = pltpu.get_barrier_semaphore()
    for p in chips:
        pl.semaphore_signal(barrier, inc=1, device_id=in_plane(p, 0), device_id_type=MESH)

    @pl.when(core == 1)
    def _():
        pl.semaphore_signal(barrier, inc=1, device_id=in_line(z, 0), device_id_type=MESH)

    def enter():
        @pl.when(core == 0)
        def _():
            pl.semaphore_wait(barrier, 2 * len(chips) + 1)
            pl.semaphore_signal(entered, inc=1, device_id=in_line(z, 1), device_id_type=MESH)

        @pl.when(core == 1)
        def _():
            pl.semaphore_wait(entered, 1)
            for d in range(1, planes):
                pl.semaphore_signal(barrier, inc=1, device_id=in_line(z + d, 1), device_id_type=MESH)

    for step in range(1, 4):
        start_loads(0, at_step(step))

    mom_copy = pltpu.make_async_copy(mom_hbm, mom, sem_mom)

    def quantize_owner(w, i):
        o = owner(i)

        def load(t):
            at = where_in(o, w * PARTS + t // TILES, t % TILES)
            return base[at] - local[at].astype(F32)

        def put(t, value, scale):
            at = (w, t // TILES, o, tile(t % TILES))
            value = value.astype(F32) * scale
            kept[at] = value
            code[at] = value.astype(BF16)

        quantize(load, PARTS * TILES, put, lambda scale: None)

    def rises(w, h):
        return (h + w) % 2 == 1

    def near_index(w, h):
        return 0 if rises(w, h) else 2

    def send_x1(w, i):
        return remote(code.at[w, 0, owner(i)], recv_x.at[w, i], x1_s.at[w, i], x1_r.at[w, i], partner)

    def coded(w, h, i):
        return code.at[w, 1, owner(i + 4 - 4 * h)]

    def mine(w, h, i):
        return kept.at[w, 1, owner(i + 4 - 4 * h)]

    def send_yf(w, h):
        to = up if rises(w, h) else down
        return remote(coded(w, h, 1), recv_yf.at[w, h], yf_s.at[w, h], yf_r.at[w, h], to)

    def send_yn(w, h):
        to = down if rises(w, h) else up
        return remote(coded(w, h, 2 - near_index(w, h)), recv_yn.at[w, h], yn_s.at[w, h], yn_r.at[w, h], to)

    def send_ym(w, h):
        to = up if rises(w, h) else down
        return remote(sum_c.at[w, h], recv_ym.at[w, h], ym_s.at[w, h], ym_r.at[w, h], to)

    def send_s(w, k):
        near = near_index(w, 0)
        to = up if rises(w, 0) == (k != 1) else down
        src = sum_x.at[w, (1, 2 - near, near)[k]]
        return remote(src, recv_s.at[w, k], s_s.at[w, k], s_r.at[w, k], to)

    def send_t(w):
        return remote(sum_y.at[w], recv_t.at[w], t_s.at[w], t_r.at[w], partner)

    def add(pieces, put):
        for t in range(TILES):
            total = None
            for ref in pieces:
                value = ref[tile(t)].astype(F32)
                total = value if total is None else total + value
            put(t, total)

    def putter(ref, index):
        def put(t, value):
            ref[(*index, tile(t))] = value.astype(ref.dtype)

        return put

    def merge_y(w, h):
        send_yf(w, h).wait_recv()
        pieces = [mine(w, h, near_index(w, h)), recv_yf.at[w, h]]
        add(pieces, putter(sum_c, (w, h)))
        send_ym(w, h).start()

    def sum_pair(w, i):
        send_x1(w, i).wait_recv()
        pieces = [kept.at[w, 0, owner(i + 4)], recv_x.at[w, i]]
        near = near_index(w, 0)
        if i == 3:
            add(pieces, putter(acc, (w, 0)))
        elif i == near:
            add(pieces, putter(acc_m, (w,)))
        else:
            add(pieces, putter(sum_x, (w, i)))
            send_s(w, 0 if i == 1 else 1).start()

    def merge_s(w):
        send_s(w, 0).wait_recv()
        pieces = [acc_m.at[w], recv_s.at[w, 0]]
        add(pieces, putter(sum_x, (w, near_index(w, 0))))
        send_s(w, 2).start()

    def sum_column(w, h):
        send_ym(w, h).wait_recv()
        send_yn(w, h).wait_recv()
        pieces = [mine(w, h, 3), recv_ym.at[w, h], recv_yn.at[w, h]]
        add(pieces, putter(sum_y, (w,)) if h else putter(acc, (w, 1)))
        if h:
            send_t(w).start()

    def average(w, part):
        if part == 0:
            send_s(w, 1).wait_recv()
            send_s(w, 2).wait_recv()
            received = [recv_s.at[w, 1], recv_s.at[w, 2]]
        else:
            send_t(w).wait_recv()
            received = [recv_t.at[w]]
        for t in range(TILES):
            total = acc[w, part, tile(t)]
            for ref in received:
                total = total + ref[tile(t)].astype(F32)
            acc[w, part, tile(t)] = total * 0.125

        def load(t):
            return acc[w, part, tile(t)]

        def put(t, value, _):
            gathered[w, part, rep, tile(t)] = value

        def put_scale(value):
            if part == 1:
                lanes = lax.broadcasted_iota(jnp.int32, (16, BLOCK), 1)
                own_scales = gathered[w, 0, rep, tile(SCALE)].astype(F32)
                value = jnp.where(lanes < TILES, own_scales, value.astype(F32)).astype(BF16)
            gathered[w, part, rep, tile(SCALE)] = value

        quantize(load, TILES, put, put_scale, part * TILES)

    def squares(w, part):
        scale = gathered[w, part, rep, tile(SCALE)].astype(F32)
        total = jnp.zeros((16, BLOCK), F32)
        for t in range(TILES):
            step = gathered[w, part, rep, tile(t)].astype(F32) * lane(scale, part * TILES + t)
            total = total + step * step
        return total[:8] + total[8:]

    def move(k, w, part, o, device):
        ref = gathered.at[w, part, o, slice(0, LINES if part else SUMS)]
        return remote(ref, ref, g_s.at[w, k], g_r.at[w, k], device)

    def near(d):
        return xh * 4 + (y + d) % 4, other * 4 + (y + d) % 4

    below, above, far = near(3), near(1), near(2)
    own, across = near(0)
    side = (below, above)

    def p_own(w, k, o):
        return move(k, w, 0, o, (up, down, partner)[k])

    def p_cross(w, k, o):
        return move((3, 4, 6)[k], w, 0, o, partner)

    def p_way(w):
        return 0 if w % 2 else 1

    def p_on(w, o):
        return move(5, w, 0, o, (up, down)[p_way(w)])

    def q_cross(w, o):
        return move(7, w, 1, o, partner)

    def q_own(w, k, o):
        return move(8 + k, w, 1, o, (up, down)[k])

    def q_across(w, k, o):
        return move(10 + k, w, 1, o, (up, down)[k])

    def q_on(w, k, o):
        return move(12 + k, w, 1, o, (up, down)[k])

    def gather_p_y(w):
        for k in (p_way(w), 1 - p_way(w)):
            p_own(w, k, own).start()

    def gather_p_x(w):
        p_own(w, 2, own).start()

    def gather_q_y(w):
        for k in range(2):
            q_own(w, k, own).start()

    def gather_q_x(w):
        q_cross(w, own).start()

    def pass_p(w, later):
        k = 1 - p_way(w) if later else p_way(w)
        p_own(w, k, side[k][0]).wait_recv()
        if not later:
            p_on(w, side[k][0]).start()
        p_cross(w, k, side[k][0]).start()

    def pass_p_far(w):
        p_on(w, far[0]).wait_recv()
        p_cross(w, 2, far[0]).start()

    def pass_q(w):
        q_cross(w, across).wait_recv()
        for k in (1, 0):
            q_across(w, k, across).start()

    def pass_q_own(w):
        q_own(w, 0, below[0]).wait_recv()
        q_on(w, 0, below[0]).start()

    def pass_q_across(w):
        q_across(w, 1, above[1]).wait_recv()
        q_on(w, 1, above[1]).start()

    def codes(w, first, last):
        @pl.loop(first, last)
        def _(step):
            i = at_step(step)
            for copy in loads(w, i):
                copy.wait()

            @pl.when(step < 4)
            def _():
                start_loads(w, at_step(step + 4))

            if w == 0:

                @pl.when(step >= 4)
                def _():
                    start_loads(1, at_step(step - 4))

            quantize_owner(w, i)
            if w == 0:

                @pl.when(step == 0)
                def _():
                    enter()

            @pl.when(i < 4)
            def _():
                send_x1(w, i).start()

            for h in range(2):
                start = 4 - 4 * h

                @pl.when(i == start + 1)
                def _():
                    send_yf(w, h).start()

                @pl.when(i == start + 2 - near_index(w, h))
                def _():
                    send_yn(w, h).start()

    def norm_core_copy():
        return remote(norm_own, norm_core, nc_s, nc_r, in_line(z, 1))

    def norm_z_copy(d, e, plane):
        slot = norm_z.at[plane]
        return remote(slot, slot, nz_s.at[d, e], nz_r.at[plane], in_line(z + d, e))

    def norm_xy_copy(k, p):
        slot = norm_xy.at[p]
        return remote(slot, slot, nx_s.at[k], nx_r.at[p], in_plane(place + k, core))

    line_peers = [(d, e) for d in range(planes) for e in range(2) if (d, e) != (0, 1)]

    codes(0, 0, 8)
    codes(1, 0, 2)
    merge_y(0, 1)
    sum_pair(0, 0)
    sum_pair(0, 1)
    codes(1, 2, 4)
    codes(1, 4, 8)
    mom_copy.start()
    merge_y(1, 1)
    sum_column(0, 1)
    sum_pair(0, 2)
    merge_s(0)
    sum_pair(1, 1)
    merge_y(0, 0)
    sum_pair(0, 3)
    merge_y(1, 0)
    sum_column(1, 1)
    sum_pair(1, 2)
    sum_pair(1, 0)
    merge_s(1)
    average(0, 0)
    sum_pair(1, 3)
    gather_p_x(0)
    gather_p_y(0)
    sum_column(0, 0)
    average(0, 1)
    gather_q_y(0)
    gather_q_x(0)
    average(1, 0)
    gather_p_x(1)
    sum_column(1, 0)
    gather_p_y(1)
    average(1, 1)
    gather_q_x(1)
    gather_q_y(1)
    norm_own[...] = squares(0, 0) + squares(0, 1) + squares(1, 0) + squares(1, 1)

    @pl.when(core == 0)
    def _():
        norm_core_copy().start()

    pass_q(0)
    pass_p(0, 1)
    @pl.when(core == 1)
    def _():
        if planes > 1:
            pl.semaphore_wait(barrier, planes - 1)
        norm_core_copy().wait_recv()
        norm_z[z] = norm_own[...] + norm_core[...]
        for d, e in line_peers:
            norm_z_copy(d, e, z).start()

    pass_p(0, 0)
    pass_p(1, 0)
    pass_q_own(0)
    pass_p(1, 1)
    pass_q(1)
    @pl.when(core == 0)
    def _():
        norm_z_copy(0, 0, z).wait_recv()

    for d in range(1, planes):
        norm_z_copy(d, 0, (z + d) % planes).wait_recv()
    total = norm_z[0]
    for plane in range(1, planes):
        total = total + norm_z[plane]
    norm_xy[place] = total
    for k in range(1, places):
        norm_xy_copy(k, place).start()
    pass_p_far(0)
    pass_q_across(0)
    pass_p_far(1)
    pass_q_own(1)
    pass_q_across(1)

    mom_copy.wait()
    for w in range(WAVES):
        for i in range(4):
            send_x1(w, i).wait_send()
        for h in range(2):
            send_yf(w, h).wait_send()
            send_yn(w, h).wait_send()
            send_ym(w, h).wait_send()
        for k in range(3):
            send_s(w, k).wait_send()
        send_t(w).wait_send()

    @pl.when(core == 0)
    def _():
        norm_core_copy().wait_send()

    @pl.when(core == 1)
    def _():
        for d, e in line_peers:
            norm_z_copy(d, e, z).wait_send()

    def send_last():
        for w in range(WAVES):
            for k in range(3):
                p_own(w, k, own).wait_send()
                p_cross(w, k, (below, above, far)[k][0]).wait_send()
            p_on(w, side[p_way(w)][0]).wait_send()
            q_cross(w, own).wait_send()
            for k in range(2):
                q_own(w, k, own).wait_send()
                q_across(w, k, across).wait_send()
                q_on(w, k, (below[0], above[1])[k]).wait_send()
        for k in range(1, places):
            norm_xy_copy(k, place).wait_send()

    for k in range(1, places):
        norm_xy_copy(k, (place + k) % places).wait_recv()
    for m in range(2):
        value = norm_xy[m * 4 * low]
        for p in range(1, 4 * low):
            value = value + norm_xy[m * 4 * low + p]
        total = jnp.sum(jnp.sum(value, axis=1, keepdims=True), axis=0, keepdims=True)
        norm = jnp.sqrt(jnp.broadcast_to(total, (8, BLOCK)) + 1e-06)
        factor[m] = jnp.minimum(1.0, 0.25 * jnp.sqrt(F32(D * KV)) / norm)

    for w in range(WAVES):
        p_own(w, 2, across).wait_recv()
        q_own(w, 1, above[0]).wait_recv()
        q_across(w, 0, below[1]).wait_recv()
        for k, o in enumerate((below, above, far)):
            p_cross(w, k, o[1]).wait_recv()
        q_on(w, 0, far[0]).wait_recv()
        q_on(w, 1, far[1]).wait_recv()
    send_last()

def update_kernel(
    gathered, factor, base, mom, local,
    base_hbm, mom_hbm, mixed_hbm,
    new_base, new_mom, mixed, sem,
):
    def stores(o, piece=None):
        if piece is None:
            rows, slot = pl.ds(pl.multiple_of(o * OWN, OWN), OWN), o
        else:
            rows, slot = pl.ds(piece * ROWS, ROWS), 8 + piece
        return [
            pltpu.make_async_copy(src.at[rows], dst.at[rows], sem.at[k, slot])
            for k, (src, dst) in enumerate(((new_base, base_hbm), (new_mom, mom_hbm), (mixed, mixed_hbm)))
        ]

    @pl.loop(0, 8)
    def _(o):
        clip = factor[o // 4, 0:1]
        for piece in range(WAVES * PARTS):
            w, part = piece // PARTS, piece % PARTS
            scale = gathered[w, 1, o, tile(SCALE)].astype(F32)
            for t in range(TILES):
                at = where_in(o, piece, t)
                grad = clip * (gathered[w, part, o, tile(t)].astype(F32) * lane(scale, part * TILES + t))
                moved = 0.9 * mom[at] + grad
                shared = base[at] - 0.7 * (grad + 0.9 * moved)
                new_mom[at] = moved
                new_base[at] = shared
                mixed[at] = (0.5 * local[at].astype(F32) + 0.5 * shared).astype(BF16)

            @pl.when(o == 0)
            def _():
                for copy in stores(0, piece):
                    copy.start()

        @pl.when(o > 0)
        def _():
            for copy in stores(o):
                copy.start()

    for piece in range(WAVES * PARTS):
        for copy in stores(0, piece):
            copy.wait()

    @pl.loop(1, 8)
    def _(o):
        for copy in stores(o):
            copy.wait()


def local_step(local_params, base, momentum):
    rows = base.shape[0] * base.shape[1]
    shards = lax.axis_size("fsdp")
    flat = lambda a: a.reshape(rows, KV)
    dma = lambda *n: pltpu.SemaphoreType.DMA(n) if n else pltpu.SemaphoreType.DMA
    vmem = pl.BlockSpec(memory_space=pltpu.VMEM)
    hbm = pl.BlockSpec(memory_space=pltpu.HBM)
    low = 2 if shards % 4 == 0 else 1
    planes = shards // (2 * low)
    waves = lambda *shape: pltpu.VMEM((WAVES, *shape, BLOCK), BF16)
    held = pl.pallas_call(
        functools.partial(gather_kernel, low, planes),
        out_shape=[
            waves(PARTS, 8, LINES),
            pltpu.VMEM((2, 8, BLOCK), F32),
            pltpu.VMEM((rows, KV), F32),
            pltpu.VMEM((rows, KV), F32),
            pltpu.VMEM((rows, KV), BF16),
        ],
        in_specs=[hbm] * 3,
        out_specs=[vmem] * 5,
        scratch_shapes=[
            waves(PARTS, 8, SUMS),
            pltpu.VMEM((WAVES, PARTS, 8, SUMS, BLOCK), F32),
            waves(4, SUMS),
            waves(2, SUMS), waves(2, SUMS), waves(2, SUMS), waves(2, SUMS),
            waves(3, SUMS), waves(3, SUMS), waves(SUMS), waves(SUMS),
            pltpu.VMEM((WAVES, PARTS, SUMS, BLOCK), F32),
            pltpu.VMEM((WAVES, SUMS, BLOCK), F32),
            pltpu.VMEM((8, BLOCK), F32),
            pltpu.VMEM((8, BLOCK), F32),
            pltpu.VMEM((planes, 8, BLOCK), F32),
            pltpu.VMEM((8 * low, 8, BLOCK), F32),
            pltpu.SemaphoreType.REGULAR,
            dma(2, 8), dma(2, 8), dma(),
            dma(2, 4), dma(2, 4), dma(2, 2), dma(2, 2), dma(2, 2), dma(2, 2), dma(2, 2), dma(2, 2),
            dma(2, 3), dma(2, 3), dma(2), dma(2),
            dma(2, 14), dma(2, 14),
            dma(8 * low), dma(8 * low), dma(), dma(), dma(planes, 2), dma(planes),
        ],
        compiler_params=pltpu.CompilerParams(
            collective_id=0, has_side_effects=True, vmem_limit_bytes=26 * 2**20
        ),
        name="gather",
    )(*[pltpu.with_memory_space_constraint(flat(a), pltpu.HBM) for a in (local_params, base, momentum)])
    new_base, new_momentum, mixed = pl.pallas_call(
        update_kernel,
        out_shape=[
            jax.ShapeDtypeStruct((rows, KV), F32),
            jax.ShapeDtypeStruct((rows, KV), F32),
            jax.ShapeDtypeStruct((rows, KV), BF16),
        ],
        in_specs=[vmem] * 5,
        out_specs=[hbm] * 3,
        scratch_shapes=[
            pltpu.VMEM((rows, KV), F32),
            pltpu.VMEM((rows, KV), F32),
            pltpu.VMEM((rows, KV), BF16),
            dma(3, 8 + WAVES * PARTS),
        ],
        compiler_params=pltpu.CompilerParams(vmem_limit_bytes=26 * 2**20),
        name="update",
    )(*held)
    return (
        new_base.reshape(base.shape),
        new_momentum.reshape(base.shape),
        mixed.reshape(local_params.shape),
    )


def solution(mesh):
    return jax.shard_map(
        local_step,
        mesh=mesh,
        in_specs=(P("rep", None, "fsdp", None), P(None, "fsdp", None), P(None, "fsdp", None)),
        out_specs=(P(None, "fsdp", None), P(None, "fsdp", None), P("rep", None, "fsdp", None)),
        check_vma=False,
    )
```
